128 devices in a mesh: prow: 8 (over y, core), pcol: 16 (over z, x).
Axes of the slice: x: 4, y: 4, z: 4, core: 2. Of those that a mesh axis runs over, the one named last changes fastest.
Arguments:
- parent: float32 [6, 8, 256, 3, 16, 256], P(None, 'prow', None, None, 'pcol')
- children: float32 [4, 8, 256, 1, 16, 256], P(None, 'prow', None, None, 'pcol')
- index_maps: int32 [2, 16], replicated, may hold values from 0 to 47, as said below
Outputs:
- factored: float32 [6, 8, 256, 3, 16, 256], P(None, 'prow', None, None, 'pcol')
The draws below stay inside these ranges and needn't reach their ends.
Inputs may be any that keep to these rules, and one draw needn't show every extreme that they name: `index_maps`: entry (k, u) is 3 u, 3 u + 1 or 3 u + 2, so each row rises strictly. Of the blocks u of one child with one remainder modulo 4, at most 1 go to parent blocks of one remainder modulo 2 * 4.
All inputs are finite; a program needn't handle non-finite values.
Results may differ from the reference program's by a relative error of at most 0.00005.
Values sent between devices are 32-bit elements; how exact they have to be, the bound alone decides.
No kernel may reach another device: no remote copies, remote signals or barrier semaphores. Data moves between devices by JAX's collectives and lax.ppermute only.
A program may use at most 128 MiB of HBM per device.

```python
import math
import jax
import jax.numpy as jnp
from jax import lax

NB = 256
PB = 48
UB = 16
KB = 5
HALF = 4
LR = 6
LC = 3
ULR = 4
ULC = 1
N_PROW = 8
N_PCOL = 16


parent_spread = 0.25


child_spread = 0.125


def symmetrize(raw_values, spread):
    return (raw_values + jnp.swapaxes(raw_values, -1, -2)) * (spread / math.sqrt(2.0))


def edge_bound():
    lead_blocks = (KB + 2) // 3
    return 2.0 * parent_spread * math.sqrt(KB * NB) + 4.0 * child_spread * math.sqrt(lead_blocks * NB)


def draw_parent(key, part):
    key = jax.random.fold_in(key, 11)
    first_key, second_key = jax.random.split(key)
    full_order = PB * NB
    bound_value = edge_bound()
    raw_values = jax.random.normal(first_key, (full_order, full_order), jnp.float32)
    diagonal = jax.random.uniform(second_key, (full_order,), jnp.float32, bound_value, 2.0 * bound_value)
    entries = symmetrize(raw_values, parent_spread)
    positions = jnp.arange(full_order)
    entries = entries.at[positions, positions].set(diagonal.astype(jnp.float32))
    return entries.reshape(LR, 2 * HALF, NB, LC, UB // ULC, NB).astype(jnp.float32)


def draw_children(key, part):
    key = jax.random.fold_in(key, 12)
    raw_values = jax.random.normal(key, (2, UB * NB, UB * NB), jnp.float32)
    entries = symmetrize(raw_values, child_spread)
    entries = entries.reshape(2, ULR, HALF, NB, ULC, UB // ULC, NB).transpose(1, 0, 2, 3, 4, 5, 6)
    return entries.reshape(ULR, 2 * HALF, NB, ULC, UB // ULC, NB).astype(jnp.float32)


def draw_index_maps(key, part):
    key = jax.random.fold_in(key, 13)
    first_key, second_key = jax.random.split(key)
    classes = 2 * HALF
    starts = jax.random.randint(first_key, (2, classes), 0, 3, jnp.int32)
    strides = jax.random.randint(second_key, (2, classes), 1, 3, jnp.int32)
    blocks = jnp.arange(UB, dtype=jnp.int32)
    last_class = (UB - 1) % classes
    last_turn = (UB - 1) // classes
    starts = starts.at[0, 0].set(0)
    starts = starts.at[1, last_class].set((2 - strides[1, last_class] * last_turn) % 3)
    turn_of = blocks // classes
    class_of = blocks % classes
    offsets = (starts[:, class_of] + strides[:, class_of] * turn_of[None, :]) % 3
    return (3 * blocks[None, :] + offsets).astype(jnp.int32)


def setup_inputs(seed: int = 0) -> dict:
    key_of = jax.random.split(jax.random.key(seed), 4)
    parent = draw_parent(jax.random.fold_in(key_of[3], 71), 0)
    children = draw_children(jax.random.fold_in(key_of[3], 71), 0)
    index_maps = draw_index_maps(jax.random.fold_in(key_of[3], 71), 0)
    return dict(parent=parent, children=children, index_maps=index_maps)


def reference(parent, children, index_maps):
    full_order = PB * NB
    front_full = parent.reshape(full_order, full_order)
    child_full = children.reshape(ULR, 2, HALF, NB, ULC, N_PCOL, NB)
    child_full = child_full.transpose(1, 0, 2, 3, 4, 5, 6).reshape(2, UB * NB, UB * NB)
    for child_index in range(2):
        positions = (index_maps[child_index][:, None] * NB + jnp.arange(NB, dtype=jnp.int32)[None, :]).reshape(-1).astype(jnp.int32)
        front_full = front_full.at[positions[:, None], positions[None, :]].add(child_full[child_index])
    panel_width = KB * NB
    leading = jnp.tril(jnp.linalg.cholesky(front_full[:panel_width, :panel_width]))
    lower_part = lax.linalg.triangular_solve(leading, front_full[panel_width:, :panel_width], left_side=False, lower=True, transpose_a=True)
    schur_part = front_full[panel_width:, panel_width:] - jnp.dot(lower_part.astype(jnp.float32), lower_part.T.astype(jnp.float32), precision=lax.Precision.HIGHEST, preferred_element_type=jnp.float32)
    upper_rows = jnp.concatenate([leading, jnp.zeros((panel_width, full_order - panel_width), jnp.float32)], axis=1)
    bottom_rows = jnp.concatenate([lower_part, schur_part], axis=1)
    result = jnp.concatenate([upper_rows, bottom_rows], axis=0)
    return result.reshape(LR, N_PROW, NB, LC, N_PCOL, NB)
```

```python
import functools
import jax
import jax.numpy as jnp
from jax import lax
from jax.experimental import pallas as pl
from jax.experimental.pallas import tpu as pltpu
from jax.sharding import PartitionSpec as P

KB = 5
NB = 256
HB = 128
LANES = 128
F32 = jnp.float32
BF16 = jnp.bfloat16
VMEM_LIMIT = 60 * 1024 * 1024
VM = pl.BlockSpec(memory_space=pltpu.VMEM)
SM = pl.BlockSpec(memory_space=pltpu.SMEM)


def route_of(meta, n):
    flip, d = n // 3, n % 3
    row = meta[32]
    residue = (3 * (row + 8 - d)) % 4
    parity = ((row + 16 - 3 * residue - d) // 4) % 2
    child = (parity + flip) % 2
    first = 4 * parity + residue
    second = first + 8
    is_first = meta[child * 16 + first] == 3 * first + d
    is_second = meta[child * 16 + second] == 3 * second + d
    block = jnp.where(is_first, first, second)
    return child, jnp.logical_or(is_first, is_second), (3 * block + d) // 8


def assemble_kernel(meta, parts_ref, out_ref):
    for j in range(KB):
        out_ref[j] = parts_ref[j, 0:6]
    for n in range(6):
        child, there, slot = route_of(meta, n)
        for v in range(2):
            column = meta[child * 16 + v]

            @pl.when(jnp.logical_and(there, column < KB))
            def _():
                out_ref[column, slot] = out_ref[column, slot] + parts_ref[v, 6 + n]


UPPER = [(k, i) for k in range(KB) for i in range(k, KB)]
CHILD_SOURCES = [(c, u, v) for c in range(2) for (u, v) in ((0, 0), (0, 1), (1, 1))]


def exact(a, b, dims):
    return lax.dot_general(a, b, (dims, ((), ())), precision=lax.Precision.HIGHEST, preferred_element_type=F32)


def factor_128(a_ref, x_ref, u_ref):
    shape = (8, LANES)
    lane = lax.broadcasted_iota(jnp.int32, (HB, LANES), 1)
    sub = lax.broadcasted_iota(jnp.int32, (HB, LANES), 0)
    x_ref[...] = jnp.where(lane == sub, 1.0, 0.0).astype(F32)
    for g in range(HB // 8):
        rows = slice(8 * g, 8 * g + 8)
        a_g = a_ref[rows, :]
        x_g = x_ref[rows, :]
        cols = [jnp.broadcast_to(a_g[:, 8 * g + s : 8 * g + s + 1], shape) for s in range(8)]
        d = [[jnp.broadcast_to(cols[s][t : t + 1, :], shape) for s in range(t + 1)] for t in range(8)]
        low = [[None] * 8 for _ in range(8)]
        rinv = []
        for s in range(8):
            r = lax.rsqrt(d[s][s])
            rinv.append(r)
            for t in range(s + 1, 8):
                low[t][s] = d[t][s] * r
            for t in range(s + 1, 8):
                for t2 in range(s + 1, t + 1):
                    d[t][t2] = d[t][t2] - low[t][s] * low[t2][s]
        ub, xb = [], []
        for t in range(8):
            ua = jnp.broadcast_to(a_g[t : t + 1, :], shape)
            xa = jnp.broadcast_to(x_g[t : t + 1, :], shape)
            for s in range(t):
                ua = ua - low[t][s] * ub[s]
                xa = xa - low[t][s] * xb[s]
            ub.append(ua * rinv[t])
            xb.append(xa * rinv[t])
            u_ref[8 * g + t : 8 * g + t + 1, :] = ub[t][0:1, :]
            x_ref[8 * g + t : 8 * g + t + 1, :] = xb[t][0:1, :]
        for i in range(g + 1, HB // 8):
            rows_i = slice(8 * i, 8 * i + 8)
            a_i = a_ref[rows_i, :]
            x_i = x_ref[rows_i, :]
            w = []
            for t in range(8):
                wt = jnp.broadcast_to(a_i[:, 8 * g + t : 8 * g + t + 1], shape)
                for s in range(t):
                    wt = wt - low[t][s] * w[s]
                w.append(wt * rinv[t])
            for t in range(8):
                a_i = a_i - w[t] * ub[t]
                x_i = x_i - w[t] * xb[t]
            a_ref[rows_i, :] = a_i
            x_ref[rows_i, :] = x_i
    u_ref[...] = jnp.where(lane >= sub, u_ref[...], 0.0)


def split(a):
    high = a.astype(BF16)
    return high, (a - high.astype(F32)).astype(BF16)


def chain_kernel(meta, parts_ref, u_ref, th_ref, tl_ref, f_ref, v_ref, a_s, x_s, u_s):
    def take(position, s, h):
        return parts_ref[s, position, pl.ds(h, 16, stride=2), :]

    for at, (k, i) in enumerate(UPPER):
        for s in range(16):
            for h in range(2):
                f_ref[k * KB + i, 16 * s : 16 * s + 16, HB * h : HB * h + HB] = take(at, s, h)
    for at, (c, u, v) in enumerate(CHILD_SOURCES):
        k = meta[c * 16 + u]
        i = meta[c * 16 + v]

        @pl.when(jnp.logical_and(k < KB, i < KB))
        def _():
            for s in range(16):
                for h in range(2):
                    place = (k * KB + i, slice(16 * s, 16 * s + 16), slice(HB * h, HB * h + HB))
                    f_ref[place] = f_ref[place] + take(15 + at, s, h)

    th_ref[...] = jnp.zeros_like(th_ref)
    tl_ref[...] = jnp.zeros_like(tl_ref)
    u_ref[...] = jnp.zeros_like(u_ref)

    @pl.loop(0, 2 * KB)
    def _(step):
        k = step // 2
        half = step % 2
        kk = k * KB + k

        @pl.when(half == 0)
        def _():
            a_s[...] = f_ref[kk, 0:HB, 0:HB]

        @pl.when(half == 1)
        def _():
            u12 = exact(v_ref[0:HB, 0:HB], f_ref[kk, 0:HB, HB:NB], ((1,), (0,)))
            u_ref[kk, 0:HB, HB:NB] = u12
            a_s[...] = f_ref[kk, HB:NB, HB:NB] - exact(u12, u12, ((0,), (0,)))

        factor_128(a_s, x_s, u_s)

        @pl.when(half == 0)
        def _():
            u_ref[kk, 0:HB, 0:HB] = u_s[...]
            v_ref[0:HB, 0:HB] = x_s[...]

        @pl.when(half == 1)
        def _():
            u_ref[kk, HB:NB, HB:NB] = u_s[...]
            v_ref[HB:NB, HB:NB] = x_s[...]
            v_ref[0:HB, HB:NB] = jnp.zeros((HB, HB), F32)
            lx = exact(u_ref[kk, 0:HB, HB:NB], v_ref[0:HB, 0:HB], ((0,), (0,)))
            v_ref[HB:NB, 0:HB] = -exact(x_s[...], lx, ((1,), (0,)))
            high, low = split(v_ref[...].T)
            th_ref[kk] = high
            tl_ref[kk] = low

            @pl.loop(k + 1, KB)
            def _(i):
                u = exact(v_ref[...], f_ref[k * KB + i], ((1,), (0,)))
                u_ref[k * KB + i] = u
                high, low = split(u)
                th_ref[k * KB + i] = high
                tl_ref[k * KB + i] = low

            @pl.loop(k + 1, KB)
            def _(i):
                @pl.loop(i, KB)
                def _(j):
                    f_ref[i * KB + j] = f_ref[i * KB + j] - exact(
                        u_ref[k * KB + i], u_ref[k * KB + j], ((0,), (0,))
                    )


def dot3(ah, al, bh, bl, dims):
    def dot(a, b):
        return lax.dot_general(a, b, (dims, ((), ())), preferred_element_type=F32)

    return dot(ah, bh) + (dot(ah, bl) + dot(al, bh))


NN = ((1,), (0,))
NT = ((1,), (1,))


def solve_rows(raw_ref, yh_ref, yl_ref, th_ref, tl_ref):
    for k in range(KB):
        at = slice(NB * k, NB * k + NB)
        t = raw_ref[:, at]
        for m in range(k):
            am = slice(NB * m, NB * m + NB)
            t = t - dot3(yh_ref[:, am], yl_ref[:, am], th_ref[m * KB + k], tl_ref[m * KB + k], NN)
        high, low = split(t)
        y = dot3(high, low, th_ref[k * KB + k], tl_ref[k * KB + k], NN)
        raw_ref[:, at] = y
        high, low = split(y)
        yh_ref[:, at] = high
        yl_ref[:, at] = low


def right_kernel(parts_ref, th_ref, tl_ref, yh_ref, yl_ref, raw):
    @pl.loop(0, 16)
    def _(s):
        for c in range(3):
            for j in range(KB):
                for h in range(2):
                    raw[pl.ds(pl.multiple_of(NB * c + 16 * s, 16), 16), NB * j + HB * h : NB * j + HB * h + HB] = parts_ref[
                        s, j, c, pl.ds(h, 16, stride=2), :
                    ]
    solve_rows(raw, yh_ref, yl_ref, th_ref, tl_ref)


ROWS_STEP = 2


def schur_kernel(meta, parts_ref, th_ref, tl_ref, rh_ref, rl_ref, u_ref, parent_ref, child_ref, out_ref, raw, yh, yl):
    step = pl.program_id(0)
    row, col = meta[32], meta[33]

    @pl.loop(0, 16)
    def _(s):
        for a in range(ROWS_STEP):
            for j in range(KB):
                for h in range(2):
                    raw[pl.ds(pl.multiple_of(NB * a + 16 * s, 16), 16), NB * j + HB * h : NB * j + HB * h + HB] = parts_ref[
                        s, j, a, pl.ds(h, 16, stride=2), :
                    ]
    solve_rows(raw, yh, yl, th_ref, tl_ref)
    for a in range(ROWS_STEP):
        slot = step * ROWS_STEP + a
        block_row = row + 8 * slot
        rows = slice(NB * a, NB * a + NB)
        for c in range(3):
            block_col = col + 16 * c

            def put(h, value):
                out_ref[pl.ds(1536 * a + 2 * c + h, NB, stride=6), :] = value

            @pl.when(jnp.logical_and(block_row >= KB, block_col >= KB))
            def _():
                cols = slice(NB * c, NB * c + NB)
                product = dot3(yh[rows, :], yl[rows, :], rh_ref[cols, :], rl_ref[cols, :], NT)
                for h in range(2):
                    put(h, parent_ref[pl.ds(1536 * a + 2 * c + h, NB, stride=6), :] - product[:, HB * h : HB * h + HB])
                turn = block_col % 3
                source = block_col // 3
                for n in range(6):
                    child, there, to = route_of(meta, n)
                    here = jnp.logical_and(there, to == slot)

                    @pl.when(jnp.logical_and(here, meta[child * 16 + source] == block_col))
                    def _():
                        for h in range(2):
                            at = pl.ds(1536 * a + 2 * c + h, NB, stride=6)
                            out_ref[at, :] = out_ref[at, :] + child_ref[turn, n, pl.ds(h, NB, stride=2), :]

            @pl.when(jnp.logical_and(block_row < KB, block_col >= KB))
            def _():
                for h in range(2):
                    put(h, jnp.zeros((NB, HB), F32))

            if c == 0:

                @pl.when(jnp.logical_and(block_row >= KB, block_col < KB))
                def _():
                    for j in range(KB):

                        @pl.when(block_col == j)
                        def _():
                            for h in range(2):
                                put(h, raw[rows, NB * j + HB * h : NB * j + HB * h + HB])

                @pl.when(jnp.logical_and(block_row < KB, block_col < KB))
                def _():
                    block = u_ref[jnp.minimum(block_col, KB - 1) * KB + jnp.minimum(block_row, KB - 1)].T
                    for h in range(2):
                        put(h, block[:, HB * h : HB * h + HB])


def call(kernel, out_shape, in_specs, scratch, **extra):
    return pl.pallas_call(
        kernel,
        out_shape=out_shape,
        in_specs=in_specs,
        out_specs=jax.tree.map(lambda _: VM, out_shape),
        scratch_shapes=scratch,
        compiler_params=pltpu.CompilerParams(vmem_limit_bytes=VMEM_LIMIT),
        **extra,
    )


def shaped(shape, dtype=F32):
    return jax.ShapeDtypeStruct(shape, dtype)


def per_device(parent, children, index_maps):
    row = lax.axis_index("prow")
    col = lax.axis_index("pcol")
    meta = jnp.concatenate([index_maps.reshape(-1), jnp.stack([row, col]).astype(jnp.int32)])
    front = parent.reshape(6, NB, 3, 2, LANES)
    lead = front[:, :, 0].reshape(6, 16, 32, LANES)
    child = children.reshape(4, 16, 32, LANES)

    first = jnp.stack([lead[0], child[0]], axis=1)
    first = lax.all_to_all(first, "pcol", 0, 0, tiled=True)
    first = jnp.concatenate([first[0:KB, 0], first[0:2, 1]], axis=0)
    every = lax.all_gather(first, "prow")
    picked = [every[k, i] for k, i in UPPER] + [every[4 * c + u, KB + v] for c, u, v in CHILD_SOURCES]
    lead_parts = lax.all_gather(jnp.stack(picked), "pcol")

    child_id, residue = row // 4, row % 4
    routed = []
    for flip in range(2):
        parity = (child_id + flip) % 2
        for d in range(3):
            block = 4 * parity + residue
            chosen = jnp.where(meta[child_id * 16 + block] == 3 * block + d, parity, parity + 2)
            piece = lax.dynamic_index_in_dim(child, chosen, 0, keepdims=False)
            perm = [(p, (3 * (p % 4) + d + 4 * ((p // 4 + flip) % 2)) % 8) for p in range(8)]
            routed.append(lax.ppermute(piece, "prow", perm))
    routed = jnp.stack(routed)

    panel = jnp.concatenate([lead, routed], axis=0).transpose(1, 0, 2, 3)
    panel = lax.all_to_all(panel, "pcol", 0, 0, tiled=True)
    slices = call(assemble_kernel, shaped((KB, 6, 32, LANES)), [SM, VM], [])(meta, panel[0:KB])

    even, odd = slices[:, 0::2], slices[:, 1::2]
    is_even = col % 2 == 0
    perm_a, perm_b = [], []
    for p in range(8):
        for s in range(16):
            perm_a.append((p * 16 + s, (s // 2) * 16 + p + 8 * (s % 2)))
            perm_b.append((p * 16 + s, (s // 2) * 16 + p + 8 * (1 - s % 2)))
    got_a = lax.ppermute(jnp.where(is_even, even, odd), ("prow", "pcol"), perm_a)
    got_b = lax.ppermute(jnp.where(is_even, odd, even), ("prow", "pcol"), perm_b)
    low_side = col < 8
    pair = jnp.stack([jnp.where(low_side, got_a, got_b), jnp.where(low_side, got_b, got_a)])

    left_parts = lax.all_gather(slices, "pcol")
    right_parts = lax.all_gather(pair, "prow").reshape(16, KB, 3, 32, LANES)

    moved = []
    for d in range(3):
        perm = [(q, (3 * q + d) % 16) for q in range(16) if 3 * q + d >= KB]
        moved.append(lax.ppermute(routed, "pcol", perm))
    moved = jnp.stack(moved).reshape(3, 6, 512, LANES)

    upper, th, tl = call(
        chain_kernel,
        (shaped((25, NB, NB)), shaped((25, NB, NB), BF16), shaped((25, NB, NB), BF16)),
        [SM, VM],
        [
            pltpu.VMEM((25, NB, NB), F32),
            pltpu.VMEM((NB, NB), F32),
            pltpu.VMEM((HB, HB), F32),
            pltpu.VMEM((HB, HB), F32),
            pltpu.VMEM((HB, HB), F32),
        ],
    )(meta, lead_parts)

    rh, rl = call(
        right_kernel,
        (shaped((768, 1280), BF16), shaped((768, 1280), BF16)),
        [VM, VM, VM],
        [pltpu.VMEM((768, 1280), F32)],
    )(right_parts, th, tl)

    rows = NB * ROWS_STEP
    whole3 = pl.BlockSpec((25, NB, NB), lambda g: (0, 0, 0))
    out = pl.pallas_call(
        schur_kernel,
        grid=(6 // ROWS_STEP,),
        out_shape=shaped((9216, LANES)),
        in_specs=[
            SM,
            pl.BlockSpec((16, KB, ROWS_STEP, 32, LANES), lambda g: (0, 0, g, 0, 0)),
            whole3,
            whole3,
            pl.BlockSpec((768, 1280), lambda g: (0, 0)),
            pl.BlockSpec((768, 1280), lambda g: (0, 0)),
            whole3,
            pl.BlockSpec((1536 * ROWS_STEP, LANES), lambda g: (g, 0)),
            pl.BlockSpec((3, 6, 512, LANES), lambda g: (0, 0, 0, 0)),
        ],
        out_specs=pl.BlockSpec((1536 * ROWS_STEP, LANES), lambda g: (g, 0)),
        scratch_shapes=[
            pltpu.VMEM((rows, 1280), F32),
            pltpu.VMEM((rows, 1280), BF16),
            pltpu.VMEM((rows, 1280), BF16),
        ],
        compiler_params=pltpu.CompilerParams(vmem_limit_bytes=VMEM_LIMIT),
    )(meta, left_parts, th, tl, rh, rl, upper, parent.reshape(9216, LANES), moved)
    return out.reshape(6, 1, NB, 3, 1, NB)


def solution(mesh):
    in_specs = (
        P(None, "prow", None, None, "pcol", None),
        P(None, "prow", None, None, "pcol", None),
        P(),
    )
    out_specs = P(None, "prow", None, None, "pcol", None)
    return jax.shard_map(
        per_device, mesh=mesh, in_specs=in_specs, out_specs=out_specs, check_vma=False
    )
```

```python
import functools
import jax
import jax.numpy as jnp
from jax import lax
from jax.experimental import pallas as pl
from jax.experimental.pallas import tpu as pltpu
from jax.sharding import PartitionSpec as P

KB = 5
NB = 256
HB = 128
LANES = 128
F32 = jnp.float32
BF16 = jnp.bfloat16
VMEM_LIMIT = 60 * 1024 * 1024
VM = pl.BlockSpec(memory_space=pltpu.VMEM)
SM = pl.BlockSpec(memory_space=pltpu.SMEM)


def route_of(meta, n):
    flip, d = n // 3, n % 3
    row = meta[32]
    residue = (3 * (row + 8 - d)) % 4
    parity = ((row + 16 - 3 * residue - d) // 4) % 2
    child = (parity + flip) % 2
    first = 4 * parity + residue
    second = first + 8
    is_first = meta[child * 16 + first] == 3 * first + d
    is_second = meta[child * 16 + second] == 3 * second + d
    block = jnp.where(is_first, first, second)
    return child, jnp.logical_or(is_first, is_second), (3 * block + d) // 8


def assemble_kernel(meta, first_ref, rest_ref, every_ref, more_ref, out_ref):
    for j in range(KB):
        out_ref[j, 0] = first_ref[j]
        out_ref[j, 1:6] = rest_ref[j]
    for child in range(2):
        for u in range(16):
            target = meta[child * 16 + u]

            @pl.when(target % 8 == meta[32])
            def _():
                for v in range(2):
                    column = meta[child * 16 + v]

                    @pl.when(column < KB)
                    def _():
                        source = 4 * child + u % 4
                        piece = every_ref[source, KB + v] if u < 4 else more_ref[source, v, u // 4 - 1]
                        out_ref[column, target // 8] = out_ref[column, target // 8] + piece


UPPER = [(k, i) for k in range(KB) for i in range(k, KB)]
CHILD_SOURCES = [(c, u, v) for c in range(2) for (u, v) in ((0, 0), (0, 1), (1, 1))]


def exact(a, b, dims):
    return lax.dot_general(a, b, (dims, ((), ())), precision=lax.Precision.HIGHEST, preferred_element_type=F32)


def factor_128(a_ref, x_ref, u_ref):
    shape = (8, LANES)
    lane = lax.broadcasted_iota(jnp.int32, (HB, LANES), 1)
    sub = lax.broadcasted_iota(jnp.int32, (HB, LANES), 0)
    x_ref[...] = jnp.where(lane == sub, 1.0, 0.0).astype(F32)
    for g in range(HB // 8):
        rows = slice(8 * g, 8 * g + 8)
        a_g = a_ref[rows, :]
        x_g = x_ref[rows, :]
        cols = [jnp.broadcast_to(a_g[:, 8 * g + s : 8 * g + s + 1], shape) for s in range(8)]
        d = [[jnp.broadcast_to(cols[s][t : t + 1, :], shape) for s in range(t + 1)] for t in range(8)]
        low = [[None] * 8 for _ in range(8)]
        rinv = []
        for s in range(8):
            r = lax.rsqrt(d[s][s])
            rinv.append(r)
            for t in range(s + 1, 8):
                low[t][s] = d[t][s] * r
            for t in range(s + 1, 8):
                for t2 in range(s + 1, t + 1):
                    d[t][t2] = d[t][t2] - low[t][s] * low[t2][s]
        ub, xb = [], []
        for t in range(8):
            ua = jnp.broadcast_to(a_g[t : t + 1, :], shape)
            xa = jnp.broadcast_to(x_g[t : t + 1, :], shape)
            for s in range(t):
                ua = ua - low[t][s] * ub[s]
                xa = xa - low[t][s] * xb[s]
            ub.append(ua * rinv[t])
            xb.append(xa * rinv[t])
            u_ref[8 * g + t : 8 * g + t + 1, :] = ub[t][0:1, :]
            x_ref[8 * g + t : 8 * g + t + 1, :] = xb[t][0:1, :]
        for i in range(g + 1, HB // 8):
            rows_i = slice(8 * i, 8 * i + 8)
            a_i = a_ref[rows_i, :]
            x_i = x_ref[rows_i, :]
            w = []
            for t in range(8):
                wt = jnp.broadcast_to(a_i[:, 8 * g + t : 8 * g + t + 1], shape)
                for s in range(t):
                    wt = wt - low[t][s] * w[s]
                w.append(wt * rinv[t])
            for t in range(8):
                a_i = a_i - w[t] * ub[t]
                x_i = x_i - w[t] * xb[t]
            a_ref[rows_i, :] = a_i
            x_ref[rows_i, :] = x_i
    u_ref[...] = jnp.where(lane >= sub, u_ref[...], 0.0)


def split(a):
    high = a.astype(BF16)
    return high, (a - high.astype(F32)).astype(BF16)


def chain_kernel(meta, parts_ref, u_ref, th_ref, tl_ref, f_ref, v_ref, a_s, x_s, u_s):
    def take(position, s, h):
        return parts_ref[s, position, pl.ds(h, 16, stride=2), :]

    for at, (k, i) in enumerate(UPPER):
        for s in range(16):
            for h in range(2):
                f_ref[k * KB + i, 16 * s : 16 * s + 16, HB * h : HB * h + HB] = take(at, s, h)
    for at, (c, u, v) in enumerate(CHILD_SOURCES):
        k = meta[c * 16 + u]
        i = meta[c * 16 + v]

        @pl.when(jnp.logical_and(k < KB, i < KB))
        def _():
            for s in range(16):
                for h in range(2):
                    place = (k * KB + i, slice(16 * s, 16 * s + 16), slice(HB * h, HB * h + HB))
                    f_ref[place] = f_ref[place] + take(15 + at, s, h)

    th_ref[...] = jnp.zeros_like(th_ref)
    tl_ref[...] = jnp.zeros_like(tl_ref)
    u_ref[...] = jnp.zeros_like(u_ref)

    @pl.loop(0, 2 * KB)
    def _(step):
        k = step // 2
        half = step % 2
        kk = k * KB + k

        @pl.when(half == 0)
        def _():
            a_s[...] = f_ref[kk, 0:HB, 0:HB]

        @pl.when(half == 1)
        def _():
            u12 = exact(v_ref[0:HB, 0:HB], f_ref[kk, 0:HB, HB:NB], ((1,), (0,)))
            u_ref[kk, 0:HB, HB:NB] = u12
            a_s[...] = f_ref[kk, HB:NB, HB:NB] - exact(u12, u12, ((0,), (0,)))

        factor_128(a_s, x_s, u_s)

        @pl.when(half == 0)
        def _():
            u_ref[kk, 0:HB, 0:HB] = u_s[...]
            v_ref[0:HB, 0:HB] = x_s[...]

        @pl.when(half == 1)
        def _():
            u_ref[kk, HB:NB, HB:NB] = u_s[...]
            v_ref[HB:NB, HB:NB] = x_s[...]
            v_ref[0:HB, HB:NB] = jnp.zeros((HB, HB), F32)
            lx = exact(u_ref[kk, 0:HB, HB:NB], v_ref[0:HB, 0:HB], ((0,), (0,)))
            v_ref[HB:NB, 0:HB] = -exact(x_s[...], lx, ((1,), (0,)))
            high, low = split(v_ref[...].T)
            th_ref[kk] = high
            tl_ref[kk] = low

            @pl.loop(k + 1, KB)
            def _(i):
                u = exact(v_ref[...], f_ref[k * KB + i], ((1,), (0,)))
                u_ref[k * KB + i] = u
                high, low = split(u)
                th_ref[k * KB + i] = high
                tl_ref[k * KB + i] = low

            @pl.loop(k + 1, KB)
            def _(i):
                @pl.loop(i, KB)
                def _(j):
                    f_ref[i * KB + j] = f_ref[i * KB + j] - exact(
                        u_ref[k * KB + i], u_ref[k * KB + j], ((0,), (0,))
                    )


def dot3(ah, al, bh, bl, dims):
    def dot(a, b):
        return lax.dot_general(a, b, (dims, ((), ())), preferred_element_type=F32)

    return dot(ah, bh) + (dot(ah, bl) + dot(al, bh))


NN = ((1,), (0,))
NT = ((1,), (1,))


def solve_rows(raw_ref, yh_ref, yl_ref, th_ref, tl_ref):
    for k in range(KB):
        at = slice(NB * k, NB * k + NB)
        t = raw_ref[:, at]
        for m in range(k):
            am = slice(NB * m, NB * m + NB)
            t = t - dot3(yh_ref[:, am], yl_ref[:, am], th_ref[m * KB + k], tl_ref[m * KB + k], NN)
        high, low = split(t)
        y = dot3(high, low, th_ref[k * KB + k], tl_ref[k * KB + k], NN)
        raw_ref[:, at] = y
        high, low = split(y)
        yh_ref[:, at] = high
        yl_ref[:, at] = low


def right_kernel(parts_ref, th_ref, tl_ref, yh_ref, yl_ref, raw):
    @pl.loop(0, 16)
    def _(s):
        for c in range(3):
            for j in range(KB):
                for h in range(2):
                    raw[pl.ds(pl.multiple_of(NB * c + 16 * s, 16), 16), NB * j + HB * h : NB * j + HB * h + HB] = parts_ref[
                        s, j, c, pl.ds(h, 16, stride=2), :
                    ]
    solve_rows(raw, yh_ref, yl_ref, th_ref, tl_ref)


ROWS_STEP = 2


def schur_kernel(meta, parts_ref, th_ref, tl_ref, rh_ref, rl_ref, u_ref, parent_ref, child_ref, out_ref, raw, yh, yl):
    step = pl.program_id(0)
    row, col = meta[32], meta[33]

    @pl.loop(0, 16)
    def _(s):
        for a in range(ROWS_STEP):
            for j in range(KB):
                for h in range(2):
                    raw[pl.ds(pl.multiple_of(NB * a + 16 * s, 16), 16), NB * j + HB * h : NB * j + HB * h + HB] = parts_ref[
                        s, j, a, pl.ds(h, 16, stride=2), :
                    ]
    solve_rows(raw, yh, yl, th_ref, tl_ref)
    for a in range(ROWS_STEP):
        slot = step * ROWS_STEP + a
        block_row = row + 8 * slot
        rows = slice(NB * a, NB * a + NB)
        for c in range(3):
            block_col = col + 16 * c

            def put(h, value):
                out_ref[pl.ds(1536 * a + 2 * c + h, NB, stride=6), :] = value

            @pl.when(jnp.logical_and(block_row >= KB, block_col >= KB))
            def _():
                cols = slice(NB * c, NB * c + NB)
                product = dot3(yh[rows, :], yl[rows, :], rh_ref[cols, :], rl_ref[cols, :], NT)
                for h in range(2):
                    put(h, parent_ref[pl.ds(1536 * a + 2 * c + h, NB, stride=6), :] - product[:, HB * h : HB * h + HB])
                turn = block_col % 3
                source = block_col // 3
                for n in range(6):
                    child, there, to = route_of(meta, n)
                    here = jnp.logical_and(there, to == slot)

                    @pl.when(jnp.logical_and(here, meta[child * 16 + source] == block_col))
                    def _():
                        for h in range(2):
                            at = pl.ds(1536 * a + 2 * c + h, NB, stride=6)
                            out_ref[at, :] = out_ref[at, :] + child_ref[turn, n, pl.ds(h, NB, stride=2), :]

            @pl.when(jnp.logical_and(block_row < KB, block_col >= KB))
            def _():
                for h in range(2):
                    put(h, jnp.zeros((NB, HB), F32))

            if c == 0:

                @pl.when(jnp.logical_and(block_row >= KB, block_col < KB))
                def _():
                    for j in range(KB):

                        @pl.when(block_col == j)
                        def _():
                            for h in range(2):
                                put(h, raw[rows, NB * j + HB * h : NB * j + HB * h + HB])

                @pl.when(jnp.logical_and(block_row < KB, block_col < KB))
                def _():
                    block = u_ref[jnp.minimum(block_col, KB - 1) * KB + jnp.minimum(block_row, KB - 1)].T
                    for h in range(2):
                        put(h, block[:, HB * h : HB * h + HB])


def cost(microseconds):
    return pl.CostEstimate(flops=int(microseconds * 1.1e9), bytes_accessed=1 << 20, transcendentals=0)


def call(kernel, out_shape, in_specs, scratch, microseconds=2):
    return pl.pallas_call(
        kernel,
        out_shape=out_shape,
        in_specs=in_specs,
        out_specs=jax.tree.map(lambda _: VM, out_shape),
        scratch_shapes=scratch,
        compiler_params=pltpu.CompilerParams(vmem_limit_bytes=VMEM_LIMIT),
        cost_estimate=cost(microseconds),
    )


def shaped(shape, dtype=F32):
    return jax.ShapeDtypeStruct(shape, dtype)


def per_device(parent, children, index_maps):
    row = lax.axis_index("prow")
    col = lax.axis_index("pcol")
    meta = jnp.concatenate([index_maps.reshape(-1), jnp.stack([row, col]).astype(jnp.int32)])
    front = parent.reshape(6, NB, 3, 2, LANES)
    lead = front[:, :, 0].reshape(6, 16, 32, LANES)
    child = children.reshape(4, 16, 32, LANES)

    first = jnp.stack([lead[0], child[0]], axis=1)
    first = lax.all_to_all(first, "pcol", 0, 0, tiled=True)
    mine = jnp.concatenate([first[0:KB, 0], first[0:2, 1]], axis=0)
    every = lax.all_gather(mine, "prow")
    picked = [every[k, i] for k, i in UPPER] + [every[4 * c + u, KB + v] for c, u, v in CHILD_SOURCES]
    lead_parts = lax.all_gather(jnp.stack(picked), "pcol")

    rest = jnp.concatenate([lead[1:], child[1:]], axis=0).transpose(1, 0, 2, 3)
    rest, every = lax.optimization_barrier((rest, every))
    rest = lax.all_to_all(rest, "pcol", 0, 0, tiled=True)
    more = lax.all_gather(rest[0:2, 5:8], "prow")
    slices = call(assemble_kernel, shaped((KB, 6, 32, LANES)), [SM, VM, VM, VM, VM], [])(
        meta, mine[0:KB], rest[0:KB, 0:5], every, more
    )

    child_id, residue = row // 4, row % 4
    free, _ = lax.optimization_barrier((child, every))
    routed = []
    for flip in range(2):
        parity = (child_id + flip) % 2
        for d in range(3):
            block = 4 * parity + residue
            chosen = jnp.where(meta[child_id * 16 + block] == 3 * block + d, parity, parity + 2)
            piece = lax.dynamic_index_in_dim(free, chosen, 0, keepdims=False)
            perm = [(p, (3 * (p % 4) + d + 4 * ((p // 4 + flip) % 2)) % 8) for p in range(8)]
            routed.append(lax.ppermute(piece, "prow", perm))
    routed = jnp.stack(routed)

    even, odd = slices[:, 0::2], slices[:, 1::2]
    is_even = col % 2 == 0
    perm_a, perm_b = [], []
    for p in range(8):
        for s in range(16):
            perm_a.append((p * 16 + s, (s // 2) * 16 + p + 8 * (s % 2)))
            perm_b.append((p * 16 + s, (s // 2) * 16 + p + 8 * (1 - s % 2)))
    got_a = lax.ppermute(jnp.where(is_even, even, odd), ("prow", "pcol"), perm_a)
    got_b = lax.ppermute(jnp.where(is_even, odd, even), ("prow", "pcol"), perm_b)
    low_side = col < 8
    pair = jnp.stack([jnp.where(low_side, got_a, got_b), jnp.where(low_side, got_b, got_a)])

    left_parts = lax.all_gather(slices, "pcol")
    pairs = jnp.broadcast_to(pair[None], (8,) + pair.shape)
    right_parts = lax.all_to_all(pairs, "prow", 0, 0, tiled=True).reshape(16, KB, 3, 32, LANES)

    moved = []
    for d in range(3):
        perm = [(q, (3 * q + d) % 16) for q in range(16) if 3 * q + d >= KB]
        moved.append(lax.ppermute(routed, "pcol", perm))
    moved = jnp.stack(moved).reshape(3, 6, 512, LANES)

    upper, th, tl = call(
        chain_kernel,
        (shaped((25, NB, NB)), shaped((25, NB, NB), BF16), shaped((25, NB, NB), BF16)),
        [SM, VM],
        [
            pltpu.VMEM((25, NB, NB), F32),
            pltpu.VMEM((NB, NB), F32),
            pltpu.VMEM((HB, HB), F32),
            pltpu.VMEM((HB, HB), F32),
            pltpu.VMEM((HB, HB), F32),
        ],
        70,
    )(meta, lead_parts)

    rh, rl = call(
        right_kernel,
        (shaped((768, 1280), BF16), shaped((768, 1280), BF16)),
        [VM, VM, VM],
        [pltpu.VMEM((768, 1280), F32)],
        12,
    )(right_parts, th, tl)

    rows = NB * ROWS_STEP
    whole3 = pl.BlockSpec((25, NB, NB), lambda g: (0, 0, 0))
    out = pl.pallas_call(
        schur_kernel,
        grid=(6 // ROWS_STEP,),
        out_shape=shaped((9216, LANES)),
        in_specs=[
            SM,
            pl.BlockSpec((16, KB, ROWS_STEP, 32, LANES), lambda g: (0, 0, g, 0, 0)),
            whole3,
            whole3,
            pl.BlockSpec((768, 1280), lambda g: (0, 0)),
            pl.BlockSpec((768, 1280), lambda g: (0, 0)),
            whole3,
            pl.BlockSpec((1536 * ROWS_STEP, LANES), lambda g: (g, 0)),
            pl.BlockSpec((3, 6, 512, LANES), lambda g: (0, 0, 0, 0)),
        ],
        out_specs=pl.BlockSpec((1536 * ROWS_STEP, LANES), lambda g: (g, 0)),
        scratch_shapes=[
            pltpu.VMEM((rows, 1280), F32),
            pltpu.VMEM((rows, 1280), BF16),
            pltpu.VMEM((rows, 1280), BF16),
        ],
        compiler_params=pltpu.CompilerParams(vmem_limit_bytes=VMEM_LIMIT),
        cost_estimate=cost(33),
    )(meta, left_parts, th, tl, rh, rl, upper, parent.reshape(9216, LANES), moved)
    return out.reshape(6, 1, NB, 3, 1, NB)


def solution(mesh):
    in_specs = (
        P(None, "prow", None, None, "pcol", None),
        P(None, "prow", None, None, "pcol", None),
        P(),
    )
    out_specs = P(None, "prow", None, None, "pcol", None)
    return jax.shard_map(
        per_device, mesh=mesh, in_specs=in_specs, out_specs=out_specs, check_vma=False
    )
```

```python
import jax
import jax.numpy as jnp
from jax import lax
from jax.experimental import pallas as pl
from jax.experimental.pallas import tpu as pltpu
from jax.sharding import PartitionSpec as P

KB = 5
NB = 256
HB = 128
LANES = 128
F32 = jnp.float32
BF16 = jnp.bfloat16
VMEM_LIMIT = 60 * 1024 * 1024
VM = pl.BlockSpec(memory_space=pltpu.VMEM)
SM = pl.BlockSpec(memory_space=pltpu.SMEM)


def route_of(meta, child, residue):
    there, slot = False, 0
    for turn in range(4):
        target = meta[child * 16 + 4 * turn + residue]
        here = target % 8 == meta[32]
        there = jnp.logical_or(there, here)
        slot = jnp.where(here, target // 8, slot)
    return there, slot


def turn_for(meta, target_row):
    child, residue = meta[32] // 4, meta[32] % 4
    chosen = 0
    for turn in range(1, 4):
        chosen = jnp.where(meta[child * 16 + 4 * turn + residue] % 8 == target_row, turn, chosen)
    return chosen


def residue_of(row, e):
    return (3 * row + 4 + e) % 4


def pick_kernel(meta, parts_ref, out_ref):
    for target_row in range(8):
        turn = turn_for(meta, target_row)
        for v in range(2):
            out_ref[target_row, v] = parts_ref[v, turn]


def copy_kernel(meta, block_ref, out_ref):
    out_ref[...] = block_ref[...]


def assemble_kernel(meta, first_ref, rest_ref, got_ref, out_ref):
    for j in range(KB):
        out_ref[j, 0] = first_ref[j]
        out_ref[j, 1:6] = rest_ref[j]
    for child in range(2):
        for residue in range(4):
            there, slot = route_of(meta, child, residue)
            for v in range(2):
                column = meta[child * 16 + v]

                @pl.when(jnp.logical_and(there, column < KB))
                def _():
                    out_ref[column, slot] = out_ref[column, slot] + got_ref[4 * child + residue, v]


def chunk_kernel(meta, mine_ref, got_a_ref, got_b_ref, out_ref):
    for row, picks in enumerate(CHUNKS):

        @pl.when(meta[32] == row)
        def _():
            for at in range(3):
                kind, index = picks[at] if at < len(picks) else (0, 0)
                source = (mine_ref, got_a_ref, got_b_ref)[kind]
                out_ref[at] = source[index]


CHUNKS = [
    [(0, 0), (0, 5), (0, 6)],
    [(0, 1), (0, 2), (0, 6)],
    [(0, 2), (0, 3), (0, 4)],
    [(0, 3), (0, 4)],
    [(0, 4), (0, 5), (0, 6)],
    [(1, 0), (1, 1), (0, 6)],
    [(1, 0), (1, 1), (1, 2)],
    [(2, 0)],
]
UPPER_AT = {
    (0, 0): (0, 0),
    (0, 1): (7, 0),
    (0, 2): (6, 0),
    (0, 3): (6, 1),
    (0, 4): (6, 2),
    (1, 1): (1, 0),
    (1, 2): (1, 1),
    (1, 3): (5, 0),
    (1, 4): (5, 1),
    (2, 2): (2, 0),
    (2, 3): (2, 1),
    (2, 4): (2, 2),
    (3, 3): (3, 0),
    (3, 4): (3, 1),
    (4, 4): (4, 0),
}
CHILD_AT = {
    (0, 0, 0): (0, 1),
    (0, 0, 1): (0, 2),
    (0, 1, 1): (1, 2),
    (1, 0, 0): (4, 1),
    (1, 0, 1): (4, 2),
    (1, 1, 1): (5, 2),
}


def exact(a, b, dims):
    return lax.dot_general(a, b, (dims, ((), ())), precision=lax.Precision.HIGHEST, preferred_element_type=F32)


def factor_128(a_ref, x_ref, u_ref):
    shape = (8, LANES)
    lane = lax.broadcasted_iota(jnp.int32, (HB, LANES), 1)
    sub = lax.broadcasted_iota(jnp.int32, (HB, LANES), 0)
    x_ref[...] = jnp.where(lane == sub, 1.0, 0.0).astype(F32)
    for g in range(HB // 8):
        rows = slice(8 * g, 8 * g + 8)
        a_g = a_ref[rows, :]
        x_g = x_ref[rows, :]
        cols = [jnp.broadcast_to(a_g[:, 8 * g + s : 8 * g + s + 1], shape) for s in range(8)]
        d = [[jnp.broadcast_to(cols[s][t : t + 1, :], shape) for s in range(t + 1)] for t in range(8)]
        low = [[None] * 8 for _ in range(8)]
        rinv = []
        for s in range(8):
            r = lax.rsqrt(d[s][s])
            rinv.append(r)
            for t in range(s + 1, 8):
                low[t][s] = d[t][s] * r
            for t in range(s + 1, 8):
                for t2 in range(s + 1, t + 1):
                    d[t][t2] = d[t][t2] - low[t][s] * low[t2][s]
        ub, xb = [], []
        for t in range(8):
            ua = jnp.broadcast_to(a_g[t : t + 1, :], shape)
            xa = jnp.broadcast_to(x_g[t : t + 1, :], shape)
            for s in range(t):
                ua = ua - low[t][s] * ub[s]
                xa = xa - low[t][s] * xb[s]
            ub.append(ua * rinv[t])
            xb.append(xa * rinv[t])
            u_ref[8 * g + t : 8 * g + t + 1, :] = ub[t][0:1, :]
            x_ref[8 * g + t : 8 * g + t + 1, :] = xb[t][0:1, :]
        for i in range(g + 1, HB // 8):
            rows_i = slice(8 * i, 8 * i + 8)
            a_i = a_ref[rows_i, :]
            x_i = x_ref[rows_i, :]
            w = []
            for t in range(8):
                wt = jnp.broadcast_to(a_i[:, 8 * g + t : 8 * g + t + 1], shape)
                for s in range(t):
                    wt = wt - low[t][s] * w[s]
                w.append(wt * rinv[t])
            for t in range(8):
                a_i = a_i - w[t] * ub[t]
                x_i = x_i - w[t] * xb[t]
            a_ref[rows_i, :] = a_i
            x_ref[rows_i, :] = x_i
    u_ref[...] = jnp.where(lane >= sub, u_ref[...], 0.0)


def split(a):
    high = a.astype(BF16)
    return high, (a - high.astype(F32)).astype(BF16)


CUT = 2
REST = KB - CUT


def eliminate(n, steps, f_ref, u_ref, th_ref, tl_ref, v_ref, a_s, x_s, u_s):
    @pl.loop(0, 2 * steps)
    def _(step):
        k = step // 2
        half = step % 2
        kk = k * n + k

        @pl.when(half == 0)
        def _():
            a_s[...] = f_ref[kk, 0:HB, 0:HB]

        @pl.when(half == 1)
        def _():
            u12 = exact(v_ref[0:HB, 0:HB], f_ref[kk, 0:HB, HB:NB], ((1,), (0,)))
            u_ref[kk, 0:HB, HB:NB] = u12
            a_s[...] = f_ref[kk, HB:NB, HB:NB] - exact(u12, u12, ((0,), (0,)))

        factor_128(a_s, x_s, u_s)

        @pl.when(half == 0)
        def _():
            u_ref[kk, 0:HB, 0:HB] = u_s[...]
            v_ref[0:HB, 0:HB] = x_s[...]

        @pl.when(half == 1)
        def _():
            u_ref[kk, HB:NB, HB:NB] = u_s[...]
            u_ref[kk, HB:NB, 0:HB] = jnp.zeros((HB, HB), F32)
            v_ref[HB:NB, HB:NB] = x_s[...]
            v_ref[0:HB, HB:NB] = jnp.zeros((HB, HB), F32)
            lx = exact(u_ref[kk, 0:HB, HB:NB], v_ref[0:HB, 0:HB], ((0,), (0,)))
            v_ref[HB:NB, 0:HB] = -exact(x_s[...], lx, ((1,), (0,)))
            high, low = split(v_ref[...].T)
            th_ref[kk] = high
            tl_ref[kk] = low

            @pl.loop(k + 1, n)
            def _(i):
                u = exact(v_ref[...], f_ref[k * n + i], ((1,), (0,)))
                u_ref[k * n + i] = u
                high, low = split(u)
                th_ref[k * n + i] = high
                tl_ref[k * n + i] = low

            @pl.loop(k + 1, n)
            def _(i):
                @pl.loop(i, n)
                def _(j):
                    f_ref[i * n + j] = f_ref[i * n + j] - exact(u_ref[k * n + i], u_ref[k * n + j], ((0,), (0,)))


def chain_head_kernel(meta, parts_ref, u_ref, th_ref, tl_ref, rest_ref, f_ref, *scratch):
    def take(at, s, h):
        return parts_ref[at[0], s, at[1], pl.ds(h, 16, stride=2), :]

    for (k, i), at in UPPER_AT.items():
        for s in range(16):
            for h in range(2):
                f_ref[k * KB + i, 16 * s : 16 * s + 16, HB * h : HB * h + HB] = take(at, s, h)
    for (c, u, v), at in CHILD_AT.items():
        k = meta[c * 16 + u]
        i = meta[c * 16 + v]

        @pl.when(jnp.logical_and(k < KB, i < KB))
        def _():
            for s in range(16):
                for h in range(2):
                    place = (k * KB + i, slice(16 * s, 16 * s + 16), slice(HB * h, HB * h + HB))
                    f_ref[place] = f_ref[place] + take(at, s, h)

    for ref in (th_ref, tl_ref, u_ref):
        ref[KB] = jnp.zeros((NB, NB), ref.dtype)
    eliminate(KB, CUT, f_ref, u_ref, th_ref, tl_ref, *scratch)
    for i in range(REST):
        for j in range(REST):
            if j >= i:
                rest_ref[i * REST + j] = f_ref[(CUT + i) * KB + CUT + j]
            else:
                rest_ref[i * REST + j] = jnp.zeros((NB, NB), F32)


def chain_tail_kernel(rest_ref, u_ref, th_ref, tl_ref, f_ref, *scratch):
    f_ref[...] = rest_ref[...]
    for i in range(REST):
        for j in range(i):
            for ref in (th_ref, tl_ref, u_ref):
                ref[i * REST + j] = jnp.zeros((NB, NB), ref.dtype)
    eliminate(REST, REST, f_ref, u_ref, th_ref, tl_ref, *scratch)


def dot3(ah, al, bh, bl, dims):
    def dot(a, b):
        return lax.dot_general(a, b, (dims, ((), ())), preferred_element_type=F32)

    return dot(ah, bh) + (dot(ah, bl) + dot(al, bh))


NN = ((1,), (0,))
NT = ((1,), (1,))


def solve_rows(raw_ref, yh_ref, yl_ref, factors):
    head_h, head_l, tail_h, tail_l = factors

    def factor(m, k):
        if m < CUT:
            return head_h[m * KB + k], head_l[m * KB + k]
        at = (m - CUT) * REST + k - CUT
        return tail_h[at], tail_l[at]

    for k in range(KB):
        at = slice(NB * k, NB * k + NB)
        t = raw_ref[:, at]
        for m in range(k):
            am = slice(NB * m, NB * m + NB)
            t = t - dot3(yh_ref[:, am], yl_ref[:, am], *factor(m, k), NN)
        high, low = split(t)
        y = dot3(high, low, *factor(k, k), NN)
        raw_ref[:, at] = y
        high, low = split(y)
        yh_ref[:, at] = high
        yl_ref[:, at] = low


def right_kernel(parts_ref, hh_ref, hl_ref, th_ref, tl_ref, yh_ref, yl_ref, raw):
    @pl.loop(0, 16)
    def _(s):
        for c in range(3):
            for j in range(KB):
                for h in range(2):
                    raw[pl.ds(pl.multiple_of(NB * c + 16 * s, 16), 16), NB * j + HB * h : NB * j + HB * h + HB] = parts_ref[
                        s, j, c, pl.ds(h, 16, stride=2), :
                    ]
    solve_rows(raw, yh_ref, yl_ref, (hh_ref, hl_ref, th_ref, tl_ref))


ROWS_STEP = 2


def left_kernel(meta, parts_ref, hh_ref, hl_ref, th_ref, tl_ref, yh_ref, yl_ref, own_ref, raw):
    @pl.loop(0, 16)
    def _(s):
        for a in range(ROWS_STEP):
            for j in range(KB):
                for h in range(2):
                    raw[pl.ds(pl.multiple_of(NB * a + 16 * s, 16), 16), NB * j + HB * h : NB * j + HB * h + HB] = parts_ref[
                        s, j, a, pl.ds(h, 16, stride=2), :
                    ]
    solve_rows(raw, yh_ref, yl_ref, (hh_ref, hl_ref, th_ref, tl_ref))
    for j in range(KB):

        @pl.when(meta[33] == j)
        def _():
            own_ref[...] = raw[:, NB * j : NB * j + NB]


def schur_kernel(meta, yh, yl, own_ref, rh_ref, rl_ref, head_ref, tail_ref, parent_ref, child_0, child_1, child_2, out_ref):
    step = pl.program_id(0)
    row, col = meta[32], meta[33]
    routes = []
    for child in range(2):
        for e in range(3):
            routes.append((child, *route_of(meta, child, residue_of(row, e))))

    for a in range(ROWS_STEP):
        slot = step * ROWS_STEP + a
        block_row = row + 8 * slot
        rows = slice(NB * a, NB * a + NB)
        for c in range(3):
            block_col = col + 16 * c

            def put(h, value):
                out_ref[pl.ds(1536 * a + 2 * c + h, NB, stride=6), :] = value

            @pl.when(jnp.logical_and(block_row >= KB, block_col >= KB))
            def _():
                cols = slice(NB * c, NB * c + NB)
                product = dot3(yh[rows, :], yl[rows, :], rh_ref[cols, :], rl_ref[cols, :], NT)
                for h in range(2):
                    put(h, parent_ref[pl.ds(1536 * a + 2 * c + h, NB, stride=6), :] - product[:, HB * h : HB * h + HB])
                turn = block_col % 3
                source = block_col // 3
                for n, (child, there, to) in enumerate(routes):
                    here = jnp.logical_and(there, to == slot)
                    here = jnp.logical_and(here, meta[child * 16 + source] == block_col)
                    for d, child_ref in enumerate((child_0, child_1, child_2)):

                        @pl.when(jnp.logical_and(here, turn == d))
                        def _():
                            for h in range(2):
                                at = pl.ds(1536 * a + 2 * c + h, NB, stride=6)
                                out_ref[at, :] = out_ref[at, :] + child_ref[n, pl.ds(h, NB, stride=2), :]

            @pl.when(jnp.logical_and(block_row < KB, block_col >= KB))
            def _():
                for h in range(2):
                    put(h, jnp.zeros((NB, HB), F32))

            if c == 0:

                @pl.when(jnp.logical_and(block_row >= KB, block_col < KB))
                def _():
                    for h in range(2):
                        put(h, own_ref[rows, HB * h : HB * h + HB])

                in_lead = jnp.logical_and(block_row < KB, block_col < KB)
                upper = block_row < block_col

                @pl.when(jnp.logical_and(in_lead, upper))
                def _():
                    for h in range(2):
                        put(h, jnp.zeros((NB, HB), F32))

                lower = jnp.logical_and(in_lead, jnp.logical_not(upper))

                @pl.when(jnp.logical_and(lower, block_col < CUT))
                def _():
                    block = head_ref[jnp.minimum(block_col, CUT - 1) * KB + jnp.minimum(block_row, KB - 1)].T
                    for h in range(2):
                        put(h, block[:, HB * h : HB * h + HB])

                @pl.when(jnp.logical_and(lower, block_col >= CUT))
                def _():
                    at_col = jnp.clip(block_col - CUT, 0, REST - 1)
                    block = tail_ref[at_col * REST + jnp.clip(block_row - CUT, 0, REST - 1)].T
                    for h in range(2):
                        put(h, block[:, HB * h : HB * h + HB])


def cost(microseconds):
    return pl.CostEstimate(flops=int(microseconds * 1.1e9), bytes_accessed=1 << 20, transcendentals=0)


def call(kernel, out_shape, in_specs, scratch, microseconds=2):
    return pl.pallas_call(
        kernel,
        out_shape=out_shape,
        in_specs=in_specs,
        out_specs=jax.tree.map(lambda _: VM, out_shape),
        scratch_shapes=scratch,
        compiler_params=pltpu.CompilerParams(vmem_limit_bytes=VMEM_LIMIT),
        cost_estimate=cost(microseconds),
    )


def shaped(shape, dtype=F32):
    return jax.ShapeDtypeStruct(shape, dtype)


def per_device(parent, children, index_maps):
    row = lax.axis_index("prow")
    col = lax.axis_index("pcol")
    meta = jnp.concatenate([index_maps.reshape(-1), jnp.stack([row, col]).astype(jnp.int32)])
    front = parent.reshape(6, NB, 3, 2, LANES)
    lead = front[:, :, 0].reshape(6, 16, 32, LANES)
    child = children.reshape(4, 16, 32, LANES)

    picked = pl.pallas_call(
        copy_kernel,
        grid_spec=pltpu.PrefetchScalarGridSpec(
            num_scalar_prefetch=1,
            grid=(8,),
            in_specs=[pl.BlockSpec((1, 512, LANES), lambda t, meta: (turn_for(meta, t), 0, 0))],
            out_specs=pl.BlockSpec((1, 512, LANES), lambda t, meta: (t, 0, 0)),
        ),
        out_shape=shaped((8, 512, LANES)),
        cost_estimate=cost(3),
    )(meta, child.reshape(4, 512, LANES))

    first = jnp.stack([lead[0], child[0]], axis=1)
    first = lax.all_to_all(first, "pcol", 0, 0, tiled=True)
    mine = jnp.concatenate([first[0:KB, 0], first[0:2, 1]], axis=0)
    shed = jnp.where(row == 0, mine[2:5], mine[3:6])
    got_a = lax.ppermute(shed, "prow", [(0, 6), (1, 5)])
    got_b = lax.ppermute(mine[1:2], "prow", [(0, 7)])
    chunk = call(chunk_kernel, shaped((3, 32, LANES)), [SM, VM, VM, VM], [])(meta, mine, got_a, got_b)
    chunk = lax.all_gather(chunk, "pcol")
    lead_parts = lax.all_gather(chunk, "prow")

    rest = jnp.concatenate([lead[1:], child], axis=0).transpose(1, 0, 2, 3)
    rest, chunk = lax.optimization_barrier((rest, chunk))
    rest = lax.all_to_all(rest, "pcol", 0, 0, tiled=True)
    pieces = call(pick_kernel, shaped((8, 2, 32, LANES)), [SM, VM], [])(meta, rest[0:2, 5:9])
    pieces = lax.all_to_all(pieces, "prow", 0, 0, tiled=True)
    slices = call(assemble_kernel, shaped((KB, 6, 32, LANES)), [SM, VM, VM, VM], [])(
        meta, mine[0:KB], rest[0:KB, 0:5], pieces
    )

    left_parts = lax.all_gather(slices, "pcol")

    lead_parts, slices, picked = lax.optimization_barrier((lead_parts, slices, picked))
    got = lax.all_to_all(picked, "prow", 0, 0, tiled=True)
    routed = jnp.stack(
        [
            lax.dynamic_index_in_dim(got, 4 * c + residue_of(row, e), 0, keepdims=False)
            for c in range(2)
            for e in range(3)
        ]
    )
    even, odd = slices[:, 0::2], slices[:, 1::2]
    is_even = col % 2 == 0
    perm_a, perm_b = [], []
    for p in range(8):
        for s in range(16):
            perm_a.append((p * 16 + s, (s // 2) * 16 + p + 8 * (s % 2)))
            perm_b.append((p * 16 + s, (s // 2) * 16 + p + 8 * (1 - s % 2)))
    pair_a = lax.ppermute(jnp.where(is_even, even, odd), ("prow", "pcol"), perm_a)
    pair_b = lax.ppermute(jnp.where(is_even, odd, even), ("prow", "pcol"), perm_b)
    low_side = col < 8
    pair = jnp.stack([jnp.where(low_side, pair_a, pair_b), jnp.where(low_side, pair_b, pair_a)])
    pairs = jnp.broadcast_to(pair[None], (8,) + pair.shape)

    scratch = [
        pltpu.VMEM((NB, NB), F32),
        pltpu.VMEM((HB, HB), F32),
        pltpu.VMEM((HB, HB), F32),
        pltpu.VMEM((HB, HB), F32),
    ]
    heads = CUT * KB
    head_u, head_h, head_l, left_over = call(
        chain_head_kernel,
        (
            shaped((heads, NB, NB)),
            shaped((heads, NB, NB), BF16),
            shaped((heads, NB, NB), BF16),
            shaped((REST * REST, NB, NB)),
        ),
        [SM, VM],
        [pltpu.VMEM((KB * KB, NB, NB), F32)] + scratch,
        32,
    )(meta, lead_parts)

    left_over, pairs, routed = lax.optimization_barrier((left_over, pairs, routed))
    right_parts = lax.all_to_all(pairs, "prow", 0, 0, tiled=True).reshape(16, KB, 3, 32, LANES)
    middle = lax.ppermute(routed, "pcol", [(q, (3 * q + 1) % 16) for q in range(1, 16)])
    tails = REST * REST
    tail_u, tail_h, tail_l = call(
        chain_tail_kernel,
        (shaped((tails, NB, NB)), shaped((tails, NB, NB), BF16), shaped((tails, NB, NB), BF16)),
        [VM],
        [pltpu.VMEM((tails, NB, NB), F32)] + scratch,
        40,
    )(left_over)

    middle, tail_h = lax.optimization_barrier((middle, tail_h))
    below = lax.ppermute(middle, "pcol", [(q, (q + 1) % 16) for q in range(16)])
    above = lax.ppermute(middle, "pcol", [(q, (q + 15) % 16) for q in range(16)])

    rh, rl = call(
        right_kernel,
        (shaped((768, 1280), BF16), shaped((768, 1280), BF16)),
        [VM] * 5,
        [pltpu.VMEM((768, 1280), F32)],
        12,
    )(right_parts, head_h, head_l, tail_h, tail_l)

    rows = NB * ROWS_STEP
    steps = 6 // ROWS_STEP
    whole_head = pl.BlockSpec((heads, NB, NB), lambda g: (0, 0, 0))
    whole_tail = pl.BlockSpec((tails, NB, NB), lambda g: (0, 0, 0))
    by_rows = pl.BlockSpec((rows, 1280), lambda g: (g, 0))
    own_rows = pl.BlockSpec((rows, NB), lambda g: (g, 0))
    yh, yl, own = pl.pallas_call(
        left_kernel,
        grid=(steps,),
        out_shape=(shaped((1536, 1280), BF16), shaped((1536, 1280), BF16), shaped((1536, NB))),
        in_specs=[
            SM,
            pl.BlockSpec((16, KB, ROWS_STEP, 32, LANES), lambda g: (0, 0, g, 0, 0)),
            whole_head,
            whole_head,
            whole_tail,
            whole_tail,
        ],
        out_specs=(by_rows, by_rows, own_rows),
        scratch_shapes=[pltpu.VMEM((rows, 1280), F32)],
        compiler_params=pltpu.CompilerParams(vmem_limit_bytes=VMEM_LIMIT),
        cost_estimate=cost(20),
    )(meta, left_parts, head_h, head_l, tail_h, tail_l)

    whole_right = pl.BlockSpec((768, 1280), lambda g: (0, 0))
    whole_child = pl.BlockSpec((6, 512, LANES), lambda g: (0, 0, 0))
    front_rows = pl.BlockSpec((1536 * ROWS_STEP, LANES), lambda g: (g, 0))
    out = pl.pallas_call(
        schur_kernel,
        grid=(steps,),
        out_shape=shaped((9216, LANES)),
        in_specs=[SM, by_rows, by_rows, own_rows, whole_right, whole_right, whole_head, whole_tail, front_rows]
        + [whole_child] * 3,
        out_specs=front_rows,
        compiler_params=pltpu.CompilerParams(vmem_limit_bytes=VMEM_LIMIT),
        cost_estimate=cost(18),
    )(
        meta,
        yh,
        yl,
        own,
        rh,
        rl,
        head_u,
        tail_u,
        parent.reshape(9216, LANES),
        *(x.reshape(6, 512, LANES) for x in (above, middle, below)),
    )
    return out.reshape(6, 1, NB, 3, 1, NB)


def solution(mesh):
    in_specs = (
        P(None, "prow", None, None, "pcol", None),
        P(None, "prow", None, None, "pcol", None),
        P(),
    )
    out_specs = P(None, "prow", None, None, "pcol", None)
    return jax.shard_map(
        per_device, mesh=mesh, in_specs=in_specs, out_specs=out_specs, check_vma=False
    )
```

```python
import jax
import jax.numpy as jnp
from jax import lax
from jax.experimental import pallas as pl
from jax.experimental.pallas import tpu as pltpu
from jax.sharding import PartitionSpec as P

KB = 5
NB = 256
HB = 128
LANES = 128
F32 = jnp.float32
BF16 = jnp.bfloat16
VMEM_LIMIT = 60 * 1024 * 1024
VM = pl.BlockSpec(memory_space=pltpu.VMEM)
SM = pl.BlockSpec(memory_space=pltpu.SMEM)


def route_of(meta, child, residue):
    there, slot = False, 0
    for turn in range(4):
        target = meta[child * 16 + 4 * turn + residue]
        here = target % 8 == meta[32]
        there = jnp.logical_or(there, here)
        slot = jnp.where(here, target // 8, slot)
    return there, slot


def turn_for(meta, target_row):
    child, residue = meta[32] // 4, meta[32] % 4
    chosen = 0
    for turn in range(1, 4):
        chosen = jnp.where(meta[child * 16 + 4 * turn + residue] % 8 == target_row, turn, chosen)
    return chosen


def residue_of(row, e):
    return (3 * row + 4 + e) % 4


def pick_kernel(meta, parts_ref, out_ref):
    for target_row in range(8):
        turn = turn_for(meta, target_row)
        for v in range(2):
            out_ref[target_row, v] = parts_ref[v, turn]


def copy_kernel(meta, block_ref, out_ref):
    out_ref[...] = block_ref[...]


def assemble_kernel(meta, first_ref, rest_ref, got_ref, out_ref):
    for j in range(KB):
        out_ref[j, 0] = first_ref[j]
        out_ref[j, 1:6] = rest_ref[j]
    for child in range(2):
        for residue in range(4):
            there, slot = route_of(meta, child, residue)
            for v in range(2):
                column = meta[child * 16 + v]

                @pl.when(jnp.logical_and(there, column < KB))
                def _():
                    out_ref[column, slot] = out_ref[column, slot] + got_ref[4 * child + residue, v]


UPPER = [(k, i) for k in range(KB) for i in range(k, KB)]
CHILD_SOURCES = [(c, u, v) for c in range(2) for (u, v) in ((0, 0), (0, 1), (1, 1))]
TRI = len(UPPER)


def packed(k, i):
    return k * (2 * KB + 1 - k) // 2 + i - k


def exact(a, b, dims):
    return lax.dot_general(a, b, (dims, ((), ())), precision=lax.Precision.HIGHEST, preferred_element_type=F32)


def dot3(ah, al, bh, bl, dims):
    def dot(a, b):
        return lax.dot_general(a, b, (dims, ((), ())), preferred_element_type=F32)

    return dot(ah, bh) + (dot(ah, bl) + dot(al, bh))


NN = ((1,), (0,))
NT = ((1,), (1,))
TN = ((0,), (0,))


def factor_128(a_ref, x_ref, u_ref):
    shape = (8, LANES)
    lane = lax.broadcasted_iota(jnp.int32, (HB, LANES), 1)
    sub = lax.broadcasted_iota(jnp.int32, (HB, LANES), 0)
    x_ref[...] = jnp.where(lane == sub, 1.0, 0.0).astype(F32)
    for g in range(HB // 8):
        rows = slice(8 * g, 8 * g + 8)
        a_g = a_ref[rows, :]
        x_g = x_ref[rows, :]
        cols = [jnp.broadcast_to(a_g[:, 8 * g + s : 8 * g + s + 1], shape) for s in range(8)]
        d = [[jnp.broadcast_to(cols[s][t : t + 1, :], shape) for s in range(t + 1)] for t in range(8)]
        low = [[None] * 8 for _ in range(8)]
        rinv = []
        for s in range(8):
            r = lax.rsqrt(d[s][s])
            rinv.append(r)
            for t in range(s + 1, 8):
                low[t][s] = d[t][s] * r
            for t in range(s + 1, 8):
                for t2 in range(s + 1, t + 1):
                    d[t][t2] = d[t][t2] - low[t][s] * low[t2][s]
        ub, xb = [], []
        for t in range(8):
            ua = jnp.broadcast_to(a_g[t : t + 1, :], shape)
            xa = jnp.broadcast_to(x_g[t : t + 1, :], shape)
            for s in range(t):
                ua = ua - low[t][s] * ub[s]
                xa = xa - low[t][s] * xb[s]
            ub.append(ua * rinv[t])
            xb.append(xa * rinv[t])
            u_ref[8 * g + t : 8 * g + t + 1, :] = ub[t][0:1, :]
            x_ref[8 * g + t : 8 * g + t + 1, :] = xb[t][0:1, :]
        for i in range(g + 1, HB // 8):
            rows_i = slice(8 * i, 8 * i + 8)
            a_i = a_ref[rows_i, :]
            x_i = x_ref[rows_i, :]
            w = []
            for t in range(8):
                wt = jnp.broadcast_to(a_i[:, 8 * g + t : 8 * g + t + 1], shape)
                for s in range(t):
                    wt = wt - low[t][s] * w[s]
                w.append(wt * rinv[t])
            for t in range(8):
                a_i = a_i - w[t] * ub[t]
                x_i = x_i - w[t] * xb[t]
            a_ref[rows_i, :] = a_i
            x_ref[rows_i, :] = x_i
    u_ref[...] = jnp.where(lane >= sub, u_ref[...], 0.0)


def split(a):
    high = a.astype(BF16)
    return high, (a - high.astype(F32)).astype(BF16)


def chain_kernel(meta, parts_ref, u_ref, th_ref, tl_ref, f_ref, v_ref, a_s, x_s, u_s, stage, sems):
    sources = UPPER + [(4 * c + u, KB + v) for c, u, v in CHILD_SOURCES]
    copies = [
        pltpu.make_async_copy(parts_ref.at[p, :, j], stage.at[at], sems.at[at]) for at, (p, j) in enumerate(sources)
    ]
    for copy in copies:
        copy.start()

    def take(at, s, h):
        return stage[at, s, pl.ds(h, 16, stride=2), :]

    for at, (k, i) in enumerate(UPPER):
        copies[at].wait()
        for s in range(16):
            for h in range(2):
                f_ref[k * KB + i, 16 * s : 16 * s + 16, HB * h : HB * h + HB] = take(at, s, h)
    for at, (c, u, v) in enumerate(CHILD_SOURCES):
        copies[TRI + at].wait()
        k = meta[c * 16 + u]
        i = meta[c * 16 + v]

        @pl.when(jnp.logical_and(k < KB, i < KB))
        def _():
            for s in range(16):
                for h in range(2):
                    place = (k * KB + i, slice(16 * s, 16 * s + 16), slice(HB * h, HB * h + HB))
                    f_ref[place] = f_ref[place] + take(TRI + at, s, h)

    @pl.loop(0, 2 * KB)
    def _(step):
        k = step // 2
        half = step % 2
        kk = k * KB + k
        pk = packed(k, k)

        @pl.when(half == 0)
        def _():
            a_s[...] = f_ref[kk, 0:HB, 0:HB]

        @pl.when(half == 1)
        def _():
            u12 = exact(v_ref[0:HB, 0:HB], f_ref[kk, 0:HB, HB:NB], NN)
            u_ref[pk, 0:HB, HB:NB] = u12
            a_s[...] = f_ref[kk, HB:NB, HB:NB] - exact(u12, u12, TN)

        factor_128(a_s, x_s, u_s)

        @pl.when(half == 0)
        def _():
            u_ref[pk, 0:HB, 0:HB] = u_s[...]
            v_ref[0:HB, 0:HB] = x_s[...]

        @pl.when(half == 1)
        def _():
            u_ref[pk, HB:NB, HB:NB] = u_s[...]
            u_ref[pk, HB:NB, 0:HB] = jnp.zeros((HB, HB), F32)
            v_ref[HB:NB, HB:NB] = x_s[...]
            v_ref[0:HB, HB:NB] = jnp.zeros((HB, HB), F32)
            lx = exact(u_ref[pk, 0:HB, HB:NB], v_ref[0:HB, 0:HB], TN)
            v_ref[HB:NB, 0:HB] = -exact(x_s[...], lx, NN)
            high, low = split(v_ref[...].T)
            th_ref[pk] = high
            tl_ref[pk] = low
            vh, vl = split(v_ref[...])

            @pl.loop(k + 1, KB)
            def _(i):
                u = dot3(vh, vl, *split(f_ref[k * KB + i]), NN)
                at = packed(k, i)
                u_ref[at] = u
                high, low = split(u)
                th_ref[at] = high
                tl_ref[at] = low

            @pl.loop(k + 1, KB)
            def _(i):
                at_i = packed(k, i)

                @pl.loop(i, KB)
                def _(j):
                    at_j = packed(k, j)
                    f_ref[i * KB + j] = f_ref[i * KB + j] - dot3(
                        th_ref[at_i], tl_ref[at_i], th_ref[at_j], tl_ref[at_j], TN
                    )


def solve_rows(raw_ref, yh_ref, yl_ref, th_ref, tl_ref):
    def factor(m, k):
        return th_ref[packed(m, k)], tl_ref[packed(m, k)]

    for k in range(KB):
        at = slice(NB * k, NB * k + NB)
        t = raw_ref[:, at]
        for m in range(k):
            am = slice(NB * m, NB * m + NB)
            t = t - dot3(yh_ref[:, am], yl_ref[:, am], *factor(m, k), NN)
        high, low = split(t)
        y = dot3(high, low, *factor(k, k), NN)
        raw_ref[:, at] = y
        high, low = split(y)
        yh_ref[:, at] = high
        yl_ref[:, at] = low


def right_kernel(parts_ref, th_ref, tl_ref, yh_ref, yl_ref, raw):
    @pl.loop(0, 16)
    def _(s):
        for c in range(3):
            for j in range(KB):
                for h in range(2):
                    raw[pl.ds(pl.multiple_of(NB * c + 16 * s, 16), 16), NB * j + HB * h : NB * j + HB * h + HB] = parts_ref[
                        s, j, c, pl.ds(h, 16, stride=2), :
                    ]
    solve_rows(raw, yh_ref, yl_ref, th_ref, tl_ref)


ROWS_STEP = 2


def left_kernel(meta, parts_ref, th_ref, tl_ref, yh_ref, yl_ref, own_ref, raw):
    @pl.loop(0, 16)
    def _(s):
        for a in range(ROWS_STEP):
            for j in range(KB):
                for h in range(2):
                    raw[pl.ds(pl.multiple_of(NB * a + 16 * s, 16), 16), NB * j + HB * h : NB * j + HB * h + HB] = parts_ref[
                        s, j, a, pl.ds(h, 16, stride=2), :
                    ]
    solve_rows(raw, yh_ref, yl_ref, th_ref, tl_ref)
    for j in range(KB):

        @pl.when(meta[33] == j)
        def _():
            own_ref[...] = raw[:, NB * j : NB * j + NB]


def schur_kernel(meta, yh, yl, own_ref, rh_ref, rl_ref, u_ref, parent_ref, child_0, child_1, child_2, out_ref):
    step = pl.program_id(0)
    row, col = meta[32], meta[33]
    routes = []
    for child in range(2):
        for e in range(3):
            routes.append((child, *route_of(meta, child, residue_of(row, e))))

    for a in range(ROWS_STEP):
        slot = step * ROWS_STEP + a
        block_row = row + 8 * slot
        rows = slice(NB * a, NB * a + NB)
        for c in range(3):
            block_col = col + 16 * c

            def put(h, value):
                out_ref[pl.ds(1536 * a + 2 * c + h, NB, stride=6), :] = value

            @pl.when(jnp.logical_and(block_row >= KB, block_col >= KB))
            def _():
                cols = slice(NB * c, NB * c + NB)
                product = dot3(yh[rows, :], yl[rows, :], rh_ref[cols, :], rl_ref[cols, :], NT)
                for h in range(2):
                    put(h, parent_ref[pl.ds(1536 * a + 2 * c + h, NB, stride=6), :] - product[:, HB * h : HB * h + HB])
                turn = block_col % 3
                source = block_col // 3
                for n, (child, there, to) in enumerate(routes):
                    here = jnp.logical_and(there, to == slot)
                    here = jnp.logical_and(here, meta[child * 16 + source] == block_col)
                    for d, child_ref in enumerate((child_0, child_1, child_2)):

                        @pl.when(jnp.logical_and(here, turn == d))
                        def _():
                            for h in range(2):
                                at = pl.ds(1536 * a + 2 * c + h, NB, stride=6)
                                out_ref[at, :] = out_ref[at, :] + child_ref[n, pl.ds(h, NB, stride=2), :]

            @pl.when(jnp.logical_and(block_row < KB, block_col >= KB))
            def _():
                for h in range(2):
                    put(h, jnp.zeros((NB, HB), F32))

            if c == 0:

                @pl.when(jnp.logical_and(block_row >= KB, block_col < KB))
                def _():
                    for h in range(2):
                        put(h, own_ref[rows, HB * h : HB * h + HB])

                in_lead = jnp.logical_and(block_row < KB, block_col < KB)
                upper = block_row < block_col

                @pl.when(jnp.logical_and(in_lead, upper))
                def _():
                    for h in range(2):
                        put(h, jnp.zeros((NB, HB), F32))

                @pl.when(jnp.logical_and(in_lead, jnp.logical_not(upper)))
                def _():
                    block = u_ref[jnp.clip(packed(block_col, block_row), 0, TRI - 1)].T
                    for h in range(2):
                        put(h, block[:, HB * h : HB * h + HB])


def cost(microseconds):
    return pl.CostEstimate(flops=int(microseconds * 1.1e9), bytes_accessed=1 << 20, transcendentals=0)


def call(kernel, out_shape, in_specs, scratch, microseconds=2):
    return pl.pallas_call(
        kernel,
        out_shape=out_shape,
        in_specs=in_specs,
        out_specs=jax.tree.map(lambda _: VM, out_shape),
        scratch_shapes=scratch,
        compiler_params=pltpu.CompilerParams(vmem_limit_bytes=VMEM_LIMIT),
        cost_estimate=cost(microseconds),
    )


def shaped(shape, dtype=F32):
    return jax.ShapeDtypeStruct(shape, dtype)


def per_device(parent, children, index_maps):
    row = lax.axis_index("prow")
    col = lax.axis_index("pcol")
    meta = jnp.concatenate([index_maps.reshape(-1), jnp.stack([row, col]).astype(jnp.int32)])
    front = parent.reshape(6, NB, 3, 2, LANES)
    lead = front[:, :, 0].reshape(6, 16, 32, LANES)
    child = children.reshape(4, 16, 32, LANES)

    picked = pl.pallas_call(
        copy_kernel,
        grid_spec=pltpu.PrefetchScalarGridSpec(
            num_scalar_prefetch=1,
            grid=(8,),
            in_specs=[pl.BlockSpec((1, 512, LANES), lambda t, meta: (turn_for(meta, t), 0, 0))],
            out_specs=pl.BlockSpec((1, 512, LANES), lambda t, meta: (t, 0, 0)),
        ),
        out_shape=shaped((8, 512, LANES)),
        cost_estimate=cost(3),
    )(meta, child.reshape(4, 512, LANES))

    first = jnp.stack([lead[0], child[0]], axis=1)
    first = lax.all_to_all(first, "pcol", 0, 0, tiled=True)
    mine = jnp.concatenate([first[0:KB, 0], first[0:2, 1]], axis=0)
    mine, picked = lax.optimization_barrier((mine, picked))
    lead_parts = lax.all_gather(mine, ("prow", "pcol")).reshape(8, 16, KB + 2, 32, LANES)

    rest = jnp.concatenate([lead[1:], child], axis=0).transpose(1, 0, 2, 3)
    rest, mine = lax.optimization_barrier((rest, mine))
    rest = lax.all_to_all(rest, "pcol", 0, 0, tiled=True)
    pieces = call(pick_kernel, shaped((8, 2, 32, LANES)), [SM, VM], [])(meta, rest[0:2, 5:9])
    pieces = lax.all_to_all(pieces, "prow", 0, 0, tiled=True)
    slices = call(assemble_kernel, shaped((KB, 6, 32, LANES)), [SM, VM, VM, VM], [])(
        meta, mine[0:KB], rest[0:KB, 0:5], pieces
    )

    left_parts = lax.all_gather(slices, "pcol")

    slices, picked = lax.optimization_barrier((slices, picked))
    got = lax.all_to_all(picked, "prow", 0, 0, tiled=True)
    routed = jnp.stack(
        [
            lax.dynamic_index_in_dim(got, 4 * c + residue_of(row, e), 0, keepdims=False)
            for c in range(2)
            for e in range(3)
        ]
    )
    even, odd = slices[:, 0::2], slices[:, 1::2]
    is_even = col % 2 == 0
    perm_a, perm_b = [], []
    for p in range(8):
        for s in range(16):
            perm_a.append((p * 16 + s, (s // 2) * 16 + p + 8 * (s % 2)))
            perm_b.append((p * 16 + s, (s // 2) * 16 + p + 8 * (1 - s % 2)))
    pair_a = lax.ppermute(jnp.where(is_even, even, odd), ("prow", "pcol"), perm_a)
    pair_b = lax.ppermute(jnp.where(is_even, odd, even), ("prow", "pcol"), perm_b)
    low_side = col < 8
    pair = jnp.stack([jnp.where(low_side, pair_a, pair_b), jnp.where(low_side, pair_b, pair_a)])
    pairs = jnp.broadcast_to(pair[None], (8,) + pair.shape)

    right_parts = lax.all_to_all(pairs, "prow", 0, 0, tiled=True).reshape(16, KB, 3, 32, LANES)
    middle = lax.ppermute(routed, "pcol", [(q, (3 * q + 1) % 16) for q in range(1, 16)])

    lead_parts, _, _ = lax.optimization_barrier((lead_parts, pairs, routed))
    upper, th, tl = pl.pallas_call(
        chain_kernel,
        out_shape=(shaped((TRI, NB, NB)), shaped((TRI, NB, NB), BF16), shaped((TRI, NB, NB), BF16)),
        in_specs=[SM, pl.BlockSpec(memory_space=pl.ANY)],
        out_specs=(VM, VM, VM),
        scratch_shapes=[
            pltpu.VMEM((KB * KB, NB, NB), F32),
            pltpu.VMEM((NB, NB), F32),
            pltpu.VMEM((HB, HB), F32),
            pltpu.VMEM((HB, HB), F32),
            pltpu.VMEM((HB, HB), F32),
            pltpu.VMEM((TRI + 6, 16, 32, LANES), F32),
            pltpu.SemaphoreType.DMA((TRI + 6,)),
        ],
        compiler_params=pltpu.CompilerParams(vmem_limit_bytes=VMEM_LIMIT),
        cost_estimate=cost(66),
    )(meta, lead_parts)

    middle, th = lax.optimization_barrier((middle, th))
    below = lax.ppermute(middle, "pcol", [(q, (q + 1) % 16) for q in range(16)])
    above = lax.ppermute(middle, "pcol", [(q, (q + 15) % 16) for q in range(16)])

    rh, rl = call(
        right_kernel,
        (shaped((768, 1280), BF16), shaped((768, 1280), BF16)),
        [VM] * 3,
        [pltpu.VMEM((768, 1280), F32)],
        12,
    )(right_parts, th, tl)

    rows = NB * ROWS_STEP
    steps = 6 // ROWS_STEP
    whole_tri = pl.BlockSpec((TRI, NB, NB), lambda g: (0, 0, 0))
    by_rows = pl.BlockSpec((rows, 1280), lambda g: (g, 0))
    own_rows = pl.BlockSpec((rows, NB), lambda g: (g, 0))
    yh, yl, own = pl.pallas_call(
        left_kernel,
        grid=(steps,),
        out_shape=(shaped((1536, 1280), BF16), shaped((1536, 1280), BF16), shaped((1536, NB))),
        in_specs=[
            SM,
            pl.BlockSpec((16, KB, ROWS_STEP, 32, LANES), lambda g: (0, 0, g, 0, 0)),
            whole_tri,
            whole_tri,
        ],
        out_specs=(by_rows, by_rows, own_rows),
        scratch_shapes=[pltpu.VMEM((rows, 1280), F32)],
        compiler_params=pltpu.CompilerParams(vmem_limit_bytes=VMEM_LIMIT),
        cost_estimate=cost(20),
    )(meta, left_parts, th, tl)

    whole_right = pl.BlockSpec((768, 1280), lambda g: (0, 0))
    whole_child = pl.BlockSpec((6, 512, LANES), lambda g: (0, 0, 0))
    front_rows = pl.BlockSpec((1536 * ROWS_STEP, LANES), lambda g: (g, 0))
    out = pl.pallas_call(
        schur_kernel,
        grid=(steps,),
        out_shape=shaped((9216, LANES)),
        in_specs=[SM, by_rows, by_rows, own_rows, whole_right, whole_right, whole_tri, front_rows]
        + [whole_child] * 3,
        out_specs=front_rows,
        compiler_params=pltpu.CompilerParams(vmem_limit_bytes=VMEM_LIMIT),
        cost_estimate=cost(18),
    )(
        meta,
        yh,
        yl,
        own,
        rh,
        rl,
        upper,
        parent.reshape(9216, LANES),
        *(x.reshape(6, 512, LANES) for x in (above, middle, below)),
    )
    return out.reshape(6, 1, NB, 3, 1, NB)


def solution(mesh):
    in_specs = (
        P(None, "prow", None, None, "pcol", None),
        P(None, "prow", None, None, "pcol", None),
        P(),
    )
    out_specs = P(None, "prow", None, None, "pcol", None)
    return jax.shard_map(
        per_device, mesh=mesh, in_specs=in_specs, out_specs=out_specs, check_vma=False
    )
```

```python
import jax
import jax.numpy as jnp
from jax import lax
from jax.experimental import pallas as pl
from jax.experimental.pallas import tpu as pltpu
from jax.sharding import PartitionSpec as P

KB = 5
NB = 256
HB = 128
LANES = 128
F32 = jnp.float32
BF16 = jnp.bfloat16
VMEM_LIMIT = 60 * 1024 * 1024
VM = pl.BlockSpec(memory_space=pltpu.VMEM)
SM = pl.BlockSpec(memory_space=pltpu.SMEM)


def route_of(meta, child, residue):
    there, slot = False, 0
    for turn in range(4):
        target = meta[child * 16 + 4 * turn + residue]
        here = target % 8 == meta[32]
        there = jnp.logical_or(there, here)
        slot = jnp.where(here, target // 8, slot)
    return there, slot


def turn_for(meta, target_row):
    child, residue = meta[32] // 4, meta[32] % 4
    chosen = 0
    for turn in range(1, 4):
        chosen = jnp.where(meta[child * 16 + 4 * turn + residue] % 8 == target_row, turn, chosen)
    return chosen


def residue_of(row, e):
    return (3 * row + 4 + e) % 4


def pick_kernel(meta, parts_ref, out_ref):
    for target_row in range(8):
        turn = turn_for(meta, target_row)
        for v in range(2):
            out_ref[target_row, v] = parts_ref[v, turn]


def copy_kernel(meta, block_ref, out_ref):
    out_ref[...] = block_ref[...]


def assemble_kernel(meta, first_ref, rest_ref, got_ref, out_ref):
    for j in range(KB):
        out_ref[j, 0] = first_ref[j]
        out_ref[j, 1:6] = rest_ref[j]
    for child in range(2):
        for residue in range(4):
            there, slot = route_of(meta, child, residue)
            for v in range(2):
                column = meta[child * 16 + v]

                @pl.when(jnp.logical_and(there, column < KB))
                def _():
                    out_ref[column, slot] = out_ref[column, slot] + got_ref[4 * child + residue, v]


def chunk_kernel(meta, mine_ref, got_a_ref, got_b_ref, out_ref):
    for row, picks in enumerate(CHUNKS):

        @pl.when(meta[32] == row)
        def _():
            for at in range(3):
                kind, index = picks[at] if at < len(picks) else (0, 0)
                source = (mine_ref, got_a_ref, got_b_ref)[kind]
                out_ref[at] = source[index]


CHUNKS = [
    [(0, 0), (0, 5), (0, 6)],
    [(0, 1), (0, 2), (0, 6)],
    [(0, 2), (0, 3), (0, 4)],
    [(0, 3), (0, 4)],
    [(0, 4), (0, 5), (0, 6)],
    [(1, 0), (1, 1), (0, 6)],
    [(1, 0), (1, 1), (1, 2)],
    [(2, 0)],
]
UPPER_AT = {
    (0, 0): (0, 0),
    (0, 1): (7, 0),
    (0, 2): (6, 0),
    (0, 3): (6, 1),
    (0, 4): (6, 2),
    (1, 1): (1, 0),
    (1, 2): (1, 1),
    (1, 3): (5, 0),
    (1, 4): (5, 1),
    (2, 2): (2, 0),
    (2, 3): (2, 1),
    (2, 4): (2, 2),
    (3, 3): (3, 0),
    (3, 4): (3, 1),
    (4, 4): (4, 0),
}
CHILD_AT = {
    (0, 0, 0): (0, 1),
    (0, 0, 1): (0, 2),
    (0, 1, 1): (1, 2),
    (1, 0, 0): (4, 1),
    (1, 0, 1): (4, 2),
    (1, 1, 1): (5, 2),
}


def exact(a, b, dims):
    return lax.dot_general(a, b, (dims, ((), ())), precision=lax.Precision.HIGHEST, preferred_element_type=F32)


def dot3(ah, al, bh, bl, dims):
    def dot(a, b):
        return lax.dot_general(a, b, (dims, ((), ())), preferred_element_type=F32)

    return dot(ah, bh) + (dot(ah, bl) + dot(al, bh))


NN = ((1,), (0,))
NT = ((1,), (1,))
TN = ((0,), (0,))


def factor_128(a_ref, x_ref, u_ref):
    shape = (8, LANES)
    lane = lax.broadcasted_iota(jnp.int32, (HB, LANES), 1)
    sub = lax.broadcasted_iota(jnp.int32, (HB, LANES), 0)
    x_ref[...] = jnp.where(lane == sub, 1.0, 0.0).astype(F32)
    for g in range(HB // 8):
        rows = slice(8 * g, 8 * g + 8)
        a_g = a_ref[rows, :]
        x_g = x_ref[rows, :]
        cols = [jnp.broadcast_to(a_g[:, 8 * g + s : 8 * g + s + 1], shape) for s in range(8)]
        d = [[jnp.broadcast_to(cols[s][t : t + 1, :], shape) for s in range(t + 1)] for t in range(8)]
        low = [[None] * 8 for _ in range(8)]
        rinv = []
        for s in range(8):
            r = lax.rsqrt(d[s][s])
            rinv.append(r)
            for t in range(s + 1, 8):
                low[t][s] = d[t][s] * r
            for t in range(s + 1, 8):
                for t2 in range(s + 1, t + 1):
                    d[t][t2] = d[t][t2] - low[t][s] * low[t2][s]
        ub, xb = [], []
        for t in range(8):
            ua = jnp.broadcast_to(a_g[t : t + 1, :], shape)
            xa = jnp.broadcast_to(x_g[t : t + 1, :], shape)
            for s in range(t):
                ua = ua - low[t][s] * ub[s]
                xa = xa - low[t][s] * xb[s]
            ub.append(ua * rinv[t])
            xb.append(xa * rinv[t])
            u_ref[8 * g + t : 8 * g + t + 1, :] = ub[t][0:1, :]
            x_ref[8 * g + t : 8 * g + t + 1, :] = xb[t][0:1, :]
        for i in range(g + 1, HB // 8):
            rows_i = slice(8 * i, 8 * i + 8)
            a_i = a_ref[rows_i, :]
            x_i = x_ref[rows_i, :]
            w = []
            for t in range(8):
                wt = jnp.broadcast_to(a_i[:, 8 * g + t : 8 * g + t + 1], shape)
                for s in range(t):
                    wt = wt - low[t][s] * w[s]
                w.append(wt * rinv[t])
            for t in range(8):
                a_i = a_i - w[t] * ub[t]
                x_i = x_i - w[t] * xb[t]
            a_ref[rows_i, :] = a_i
            x_ref[rows_i, :] = x_i
    u_ref[...] = jnp.where(lane >= sub, u_ref[...], 0.0)


def split(a):
    high = a.astype(BF16)
    return high, (a - high.astype(F32)).astype(BF16)


CUT = 2
REST = KB - CUT


def packed(n, k, i):
    return k * (2 * n + 1 - k) // 2 + i - k


HEADS = packed(KB, CUT, CUT)
TAILS = packed(REST, REST, REST)


def eliminate(n, steps, f_ref, u_ref, th_ref, tl_ref, v_ref, a_s, x_s, u_s):
    @pl.loop(0, 2 * steps)
    def _(step):
        k = step // 2
        half = step % 2
        kk = k * n + k
        pk = packed(n, k, k)

        @pl.when(half == 0)
        def _():
            a_s[...] = f_ref[kk, 0:HB, 0:HB]

        @pl.when(half == 1)
        def _():
            u12 = exact(v_ref[0:HB, 0:HB], f_ref[kk, 0:HB, HB:NB], NN)
            u_ref[pk, 0:HB, HB:NB] = u12
            a_s[...] = f_ref[kk, HB:NB, HB:NB] - exact(u12, u12, TN)

        factor_128(a_s, x_s, u_s)

        @pl.when(half == 0)
        def _():
            u_ref[pk, 0:HB, 0:HB] = u_s[...]
            v_ref[0:HB, 0:HB] = x_s[...]

        @pl.when(half == 1)
        def _():
            u_ref[pk, HB:NB, HB:NB] = u_s[...]
            u_ref[pk, HB:NB, 0:HB] = jnp.zeros((HB, HB), F32)
            v_ref[HB:NB, HB:NB] = x_s[...]
            v_ref[0:HB, HB:NB] = jnp.zeros((HB, HB), F32)
            lx = exact(u_ref[pk, 0:HB, HB:NB], v_ref[0:HB, 0:HB], TN)
            v_ref[HB:NB, 0:HB] = -exact(x_s[...], lx, NN)
            high, low = split(v_ref[...].T)
            th_ref[pk] = high
            tl_ref[pk] = low
            vh, vl = split(v_ref[...])

            @pl.loop(k + 1, n)
            def _(i):
                u = dot3(vh, vl, *split(f_ref[k * n + i]), NN)
                at = packed(n, k, i)
                u_ref[at] = u
                high, low = split(u)
                th_ref[at] = high
                tl_ref[at] = low

            @pl.loop(k + 1, n)
            def _(i):
                at_i = packed(n, k, i)

                @pl.loop(i, n)
                def _(j):
                    at_j = packed(n, k, j)
                    f_ref[i * n + j] = f_ref[i * n + j] - dot3(
                        th_ref[at_i], tl_ref[at_i], th_ref[at_j], tl_ref[at_j], TN
                    )


def chain_head_kernel(meta, parts_ref, u_ref, th_ref, tl_ref, rest_ref, f_ref, *scratch):
    def take(at, s, h):
        return parts_ref[at[0], s, at[1], pl.ds(h, 16, stride=2), :]

    for (k, i), at in UPPER_AT.items():
        for s in range(16):
            for h in range(2):
                f_ref[k * KB + i, 16 * s : 16 * s + 16, HB * h : HB * h + HB] = take(at, s, h)
    for (c, u, v), at in CHILD_AT.items():
        k = meta[c * 16 + u]
        i = meta[c * 16 + v]

        @pl.when(jnp.logical_and(k < KB, i < KB))
        def _():
            for s in range(16):
                for h in range(2):
                    place = (k * KB + i, slice(16 * s, 16 * s + 16), slice(HB * h, HB * h + HB))
                    f_ref[place] = f_ref[place] + take(at, s, h)

    eliminate(KB, CUT, f_ref, u_ref, th_ref, tl_ref, *scratch)
    for i in range(REST):
        for j in range(i, REST):
            rest_ref[packed(REST, i, j)] = f_ref[(CUT + i) * KB + CUT + j]


def chain_tail_kernel(rest_ref, u_ref, th_ref, tl_ref, f_ref, *scratch):
    for i in range(REST):
        for j in range(i, REST):
            f_ref[i * REST + j] = rest_ref[packed(REST, i, j)]
    eliminate(REST, REST, f_ref, u_ref, th_ref, tl_ref, *scratch)


def solve_rows(raw_ref, yh_ref, yl_ref, factors):
    head_h, head_l, tail_h, tail_l = factors

    def factor(m, k):
        if m < CUT:
            return head_h[packed(KB, m, k)], head_l[packed(KB, m, k)]
        at = packed(REST, m - CUT, k - CUT)
        return tail_h[at], tail_l[at]

    for k in range(KB):
        at = slice(NB * k, NB * k + NB)
        t = raw_ref[:, at]
        for m in range(k):
            am = slice(NB * m, NB * m + NB)
            t = t - dot3(yh_ref[:, am], yl_ref[:, am], *factor(m, k), NN)
        high, low = split(t)
        y = dot3(high, low, *factor(k, k), NN)
        raw_ref[:, at] = y
        high, low = split(y)
        yh_ref[:, at] = high
        yl_ref[:, at] = low


def right_kernel(parts_ref, hh_ref, hl_ref, th_ref, tl_ref, yh_ref, yl_ref, raw):
    @pl.loop(0, 16)
    def _(s):
        for c in range(3):
            for j in range(KB):
                for h in range(2):
                    raw[pl.ds(pl.multiple_of(NB * c + 16 * s, 16), 16), NB * j + HB * h : NB * j + HB * h + HB] = parts_ref[
                        s, j, c, pl.ds(h, 16, stride=2), :
                    ]
    solve_rows(raw, yh_ref, yl_ref, (hh_ref, hl_ref, th_ref, tl_ref))


ROWS_STEP = 2


def left_kernel(meta, parts_ref, hh_ref, hl_ref, th_ref, tl_ref, yh_ref, yl_ref, own_ref, raw):
    @pl.loop(0, 16)
    def _(s):
        for a in range(ROWS_STEP):
            for j in range(KB):
                for h in range(2):
                    raw[pl.ds(pl.multiple_of(NB * a + 16 * s, 16), 16), NB * j + HB * h : NB * j + HB * h + HB] = parts_ref[
                        s, j, a, pl.ds(h, 16, stride=2), :
                    ]
    solve_rows(raw, yh_ref, yl_ref, (hh_ref, hl_ref, th_ref, tl_ref))
    for j in range(KB):

        @pl.when(meta[33] == j)
        def _():
            own_ref[...] = raw[:, NB * j : NB * j + NB]


def schur_kernel(meta, yh, yl, own_ref, rh_ref, rl_ref, head_ref, tail_ref, parent_ref, child_0, child_1, child_2, out_ref):
    step = pl.program_id(0)
    row, col = meta[32], meta[33]
    routes = []
    for child in range(2):
        for e in range(3):
            routes.append((child, *route_of(meta, child, residue_of(row, e))))

    for a in range(ROWS_STEP):
        slot = step * ROWS_STEP + a
        block_row = row + 8 * slot
        rows = slice(NB * a, NB * a + NB)
        for c in range(3):
            block_col = col + 16 * c

            def put(h, value):
                out_ref[pl.ds(1536 * a + 2 * c + h, NB, stride=6), :] = value

            @pl.when(jnp.logical_and(block_row >= KB, block_col >= KB))
            def _():
                cols = slice(NB * c, NB * c + NB)
                product = dot3(yh[rows, :], yl[rows, :], rh_ref[cols, :], rl_ref[cols, :], NT)
                for h in range(2):
                    put(h, parent_ref[pl.ds(1536 * a + 2 * c + h, NB, stride=6), :] - product[:, HB * h : HB * h + HB])
                turn = block_col % 3
                source = block_col // 3
                for n, (child, there, to) in enumerate(routes):
                    here = jnp.logical_and(there, to == slot)
                    here = jnp.logical_and(here, meta[child * 16 + source] == block_col)
                    for d, child_ref in enumerate((child_0, child_1, child_2)):

                        @pl.when(jnp.logical_and(here, turn == d))
                        def _():
                            for h in range(2):
                                at = pl.ds(1536 * a + 2 * c + h, NB, stride=6)
                                out_ref[at, :] = out_ref[at, :] + child_ref[n, pl.ds(h, NB, stride=2), :]

            @pl.when(jnp.logical_and(block_row < KB, block_col >= KB))
            def _():
                for h in range(2):
                    put(h, jnp.zeros((NB, HB), F32))

            if c == 0:

                @pl.when(jnp.logical_and(block_row >= KB, block_col < KB))
                def _():
                    for h in range(2):
                        put(h, own_ref[rows, HB * h : HB * h + HB])

                in_lead = jnp.logical_and(block_row < KB, block_col < KB)
                upper = block_row < block_col

                @pl.when(jnp.logical_and(in_lead, upper))
                def _():
                    for h in range(2):
                        put(h, jnp.zeros((NB, HB), F32))

                lower = jnp.logical_and(in_lead, jnp.logical_not(upper))

                @pl.when(jnp.logical_and(lower, block_col < CUT))
                def _():
                    block = head_ref[jnp.clip(packed(KB, block_col, block_row), 0, HEADS - 1)].T
                    for h in range(2):
                        put(h, block[:, HB * h : HB * h + HB])

                @pl.when(jnp.logical_and(lower, block_col >= CUT))
                def _():
                    at = jnp.clip(packed(REST, block_col - CUT, block_row - CUT), 0, TAILS - 1)
                    block = tail_ref[at].T
                    for h in range(2):
                        put(h, block[:, HB * h : HB * h + HB])


def cost(microseconds):
    return pl.CostEstimate(flops=int(microseconds * 1.1e9), bytes_accessed=1 << 20, transcendentals=0)


def call(kernel, out_shape, in_specs, scratch, microseconds=2):
    return pl.pallas_call(
        kernel,
        out_shape=out_shape,
        in_specs=in_specs,
        out_specs=jax.tree.map(lambda _: VM, out_shape),
        scratch_shapes=scratch,
        compiler_params=pltpu.CompilerParams(vmem_limit_bytes=VMEM_LIMIT),
        cost_estimate=cost(microseconds),
    )


def shaped(shape, dtype=F32):
    return jax.ShapeDtypeStruct(shape, dtype)


def per_device(parent, children, index_maps):
    row = lax.axis_index("prow")
    col = lax.axis_index("pcol")
    meta = jnp.concatenate([index_maps.reshape(-1), jnp.stack([row, col]).astype(jnp.int32)])
    front = parent.reshape(6, NB, 3, 2, LANES)
    lead = front[:, :, 0].reshape(6, 16, 32, LANES)
    child = children.reshape(4, 16, 32, LANES)

    picked = pl.pallas_call(
        copy_kernel,
        grid_spec=pltpu.PrefetchScalarGridSpec(
            num_scalar_prefetch=1,
            grid=(8,),
            in_specs=[pl.BlockSpec((1, 512, LANES), lambda t, meta: (turn_for(meta, t), 0, 0))],
            out_specs=pl.BlockSpec((1, 512, LANES), lambda t, meta: (t, 0, 0)),
        ),
        out_shape=shaped((8, 512, LANES)),
        cost_estimate=cost(3),
    )(meta, child.reshape(4, 512, LANES))

    first = jnp.stack([lead[0], child[0]], axis=1)
    first = lax.all_to_all(first, "pcol", 0, 0, tiled=True)
    mine = jnp.concatenate([first[0:KB, 0], first[0:2, 1]], axis=0)
    mine, picked = lax.optimization_barrier((mine, picked))
    shed = jnp.where(row == 0, mine[2:5], mine[3:6])
    got_a = lax.ppermute(shed, "prow", [(0, 6), (1, 5)])
    got_b = lax.ppermute(mine[1:2], "prow", [(0, 7)])
    chunk = call(chunk_kernel, shaped((3, 32, LANES)), [SM, VM, VM, VM], [])(meta, mine, got_a, got_b)
    chunk = lax.all_gather(chunk, "pcol")
    lead_parts = lax.all_gather(chunk, "prow")

    rest = jnp.concatenate([lead[1:], child], axis=0).transpose(1, 0, 2, 3)
    rest, chunk = lax.optimization_barrier((rest, chunk))
    rest = lax.all_to_all(rest, "pcol", 0, 0, tiled=True)
    pieces = call(pick_kernel, shaped((8, 2, 32, LANES)), [SM, VM], [])(meta, rest[0:2, 5:9])
    pieces = lax.all_to_all(pieces, "prow", 0, 0, tiled=True)
    slices = call(assemble_kernel, shaped((KB, 6, 32, LANES)), [SM, VM, VM, VM], [])(
        meta, mine[0:KB], rest[0:KB, 0:5], pieces
    )

    left_parts = lax.all_gather(slices, "pcol")

    lead_parts, slices, picked = lax.optimization_barrier((lead_parts, slices, picked))
    got = lax.all_to_all(picked, "prow", 0, 0, tiled=True)
    routed = jnp.stack(
        [
            lax.dynamic_index_in_dim(got, 4 * c + residue_of(row, e), 0, keepdims=False)
            for c in range(2)
            for e in range(3)
        ]
    )
    even, odd = slices[:, 0::2], slices[:, 1::2]
    is_even = col % 2 == 0
    perm_a, perm_b = [], []
    for p in range(8):
        for s in range(16):
            perm_a.append((p * 16 + s, (s // 2) * 16 + p + 8 * (s % 2)))
            perm_b.append((p * 16 + s, (s // 2) * 16 + p + 8 * (1 - s % 2)))
    pair_a = lax.ppermute(jnp.where(is_even, even, odd), ("prow", "pcol"), perm_a)
    pair_b = lax.ppermute(jnp.where(is_even, odd, even), ("prow", "pcol"), perm_b)
    low_side = col < 8
    pair = jnp.stack([jnp.where(low_side, pair_a, pair_b), jnp.where(low_side, pair_b, pair_a)])
    pairs = jnp.broadcast_to(pair[None], (8,) + pair.shape)

    scratch = [
        pltpu.VMEM((NB, NB), F32),
        pltpu.VMEM((HB, HB), F32),
        pltpu.VMEM((HB, HB), F32),
        pltpu.VMEM((HB, HB), F32),
    ]
    head_u, head_h, head_l, left_over = call(
        chain_head_kernel,
        (
            shaped((HEADS, NB, NB)),
            shaped((HEADS, NB, NB), BF16),
            shaped((HEADS, NB, NB), BF16),
            shaped((TAILS, NB, NB)),
        ),
        [SM, VM],
        [pltpu.VMEM((KB * KB, NB, NB), F32)] + scratch,
        32,
    )(meta, lead_parts)

    left_over, pairs, routed = lax.optimization_barrier((left_over, pairs, routed))
    middle = lax.ppermute(routed, "pcol", [(q, (3 * q + 1) % 16) for q in range(1, 16)])
    right_parts = lax.all_to_all(pairs, "prow", 0, 0, tiled=True).reshape(16, KB, 3, 32, LANES)
    tail_u, tail_h, tail_l = call(
        chain_tail_kernel,
        (shaped((TAILS, NB, NB)), shaped((TAILS, NB, NB), BF16), shaped((TAILS, NB, NB), BF16)),
        [VM],
        [pltpu.VMEM((REST * REST, NB, NB), F32)] + scratch,
        40,
    )(left_over)

    middle, tail_h = lax.optimization_barrier((middle, tail_h))
    below = lax.ppermute(middle, "pcol", [(q, (q + 1) % 16) for q in range(16)])
    above = lax.ppermute(middle, "pcol", [(q, (q + 15) % 16) for q in range(16)])

    rh, rl = call(
        right_kernel,
        (shaped((768, 1280), BF16), shaped((768, 1280), BF16)),
        [VM] * 5,
        [pltpu.VMEM((768, 1280), F32)],
        12,
    )(right_parts, head_h, head_l, tail_h, tail_l)

    rows = NB * ROWS_STEP
    steps = 6 // ROWS_STEP
    whole_head = pl.BlockSpec((HEADS, NB, NB), lambda g: (0, 0, 0))
    whole_tail = pl.BlockSpec((TAILS, NB, NB), lambda g: (0, 0, 0))
    by_rows = pl.BlockSpec((rows, 1280), lambda g: (g, 0))
    own_rows = pl.BlockSpec((rows, NB), lambda g: (g, 0))
    yh, yl, own = pl.pallas_call(
        left_kernel,
        grid=(steps,),
        out_shape=(shaped((1536, 1280), BF16), shaped((1536, 1280), BF16), shaped((1536, NB))),
        in_specs=[
            SM,
            pl.BlockSpec((16, KB, ROWS_STEP, 32, LANES), lambda g: (0, 0, g, 0, 0)),
            whole_head,
            whole_head,
            whole_tail,
            whole_tail,
        ],
        out_specs=(by_rows, by_rows, own_rows),
        scratch_shapes=[pltpu.VMEM((rows, 1280), F32)],
        compiler_params=pltpu.CompilerParams(vmem_limit_bytes=VMEM_LIMIT),
        cost_estimate=cost(20),
    )(meta, left_parts, head_h, head_l, tail_h, tail_l)

    whole_right = pl.BlockSpec((768, 1280), lambda g: (0, 0))
    whole_child = pl.BlockSpec((6, 512, LANES), lambda g: (0, 0, 0))
    front_rows = pl.BlockSpec((1536 * ROWS_STEP, LANES), lambda g: (g, 0))
    out = pl.pallas_call(
        schur_kernel,
        grid=(steps,),
        out_shape=shaped((9216, LANES)),
        in_specs=[SM, by_rows, by_rows, own_rows, whole_right, whole_right, whole_head, whole_tail, front_rows]
        + [whole_child] * 3,
        out_specs=front_rows,
        compiler_params=pltpu.CompilerParams(vmem_limit_bytes=VMEM_LIMIT),
        cost_estimate=cost(18),
    )(
        meta,
        yh,
        yl,
        own,
        rh,
        rl,
        head_u,
        tail_u,
        parent.reshape(9216, LANES),
        *(x.reshape(6, 512, LANES) for x in (above, middle, below)),
    )
    return out.reshape(6, 1, NB, 3, 1, NB)


def solution(mesh):
    in_specs = (
        P(None, "prow", None, None, "pcol", None),
        P(None, "prow", None, None, "pcol", None),
        P(),
    )
    out_specs = P(None, "prow", None, None, "pcol", None)
    return jax.shard_map(
        per_device, mesh=mesh, in_specs=in_specs, out_specs=out_specs, check_vma=False
    )
```

```python
import jax
import jax.numpy as jnp
from jax import lax
from jax.experimental import pallas as pl
from jax.experimental.pallas import tpu as pltpu
from jax.sharding import PartitionSpec as P

KB = 5
NB = 256
HB = 128
LANES = 128
F32 = jnp.float32
BF16 = jnp.bfloat16
VMEM_LIMIT = 60 * 1024 * 1024
VM = pl.BlockSpec(memory_space=pltpu.VMEM)
SM = pl.BlockSpec(memory_space=pltpu.SMEM)


def route_of(meta, child, residue):
    there, slot = False, 0
    for turn in range(4):
        target = meta[child * 16 + 4 * turn + residue]
        here = target % 8 == meta[32]
        there = jnp.logical_or(there, here)
        slot = jnp.where(here, target // 8, slot)
    return there, slot


def turn_for(meta, target_row):
    child, residue = meta[32] // 4, meta[32] % 4
    chosen = 0
    for turn in range(1, 4):
        chosen = jnp.where(meta[child * 16 + 4 * turn + residue] % 8 == target_row, turn, chosen)
    return chosen


def residue_of(row, e):
    return (3 * row + 4 + e) % 4


def pick_kernel(meta, parts_ref, out_ref):
    for target_row in range(8):
        turn = turn_for(meta, target_row)
        for v in range(2):
            out_ref[target_row, v] = parts_ref[v, turn]


def copy_kernel(meta, block_ref, out_ref):
    out_ref[...] = block_ref[...]


def assemble_kernel(meta, rest_ref, got_ref, out_ref):
    out_ref[...] = rest_ref[...]
    for child in range(2):
        for residue in range(4):
            there, slot = route_of(meta, child, residue)
            for v in range(2):
                column = meta[child * 16 + v]

                @pl.when(jnp.logical_and(there, column < KB))
                def _():
                    out_ref[column, slot] = out_ref[column, slot] + got_ref[4 * child + residue, v]


def chunk_kernel(meta, mine_ref, got_a_ref, got_b_ref, out_ref):
    for row, picks in enumerate(CHUNKS):

        @pl.when(meta[32] == row)
        def _():
            for at in range(3):
                kind, index = picks[at] if at < len(picks) else (0, 0)
                source = (mine_ref, got_a_ref, got_b_ref)[kind]
                out_ref[at] = source[index]


CHUNKS = [
    [(0, 0), (0, 5), (0, 6)],
    [(0, 1), (0, 2), (0, 6)],
    [(0, 2), (0, 3), (0, 4)],
    [(0, 3), (0, 4)],
    [(0, 4), (0, 5), (0, 6)],
    [(1, 0), (1, 1), (0, 6)],
    [(1, 0), (1, 1), (1, 2)],
    [(2, 0)],
]
UPPER_AT = {
    (0, 0): (0, 0),
    (0, 1): (7, 0),
    (0, 2): (6, 0),
    (0, 3): (6, 1),
    (0, 4): (6, 2),
    (1, 1): (1, 0),
    (1, 2): (1, 1),
    (1, 3): (5, 0),
    (1, 4): (5, 1),
    (2, 2): (2, 0),
    (2, 3): (2, 1),
    (2, 4): (2, 2),
    (3, 3): (3, 0),
    (3, 4): (3, 1),
    (4, 4): (4, 0),
}
CHILD_AT = {
    (0, 0, 0): (0, 1),
    (0, 0, 1): (0, 2),
    (0, 1, 1): (1, 2),
    (1, 0, 0): (4, 1),
    (1, 0, 1): (4, 2),
    (1, 1, 1): (5, 2),
}


UPPER = list(UPPER_AT)
TRI = len(UPPER)


def packed(k, i):
    return k * (2 * KB + 1 - k) // 2 + i - k


def exact(a, b, dims):
    return lax.dot_general(a, b, (dims, ((), ())), precision=lax.Precision.HIGHEST, preferred_element_type=F32)


def dot3(ah, al, bh, bl, dims):
    def dot(a, b):
        return lax.dot_general(a, b, (dims, ((), ())), preferred_element_type=F32)

    return dot(ah, bh) + (dot(ah, bl) + dot(al, bh))


NN = ((1,), (0,))
NT = ((1,), (1,))
TN = ((0,), (0,))


def factor_128(a_ref, x_ref, u_ref):
    shape = (8, LANES)
    lane = lax.broadcasted_iota(jnp.int32, (HB, LANES), 1)
    sub = lax.broadcasted_iota(jnp.int32, (HB, LANES), 0)
    x_ref[...] = jnp.where(lane == sub, 1.0, 0.0).astype(F32)
    for g in range(HB // 8):
        rows = slice(8 * g, 8 * g + 8)
        a_g = a_ref[rows, :]
        x_g = x_ref[rows, :]
        cols = [jnp.broadcast_to(a_g[:, 8 * g + s : 8 * g + s + 1], shape) for s in range(8)]
        d = [[jnp.broadcast_to(cols[s][t : t + 1, :], shape) for s in range(t + 1)] for t in range(8)]
        low = [[None] * 8 for _ in range(8)]
        rinv = []
        for s in range(8):
            r = lax.rsqrt(d[s][s])
            rinv.append(r)
            for t in range(s + 1, 8):
                low[t][s] = d[t][s] * r
            for t in range(s + 1, 8):
                for t2 in range(s + 1, t + 1):
                    d[t][t2] = d[t][t2] - low[t][s] * low[t2][s]
        ub, xb = [], []
        for t in range(8):
            ua = jnp.broadcast_to(a_g[t : t + 1, :], shape)
            xa = jnp.broadcast_to(x_g[t : t + 1, :], shape)
            for s in range(t):
                ua = ua - low[t][s] * ub[s]
                xa = xa - low[t][s] * xb[s]
            ub.append(ua * rinv[t])
            xb.append(xa * rinv[t])
            u_ref[8 * g + t : 8 * g + t + 1, :] = ub[t][0:1, :]
            x_ref[8 * g + t : 8 * g + t + 1, :] = xb[t][0:1, :]
        for i in range(g + 1, HB // 8):
            rows_i = slice(8 * i, 8 * i + 8)
            a_i = a_ref[rows_i, :]
            x_i = x_ref[rows_i, :]
            w = []
            for t in range(8):
                wt = jnp.broadcast_to(a_i[:, 8 * g + t : 8 * g + t + 1], shape)
                for s in range(t):
                    wt = wt - low[t][s] * w[s]
                w.append(wt * rinv[t])
            for t in range(8):
                a_i = a_i - w[t] * ub[t]
                x_i = x_i - w[t] * xb[t]
            a_ref[rows_i, :] = a_i
            x_ref[rows_i, :] = x_i
    u_ref[...] = jnp.where(lane >= sub, u_ref[...], 0.0)


def split(a):
    high = a.astype(BF16)
    return high, (a - high.astype(F32)).astype(BF16)


def chain_kernel(meta, parts_ref, u_ref, th_ref, tl_ref, f_ref, v_ref, a_s, x_s, u_s, stage, sems):
    sources = list(UPPER_AT.values()) + list(CHILD_AT.values())
    copies = [
        pltpu.make_async_copy(parts_ref.at[p, :, j], stage.at[at], sems.at[at]) for at, (p, j) in enumerate(sources)
    ]
    for copy in copies:
        copy.start()

    def take(at, s, h):
        return stage[at, s, pl.ds(h, 16, stride=2), :]

    for at, (k, i) in enumerate(UPPER):
        copies[at].wait()
        for s in range(16):
            for h in range(2):
                f_ref[k * KB + i, 16 * s : 16 * s + 16, HB * h : HB * h + HB] = take(at, s, h)
    for at, (c, u, v) in enumerate(CHILD_AT):
        copies[TRI + at].wait()
        k = meta[c * 16 + u]
        i = meta[c * 16 + v]

        @pl.when(jnp.logical_and(k < KB, i < KB))
        def _():
            for s in range(16):
                for h in range(2):
                    place = (k * KB + i, slice(16 * s, 16 * s + 16), slice(HB * h, HB * h + HB))
                    f_ref[place] = f_ref[place] + take(TRI + at, s, h)

    @pl.loop(0, 2 * KB)
    def _(step):
        k = step // 2
        half = step % 2
        kk = k * KB + k
        pk = packed(k, k)

        @pl.when(half == 0)
        def _():
            a_s[...] = f_ref[kk, 0:HB, 0:HB]

        @pl.when(half == 1)
        def _():
            u12 = exact(v_ref[0:HB, 0:HB], f_ref[kk, 0:HB, HB:NB], NN)
            u_ref[pk, 0:HB, HB:NB] = u12
            a_s[...] = f_ref[kk, HB:NB, HB:NB] - exact(u12, u12, TN)

        factor_128(a_s, x_s, u_s)

        @pl.when(half == 0)
        def _():
            u_ref[pk, 0:HB, 0:HB] = u_s[...]
            v_ref[0:HB, 0:HB] = x_s[...]

        @pl.when(half == 1)
        def _():
            u_ref[pk, HB:NB, HB:NB] = u_s[...]
            u_ref[pk, HB:NB, 0:HB] = jnp.zeros((HB, HB), F32)
            v_ref[HB:NB, HB:NB] = x_s[...]
            v_ref[0:HB, HB:NB] = jnp.zeros((HB, HB), F32)
            lx = exact(u_ref[pk, 0:HB, HB:NB], v_ref[0:HB, 0:HB], TN)
            v_ref[HB:NB, 0:HB] = -exact(x_s[...], lx, NN)
            high, low = split(v_ref[...].T)
            th_ref[pk] = high
            tl_ref[pk] = low
            vh, vl = split(v_ref[...])

            @pl.loop(k + 1, KB)
            def _(i):
                u = dot3(vh, vl, *split(f_ref[k * KB + i]), NN)
                at = packed(k, i)
                u_ref[at] = u
                high, low = split(u)
                th_ref[at] = high
                tl_ref[at] = low

            @pl.loop(k + 1, KB)
            def _(i):
                at_i = packed(k, i)

                @pl.loop(i, KB)
                def _(j):
                    at_j = packed(k, j)
                    f_ref[i * KB + j] = f_ref[i * KB + j] - dot3(
                        th_ref[at_i], tl_ref[at_i], th_ref[at_j], tl_ref[at_j], TN
                    )


def solve_rows(raw_ref, yh_ref, yl_ref, th_ref, tl_ref):
    def factor(m, k):
        return th_ref[packed(m, k)], tl_ref[packed(m, k)]

    for k in range(KB):
        at = slice(NB * k, NB * k + NB)
        t = raw_ref[:, at]
        for m in range(k):
            am = slice(NB * m, NB * m + NB)
            t = t - dot3(yh_ref[:, am], yl_ref[:, am], *factor(m, k), NN)
        high, low = split(t)
        y = dot3(high, low, *factor(k, k), NN)
        raw_ref[:, at] = y
        high, low = split(y)
        yh_ref[:, at] = high
        yl_ref[:, at] = low


def right_kernel(parts_ref, th_ref, tl_ref, yh_ref, yl_ref, raw):
    @pl.loop(0, 16)
    def _(s):
        for c in range(3):
            for j in range(KB):
                for h in range(2):
                    raw[pl.ds(pl.multiple_of(NB * c + 16 * s, 16), 16), NB * j + HB * h : NB * j + HB * h + HB] = parts_ref[
                        s, j, c, pl.ds(h, 16, stride=2), :
                    ]
    solve_rows(raw, yh_ref, yl_ref, th_ref, tl_ref)


ROWS_STEP = 2


def left_kernel(meta, parts_ref, th_ref, tl_ref, yh_ref, yl_ref, own_ref, raw):
    @pl.loop(0, 16)
    def _(s):
        for a in range(ROWS_STEP):
            for j in range(KB):
                for h in range(2):
                    raw[pl.ds(pl.multiple_of(NB * a + 16 * s, 16), 16), NB * j + HB * h : NB * j + HB * h + HB] = parts_ref[
                        s, j, a, pl.ds(h, 16, stride=2), :
                    ]
    solve_rows(raw, yh_ref, yl_ref, th_ref, tl_ref)
    for j in range(KB):

        @pl.when(meta[33] == j)
        def _():
            own_ref[...] = raw[:, NB * j : NB * j + NB]


def schur_kernel(meta, yh, yl, own_ref, rh_ref, rl_ref, u_ref, parent_ref, child_0, child_1, child_2, out_ref):
    step = pl.program_id(0)
    row, col = meta[32], meta[33]
    routes = []
    for child in range(2):
        for e in range(3):
            routes.append((child, *route_of(meta, child, residue_of(row, e))))

    for a in range(ROWS_STEP):
        slot = step * ROWS_STEP + a
        block_row = row + 8 * slot
        rows = slice(NB * a, NB * a + NB)
        for c in range(3):
            block_col = col + 16 * c

            def put(h, value):
                out_ref[pl.ds(1536 * a + 2 * c + h, NB, stride=6), :] = value

            @pl.when(jnp.logical_and(block_row >= KB, block_col >= KB))
            def _():
                cols = slice(NB * c, NB * c + NB)
                product = dot3(yh[rows, :], yl[rows, :], rh_ref[cols, :], rl_ref[cols, :], NT)
                for h in range(2):
                    put(h, parent_ref[pl.ds(1536 * a + 2 * c + h, NB, stride=6), :] - product[:, HB * h : HB * h + HB])
                turn = block_col % 3
                source = block_col // 3
                for n, (child, there, to) in enumerate(routes):
                    here = jnp.logical_and(there, to == slot)
                    here = jnp.logical_and(here, meta[child * 16 + source] == block_col)
                    for d, child_ref in enumerate((child_0, child_1, child_2)):

                        @pl.when(jnp.logical_and(here, turn == d))
                        def _():
                            for h in range(2):
                                at = pl.ds(1536 * a + 2 * c + h, NB, stride=6)
                                out_ref[at, :] = out_ref[at, :] + child_ref[n, pl.ds(h, NB, stride=2), :]

            @pl.when(jnp.logical_and(block_row < KB, block_col >= KB))
            def _():
                for h in range(2):
                    put(h, jnp.zeros((NB, HB), F32))

            if c == 0:

                @pl.when(jnp.logical_and(block_row >= KB, block_col < KB))
                def _():
                    for h in range(2):
                        put(h, own_ref[rows, HB * h : HB * h + HB])

                in_lead = jnp.logical_and(block_row < KB, block_col < KB)
                upper = block_row < block_col

                @pl.when(jnp.logical_and(in_lead, upper))
                def _():
                    for h in range(2):
                        put(h, jnp.zeros((NB, HB), F32))

                @pl.when(jnp.logical_and(in_lead, jnp.logical_not(upper)))
                def _():
                    block = u_ref[jnp.clip(packed(block_col, block_row), 0, TRI - 1)].T
                    for h in range(2):
                        put(h, block[:, HB * h : HB * h + HB])


def cost(microseconds):
    return pl.CostEstimate(flops=int(microseconds * 1.1e9), bytes_accessed=1 << 20, transcendentals=0)


def call(kernel, out_shape, in_specs, scratch, microseconds=2):
    return pl.pallas_call(
        kernel,
        out_shape=out_shape,
        in_specs=in_specs,
        out_specs=jax.tree.map(lambda _: VM, out_shape),
        scratch_shapes=scratch,
        compiler_params=pltpu.CompilerParams(vmem_limit_bytes=VMEM_LIMIT),
        cost_estimate=cost(microseconds),
    )


def shaped(shape, dtype=F32):
    return jax.ShapeDtypeStruct(shape, dtype)


def per_device(parent, children, index_maps):
    row = lax.axis_index("prow")
    col = lax.axis_index("pcol")
    meta = jnp.concatenate([index_maps.reshape(-1), jnp.stack([row, col]).astype(jnp.int32)])
    front = parent.reshape(6, NB, 3, 2, LANES)
    lead = front[:, :, 0].reshape(6, 16, 32, LANES)
    child = children.reshape(4, 16, 32, LANES)

    picked = pl.pallas_call(
        copy_kernel,
        grid_spec=pltpu.PrefetchScalarGridSpec(
            num_scalar_prefetch=1,
            grid=(8,),
            in_specs=[pl.BlockSpec((1, 512, LANES), lambda t, meta: (turn_for(meta, t), 0, 0))],
            out_specs=pl.BlockSpec((1, 512, LANES), lambda t, meta: (t, 0, 0)),
        ),
        out_shape=shaped((8, 512, LANES)),
        cost_estimate=cost(3),
    )(meta, child.reshape(4, 512, LANES))

    rest = jnp.concatenate([lead, child], axis=0).transpose(1, 0, 2, 3)
    rest = lax.all_to_all(rest, "pcol", 0, 0, tiled=True)

    mine = jnp.concatenate([rest[0:KB, 0], rest[0:2, 6]], axis=0)
    mine, picked = lax.optimization_barrier((mine, picked))
    shed = jnp.where(row == 0, mine[2:5], mine[3:6])
    got_a = lax.ppermute(shed, "prow", [(0, 6), (1, 5)])
    got_b = lax.ppermute(mine[1:2], "prow", [(0, 7)])
    chunk = call(chunk_kernel, shaped((3, 32, LANES)), [SM, VM, VM, VM], [])(meta, mine, got_a, got_b)
    chunk = lax.all_gather(chunk, "pcol")
    lead_parts = lax.all_gather(chunk, "prow")

    rest, chunk = lax.optimization_barrier((rest, chunk))
    pieces = call(pick_kernel, shaped((8, 2, 32, LANES)), [SM, VM], [])(meta, rest[0:2, 6:10])
    pieces = lax.all_to_all(pieces, "prow", 0, 0, tiled=True)
    slices = call(assemble_kernel, shaped((KB, 6, 32, LANES)), [SM, VM, VM], [])(meta, rest[0:KB, 0:6], pieces)

    left_parts = lax.all_gather(slices, "pcol")

    slices, picked = lax.optimization_barrier((slices, picked))
    got = lax.all_to_all(picked, "prow", 0, 0, tiled=True)
    routed = jnp.stack(
        [
            lax.dynamic_index_in_dim(got, 4 * c + residue_of(row, e), 0, keepdims=False)
            for c in range(2)
            for e in range(3)
        ]
    )
    even, odd = slices[:, 0::2], slices[:, 1::2]
    is_even = col % 2 == 0
    perm_a, perm_b = [], []
    for p in range(8):
        for s in range(16):
            perm_a.append((p * 16 + s, (s // 2) * 16 + p + 8 * (s % 2)))
            perm_b.append((p * 16 + s, (s // 2) * 16 + p + 8 * (1 - s % 2)))
    pair_a = lax.ppermute(jnp.where(is_even, even, odd), ("prow", "pcol"), perm_a)
    pair_b = lax.ppermute(jnp.where(is_even, odd, even), ("prow", "pcol"), perm_b)
    low_side = col < 8
    pair = jnp.stack([jnp.where(low_side, pair_a, pair_b), jnp.where(low_side, pair_b, pair_a)])
    pairs = jnp.broadcast_to(pair[None], (8,) + pair.shape)

    right_parts = lax.all_to_all(pairs, "prow", 0, 0, tiled=True).reshape(16, KB, 3, 32, LANES)
    middle = lax.ppermute(routed, "pcol", [(q, (3 * q + 1) % 16) for q in range(1, 16)])

    lead_parts, _, _ = lax.optimization_barrier((lead_parts, pairs, routed))
    upper, th, tl = pl.pallas_call(
        chain_kernel,
        out_shape=(shaped((TRI, NB, NB)), shaped((TRI, NB, NB), BF16), shaped((TRI, NB, NB), BF16)),
        in_specs=[SM, pl.BlockSpec(memory_space=pl.ANY)],
        out_specs=(VM, VM, VM),
        scratch_shapes=[
            pltpu.VMEM((KB * KB, NB, NB), F32),
            pltpu.VMEM((NB, NB), F32),
            pltpu.VMEM((HB, HB), F32),
            pltpu.VMEM((HB, HB), F32),
            pltpu.VMEM((HB, HB), F32),
            pltpu.VMEM((TRI + 6, 16, 32, LANES), F32),
            pltpu.SemaphoreType.DMA((TRI + 6,)),
        ],
        compiler_params=pltpu.CompilerParams(vmem_limit_bytes=VMEM_LIMIT),
        cost_estimate=cost(66),
    )(meta, lead_parts)

    middle, th = lax.optimization_barrier((middle, th))
    below = lax.ppermute(middle, "pcol", [(q, (q + 1) % 16) for q in range(16)])
    above = lax.ppermute(middle, "pcol", [(q, (q + 15) % 16) for q in range(16)])

    rh, rl = call(
        right_kernel,
        (shaped((768, 1280), BF16), shaped((768, 1280), BF16)),
        [VM] * 3,
        [pltpu.VMEM((768, 1280), F32)],
        12,
    )(right_parts, th, tl)

    rows = NB * ROWS_STEP
    steps = 6 // ROWS_STEP
    whole_tri = pl.BlockSpec((TRI, NB, NB), lambda g: (0, 0, 0))
    by_rows = pl.BlockSpec((rows, 1280), lambda g: (g, 0))
    own_rows = pl.BlockSpec((rows, NB), lambda g: (g, 0))
    yh, yl, own = pl.pallas_call(
        left_kernel,
        grid=(steps,),
        out_shape=(shaped((1536, 1280), BF16), shaped((1536, 1280), BF16), shaped((1536, NB))),
        in_specs=[
            SM,
            pl.BlockSpec((16, KB, ROWS_STEP, 32, LANES), lambda g: (0, 0, g, 0, 0)),
            whole_tri,
            whole_tri,
        ],
        out_specs=(by_rows, by_rows, own_rows),
        scratch_shapes=[pltpu.VMEM((rows, 1280), F32)],
        compiler_params=pltpu.CompilerParams(vmem_limit_bytes=VMEM_LIMIT),
        cost_estimate=cost(20),
    )(meta, left_parts, th, tl)

    whole_right = pl.BlockSpec((768, 1280), lambda g: (0, 0))
    whole_child = pl.BlockSpec((6, 512, LANES), lambda g: (0, 0, 0))
    front_rows = pl.BlockSpec((1536 * ROWS_STEP, LANES), lambda g: (g, 0))
    out = pl.pallas_call(
        schur_kernel,
        grid=(steps,),
        out_shape=shaped((9216, LANES)),
        in_specs=[SM, by_rows, by_rows, own_rows, whole_right, whole_right, whole_tri, front_rows]
        + [whole_child] * 3,
        out_specs=front_rows,
        compiler_params=pltpu.CompilerParams(vmem_limit_bytes=VMEM_LIMIT),
        cost_estimate=cost(18),
    )(
        meta,
        yh,
        yl,
        own,
        rh,
        rl,
        upper,
        parent.reshape(9216, LANES),
        *(x.reshape(6, 512, LANES) for x in (above, middle, below)),
    )
    return out.reshape(6, 1, NB, 3, 1, NB)


def solution(mesh):
    in_specs = (
        P(None, "prow", None, None, "pcol", None),
        P(None, "prow", None, None, "pcol", None),
        P(),
    )
    out_specs = P(None, "prow", None, None, "pcol", None)
    return jax.shard_map(
        per_device, mesh=mesh, in_specs=in_specs, out_specs=out_specs, check_vma=False
    )
```

```python
import jax
import jax.numpy as jnp
from jax import lax
from jax.experimental import pallas as pl
from jax.experimental.pallas import tpu as pltpu
from jax.sharding import PartitionSpec as P

KB = 5
NB = 256
HB = 128
LANES = 128
F32 = jnp.float32
BF16 = jnp.bfloat16
VMEM_LIMIT = 60 * 1024 * 1024
VM = pl.BlockSpec(memory_space=pltpu.VMEM)
SM = pl.BlockSpec(memory_space=pltpu.SMEM)


def route_of(meta, child, residue):
    there, slot = False, 0
    for turn in range(4):
        target = meta[child * 16 + 4 * turn + residue]
        here = target % 8 == meta[32]
        there = jnp.logical_or(there, here)
        slot = jnp.where(here, target // 8, slot)
    return there, slot


def turn_for(meta, target_row):
    child, residue = meta[32] // 4, meta[32] % 4
    chosen = 0
    for turn in range(1, 4):
        chosen = jnp.where(meta[child * 16 + 4 * turn + residue] % 8 == target_row, turn, chosen)
    return chosen


def routed_from(meta, n):
    flip, d = n // 3, n % 3
    row = meta[32]
    residue = (3 * (row + 8 - d)) % 4
    parity = ((row + 16 - 3 * residue - d) // 4) % 2
    child = (parity + flip) % 2
    first = 4 * parity + residue
    second = first + 8
    is_first = meta[child * 16 + first] == 3 * first + d
    is_second = meta[child * 16 + second] == 3 * second + d
    block = jnp.where(is_first, first, second)
    return child, jnp.logical_or(is_first, is_second), (3 * block + d) // 8


ROUTED = (1, 4, 0, 3, 2, 5)


def pick_kernel(meta, parts_ref, out_ref):
    for target_row in range(8):
        turn = turn_for(meta, target_row)
        for v in range(2):
            out_ref[target_row, v] = parts_ref[v, turn]


def assemble_kernel(meta, first_ref, rest_ref, got_ref, out_ref):
    for j in range(KB):
        out_ref[j, 0] = first_ref[j]
        out_ref[j, 1:6] = rest_ref[j]
    for child in range(2):
        for residue in range(4):
            there, slot = route_of(meta, child, residue)
            for v in range(2):
                column = meta[child * 16 + v]

                @pl.when(jnp.logical_and(there, column < KB))
                def _():
                    out_ref[column, slot] = out_ref[column, slot] + got_ref[4 * child + residue, v]


def chunk_kernel(meta, mine_ref, got_a_ref, got_b_ref, out_ref):
    for row, picks in enumerate(CHUNKS):

        @pl.when(meta[32] == row)
        def _():
            for at in range(3):
                kind, index = picks[at] if at < len(picks) else (0, 0)
                source = (mine_ref, got_a_ref, got_b_ref)[kind]
                out_ref[at] = source[index]


CHUNKS = [
    [(0, 0), (0, 5), (0, 6)],
    [(0, 1), (0, 2), (0, 6)],
    [(0, 2), (0, 3), (0, 4)],
    [(0, 3), (0, 4)],
    [(0, 4), (0, 5), (0, 6)],
    [(1, 0), (1, 1), (0, 6)],
    [(1, 0), (1, 1), (1, 2)],
    [(2, 0)],
]
UPPER_AT = {
    (0, 0): (0, 0),
    (0, 1): (7, 0),
    (0, 2): (6, 0),
    (0, 3): (6, 1),
    (0, 4): (6, 2),
    (1, 1): (1, 0),
    (1, 2): (1, 1),
    (1, 3): (5, 0),
    (1, 4): (5, 1),
    (2, 2): (2, 0),
    (2, 3): (2, 1),
    (2, 4): (2, 2),
    (3, 3): (3, 0),
    (3, 4): (3, 1),
    (4, 4): (4, 0),
}
CHILD_AT = {
    (0, 0, 0): (0, 1),
    (0, 0, 1): (0, 2),
    (0, 1, 1): (1, 2),
    (1, 0, 0): (4, 1),
    (1, 0, 1): (4, 2),
    (1, 1, 1): (5, 2),
}


def exact(a, b, dims):
    return lax.dot_general(a, b, (dims, ((), ())), precision=lax.Precision.HIGHEST, preferred_element_type=F32)


def dot3(ah, al, bh, bl, dims):
    def dot(a, b):
        return lax.dot_general(a, b, (dims, ((), ())), preferred_element_type=F32)

    return dot(ah, bh) + (dot(ah, bl) + dot(al, bh))


NN = ((1,), (0,))
NT = ((1,), (1,))
TN = ((0,), (0,))


def factor_128(a_ref, x_ref, u_ref):
    shape = (8, LANES)
    lane = lax.broadcasted_iota(jnp.int32, (HB, LANES), 1)
    sub = lax.broadcasted_iota(jnp.int32, (HB, LANES), 0)
    x_ref[...] = jnp.where(lane == sub, 1.0, 0.0).astype(F32)
    for g in range(HB // 8):
        rows = slice(8 * g, 8 * g + 8)
        a_g = a_ref[rows, :]
        x_g = x_ref[rows, :]
        cols = [jnp.broadcast_to(a_g[:, 8 * g + s : 8 * g + s + 1], shape) for s in range(8)]
        d = [[jnp.broadcast_to(cols[s][t : t + 1, :], shape) for s in range(t + 1)] for t in range(8)]
        low = [[None] * 8 for _ in range(8)]
        rinv = []
        for s in range(8):
            r = lax.rsqrt(d[s][s])
            rinv.append(r)
            for t in range(s + 1, 8):
                low[t][s] = d[t][s] * r
            for t in range(s + 1, 8):
                for t2 in range(s + 1, t + 1):
                    d[t][t2] = d[t][t2] - low[t][s] * low[t2][s]
        ub, xb = [], []
        for t in range(8):
            ua = jnp.broadcast_to(a_g[t : t + 1, :], shape)
            xa = jnp.broadcast_to(x_g[t : t + 1, :], shape)
            for s in range(t):
                ua = ua - low[t][s] * ub[s]
                xa = xa - low[t][s] * xb[s]
            ub.append(ua * rinv[t])
            xb.append(xa * rinv[t])
            u_ref[8 * g + t : 8 * g + t + 1, :] = ub[t][0:1, :]
            x_ref[8 * g + t : 8 * g + t + 1, :] = xb[t][0:1, :]
        for i in range(g + 1, HB // 8):
            rows_i = slice(8 * i, 8 * i + 8)
            a_i = a_ref[rows_i, :]
            x_i = x_ref[rows_i, :]
            w = []
            for t in range(8):
                wt = jnp.broadcast_to(a_i[:, 8 * g + t : 8 * g + t + 1], shape)
                for s in range(t):
                    wt = wt - low[t][s] * w[s]
                w.append(wt * rinv[t])
            for t in range(8):
                a_i = a_i - w[t] * ub[t]
                x_i = x_i - w[t] * xb[t]
            a_ref[rows_i, :] = a_i
            x_ref[rows_i, :] = x_i
    u_ref[...] = jnp.where(lane >= sub, u_ref[...], 0.0)


def split(a):
    high = a.astype(BF16)
    return high, (a - high.astype(F32)).astype(BF16)


CUT = 2
REST = KB - CUT


def packed(n, k, i):
    return k * (2 * n + 1 - k) // 2 + i - k


HEADS = packed(KB, CUT, CUT)
TAILS = packed(REST, REST, REST)


def eliminate(n, steps, f_ref, u_ref, th_ref, tl_ref, v_ref, a_s, x_s, u_s):
    @pl.loop(0, 2 * steps)
    def _(step):
        k = step // 2
        half = step % 2
        kk = k * n + k
        pk = packed(n, k, k)

        @pl.when(half == 0)
        def _():
            a_s[...] = f_ref[kk, 0:HB, 0:HB]

        @pl.when(half == 1)
        def _():
            u12 = exact(v_ref[0:HB, 0:HB], f_ref[kk, 0:HB, HB:NB], NN)
            u_ref[pk, 0:HB, HB:NB] = u12
            a_s[...] = f_ref[kk, HB:NB, HB:NB] - exact(u12, u12, TN)

        factor_128(a_s, x_s, u_s)

        @pl.when(half == 0)
        def _():
            u_ref[pk, 0:HB, 0:HB] = u_s[...]
            v_ref[0:HB, 0:HB] = x_s[...]

        @pl.when(half == 1)
        def _():
            u_ref[pk, HB:NB, HB:NB] = u_s[...]
            u_ref[pk, HB:NB, 0:HB] = jnp.zeros((HB, HB), F32)
            v_ref[HB:NB, HB:NB] = x_s[...]
            v_ref[0:HB, HB:NB] = jnp.zeros((HB, HB), F32)
            lx = exact(u_ref[pk, 0:HB, HB:NB], v_ref[0:HB, 0:HB], TN)
            v_ref[HB:NB, 0:HB] = -exact(x_s[...], lx, NN)
            high, low = split(v_ref[...].T)
            th_ref[pk] = high
            tl_ref[pk] = low
            vh, vl = split(v_ref[...])

            @pl.loop(k + 1, n)
            def _(i):
                u = dot3(vh, vl, *split(f_ref[k * n + i]), NN)
                at = packed(n, k, i)
                u_ref[at] = u
                high, low = split(u)
                th_ref[at] = high
                tl_ref[at] = low

            @pl.loop(k + 1, n)
            def _(i):
                at_i = packed(n, k, i)

                @pl.loop(i, n)
                def _(j):
                    at_j = packed(n, k, j)
                    f_ref[i * n + j] = f_ref[i * n + j] - dot3(
                        th_ref[at_i], tl_ref[at_i], th_ref[at_j], tl_ref[at_j], TN
                    )


def chain_head_kernel(meta, parts_ref, u_ref, th_ref, tl_ref, rest_ref, f_ref, *scratch):
    def take(at, s, h):
        return parts_ref[at[0], s, at[1], pl.ds(h, 16, stride=2), :]

    for (k, i), at in UPPER_AT.items():
        for s in range(16):
            for h in range(2):
                f_ref[k * KB + i, 16 * s : 16 * s + 16, HB * h : HB * h + HB] = take(at, s, h)
    for (c, u, v), at in CHILD_AT.items():
        k = meta[c * 16 + u]
        i = meta[c * 16 + v]

        @pl.when(jnp.logical_and(k < KB, i < KB))
        def _():
            for s in range(16):
                for h in range(2):
                    place = (k * KB + i, slice(16 * s, 16 * s + 16), slice(HB * h, HB * h + HB))
                    f_ref[place] = f_ref[place] + take(at, s, h)

    eliminate(KB, CUT, f_ref, u_ref, th_ref, tl_ref, *scratch)
    for i in range(REST):
        for j in range(i, REST):
            rest_ref[packed(REST, i, j)] = f_ref[(CUT + i) * KB + CUT + j]


def chain_tail_kernel(rest_ref, u_ref, th_ref, tl_ref, f_ref, *scratch):
    for i in range(REST):
        for j in range(i, REST):
            f_ref[i * REST + j] = rest_ref[packed(REST, i, j)]
    eliminate(REST, REST, f_ref, u_ref, th_ref, tl_ref, *scratch)


def solve_rows(raw_ref, yh_ref, yl_ref, factors):
    head_h, head_l, tail_h, tail_l = factors

    def factor(m, k):
        if m < CUT:
            return head_h[packed(KB, m, k)], head_l[packed(KB, m, k)]
        at = packed(REST, m - CUT, k - CUT)
        return tail_h[at], tail_l[at]

    for k in range(KB):
        at = slice(NB * k, NB * k + NB)
        t = raw_ref[:, at]
        for m in range(k):
            am = slice(NB * m, NB * m + NB)
            t = t - dot3(yh_ref[:, am], yl_ref[:, am], *factor(m, k), NN)
        high, low = split(t)
        y = dot3(high, low, *factor(k, k), NN)
        raw_ref[:, at] = y
        high, low = split(y)
        yh_ref[:, at] = high
        yl_ref[:, at] = low


def right_kernel(parts_ref, hh_ref, hl_ref, th_ref, tl_ref, yh_ref, yl_ref, raw):
    @pl.loop(0, 16)
    def _(s):
        for c in range(3):
            for j in range(KB):
                for h in range(2):
                    raw[pl.ds(pl.multiple_of(NB * c + 16 * s, 16), 16), NB * j + HB * h : NB * j + HB * h + HB] = parts_ref[
                        s, j, c, pl.ds(h, 16, stride=2), :
                    ]
    solve_rows(raw, yh_ref, yl_ref, (hh_ref, hl_ref, th_ref, tl_ref))


ROWS_STEP = 2


def left_kernel(meta, parts_ref, hh_ref, hl_ref, th_ref, tl_ref, yh_ref, yl_ref, own_ref, raw):
    @pl.loop(0, 16)
    def _(s):
        for a in range(ROWS_STEP):
            for j in range(KB):
                for h in range(2):
                    raw[pl.ds(pl.multiple_of(NB * a + 16 * s, 16), 16), NB * j + HB * h : NB * j + HB * h + HB] = parts_ref[
                        s, j, a, pl.ds(h, 16, stride=2), :
                    ]
    solve_rows(raw, yh_ref, yl_ref, (hh_ref, hl_ref, th_ref, tl_ref))
    for j in range(KB):

        @pl.when(meta[33] == j)
        def _():
            own_ref[...] = raw[:, NB * j : NB * j + NB]


def schur_kernel(meta, yh, yl, own_ref, rh_ref, rl_ref, head_ref, tail_ref, parent_ref, child_0, child_1, child_2, out_ref):
    step = pl.program_id(0)
    row, col = meta[32], meta[33]
    routes = []
    for n in ROUTED:
        routes.append(routed_from(meta, n))

    for a in range(ROWS_STEP):
        slot = step * ROWS_STEP + a
        block_row = row + 8 * slot
        rows = slice(NB * a, NB * a + NB)
        for c in range(3):
            block_col = col + 16 * c

            def put(h, value):
                out_ref[pl.ds(1536 * a + 2 * c + h, NB, stride=6), :] = value

            @pl.when(jnp.logical_and(block_row >= KB, block_col >= KB))
            def _():
                cols = slice(NB * c, NB * c + NB)
                product = dot3(yh[rows, :], yl[rows, :], rh_ref[cols, :], rl_ref[cols, :], NT)
                for h in range(2):
                    put(h, parent_ref[pl.ds(1536 * a + 2 * c + h, NB, stride=6), :] - product[:, HB * h : HB * h + HB])
                turn = block_col % 3
                source = block_col // 3
                for n, (child, there, to) in enumerate(routes):
                    here = jnp.logical_and(there, to == slot)
                    here = jnp.logical_and(here, meta[child * 16 + source] == block_col)
                    for d, child_ref in enumerate((child_0, child_1, child_2)):

                        @pl.when(jnp.logical_and(here, turn == d))
                        def _():
                            for h in range(2):
                                at = pl.ds(1536 * a + 2 * c + h, NB, stride=6)
                                out_ref[at, :] = out_ref[at, :] + child_ref[n, pl.ds(h, NB, stride=2), :]

            @pl.when(jnp.logical_and(block_row < KB, block_col >= KB))
            def _():
                for h in range(2):
                    put(h, jnp.zeros((NB, HB), F32))

            if c == 0:

                @pl.when(jnp.logical_and(block_row >= KB, block_col < KB))
                def _():
                    for h in range(2):
                        put(h, own_ref[rows, HB * h : HB * h + HB])

                in_lead = jnp.logical_and(block_row < KB, block_col < KB)
                upper = block_row < block_col

                @pl.when(jnp.logical_and(in_lead, upper))
                def _():
                    for h in range(2):
                        put(h, jnp.zeros((NB, HB), F32))

                lower = jnp.logical_and(in_lead, jnp.logical_not(upper))

                @pl.when(jnp.logical_and(lower, block_col < CUT))
                def _():
                    block = head_ref[jnp.clip(packed(KB, block_col, block_row), 0, HEADS - 1)].T
                    for h in range(2):
                        put(h, block[:, HB * h : HB * h + HB])

                @pl.when(jnp.logical_and(lower, block_col >= CUT))
                def _():
                    at = jnp.clip(packed(REST, block_col - CUT, block_row - CUT), 0, TAILS - 1)
                    block = tail_ref[at].T
                    for h in range(2):
                        put(h, block[:, HB * h : HB * h + HB])


def cost(microseconds):
    return pl.CostEstimate(flops=int(microseconds * 1.1e9), bytes_accessed=1 << 20, transcendentals=0)


def call(kernel, out_shape, in_specs, scratch, microseconds=2):
    return pl.pallas_call(
        kernel,
        out_shape=out_shape,
        in_specs=in_specs,
        out_specs=jax.tree.map(lambda _: VM, out_shape),
        scratch_shapes=scratch,
        compiler_params=pltpu.CompilerParams(vmem_limit_bytes=VMEM_LIMIT),
        cost_estimate=cost(microseconds),
    )


def shaped(shape, dtype=F32):
    return jax.ShapeDtypeStruct(shape, dtype)


def per_device(parent, children, index_maps):
    row = lax.axis_index("prow")
    col = lax.axis_index("pcol")
    meta = jnp.concatenate([index_maps.reshape(-1), jnp.stack([row, col]).astype(jnp.int32)])
    front = parent.reshape(6, NB, 3, 2, LANES)
    lead = front[:, :, 0].reshape(6, 16, 32, LANES)
    child = children.reshape(4, 16, 32, LANES)

    child_id = row // 4
    twos = child.reshape(2, 2, 512, LANES)
    picked = [lax.dynamic_index_in_dim(twos, (child_id + flip) % 2, 1, keepdims=False) for flip in range(2)]

    first = jnp.stack([lead[0], child[0]], axis=1)
    first = lax.all_to_all(first, "pcol", 0, 0, tiled=True)
    mine = jnp.concatenate([first[0:KB, 0], first[0:2, 1]], axis=0)
    mine, *picked = lax.optimization_barrier((mine, *picked))
    shed = jnp.where(row == 0, mine[2:5], mine[3:6])
    got_a = lax.ppermute(shed, "prow", [(0, 6), (1, 5)])
    got_b = lax.ppermute(mine[1:2], "prow", [(0, 7)])
    chunk = call(chunk_kernel, shaped((3, 32, LANES)), [SM, VM, VM, VM], [])(meta, mine, got_a, got_b)
    chunk = lax.all_gather(chunk, "pcol")
    lead_parts = lax.all_gather(chunk, "prow")

    rest = jnp.concatenate([lead[1:], child], axis=0).transpose(1, 0, 2, 3)
    rest, chunk = lax.optimization_barrier((rest, chunk))
    rest = lax.all_to_all(rest, "pcol", 0, 0, tiled=True)
    pieces = call(pick_kernel, shaped((8, 2, 32, LANES)), [SM, VM], [])(meta, rest[0:2, 5:9])
    pieces = lax.all_to_all(pieces, "prow", 0, 0, tiled=True)
    slices = call(assemble_kernel, shaped((KB, 6, 32, LANES)), [SM, VM, VM, VM], [])(
        meta, mine[0:KB], rest[0:KB, 0:5], pieces
    )

    left_parts = lax.all_gather(slices, "pcol")

    lead_parts, slices, *picked = lax.optimization_barrier((lead_parts, slices, *picked))
    got = []
    for flip in range(2):
        perm = []
        for p in range(8):
            target = (3 * (p % 4) + 1 + 4 * ((p // 4 + flip) % 2)) % 8
            perm += [(p * 16 + q, target * 16 + (3 * q + 1) % 16) for q in range(1, 16)]
        got.append(lax.ppermute(picked[flip], ("prow", "pcol"), perm))
    even, odd = slices[:, 0::2], slices[:, 1::2]
    is_even = col % 2 == 0
    perm_a, perm_b = [], []
    for p in range(8):
        for s in range(16):
            perm_a.append((p * 16 + s, (s // 2) * 16 + p + 8 * (s % 2)))
            perm_b.append((p * 16 + s, (s // 2) * 16 + p + 8 * (1 - s % 2)))
    pair_a = lax.ppermute(jnp.where(is_even, even, odd), ("prow", "pcol"), perm_a)
    pair_b = lax.ppermute(jnp.where(is_even, odd, even), ("prow", "pcol"), perm_b)
    low_side = col < 8
    pair = jnp.stack([jnp.where(low_side, pair_a, pair_b), jnp.where(low_side, pair_b, pair_a)])
    pairs = jnp.broadcast_to(pair[None], (8,) + pair.shape)

    scratch = [
        pltpu.VMEM((NB, NB), F32),
        pltpu.VMEM((HB, HB), F32),
        pltpu.VMEM((HB, HB), F32),
        pltpu.VMEM((HB, HB), F32),
    ]
    head_u, head_h, head_l, left_over = call(
        chain_head_kernel,
        (
            shaped((HEADS, NB, NB)),
            shaped((HEADS, NB, NB), BF16),
            shaped((HEADS, NB, NB), BF16),
            shaped((TAILS, NB, NB)),
        ),
        [SM, VM],
        [pltpu.VMEM((KB * KB, NB, NB), F32)] + scratch,
        32,
    )(meta, lead_parts)

    left_over, pairs, *got = lax.optimization_barrier((left_over, pairs, *got))

    residue = (3 * (row + 7)) % 4
    parity = ((row + 15 - 3 * residue) // 4) % 2
    chosen = {}
    for flip in range(2):
        block = 4 * parity + residue
        origin = meta[(parity + flip) % 2 * 16 + block] - 3 * block
        for d in range(3):
            which = jnp.where(origin == d, 0, 1)
            chosen[flip, d] = lax.dynamic_index_in_dim(got[flip], which, 0, keepdims=False)
    down = jnp.stack([chosen[0, 0], chosen[1, 0]])
    up = jnp.stack([chosen[0, 2], chosen[1, 2]])
    down = lax.ppermute(down, "prow", [(p, (p + 7) % 8) for p in range(8)])
    up = lax.ppermute(up, "prow", [(p, (p + 1) % 8) for p in range(8)])
    right_parts = lax.all_to_all(pairs, "prow", 0, 0, tiled=True).reshape(16, KB, 3, 32, LANES)
    tail_u, tail_h, tail_l = call(
        chain_tail_kernel,
        (shaped((TAILS, NB, NB)), shaped((TAILS, NB, NB), BF16), shaped((TAILS, NB, NB), BF16)),
        [VM],
        [pltpu.VMEM((REST * REST, NB, NB), F32)] + scratch,
        40,
    )(left_over)

    middle = jnp.concatenate([jnp.stack([chosen[0, 1], chosen[1, 1]]), down, up])
    middle, tail_h = lax.optimization_barrier((middle, tail_h))
    below = lax.ppermute(middle, "pcol", [(q, (q + 1) % 16) for q in range(16)])
    above = lax.ppermute(middle, "pcol", [(q, (q + 15) % 16) for q in range(16)])

    rh, rl = call(
        right_kernel,
        (shaped((768, 1280), BF16), shaped((768, 1280), BF16)),
        [VM] * 5,
        [pltpu.VMEM((768, 1280), F32)],
        12,
    )(right_parts, head_h, head_l, tail_h, tail_l)

    rows = NB * ROWS_STEP
    steps = 6 // ROWS_STEP
    whole_head = pl.BlockSpec((HEADS, NB, NB), lambda g: (0, 0, 0))
    whole_tail = pl.BlockSpec((TAILS, NB, NB), lambda g: (0, 0, 0))
    by_rows = pl.BlockSpec((rows, 1280), lambda g: (g, 0))
    own_rows = pl.BlockSpec((rows, NB), lambda g: (g, 0))
    yh, yl, own = pl.pallas_call(
        left_kernel,
        grid=(steps,),
        out_shape=(shaped((1536, 1280), BF16), shaped((1536, 1280), BF16), shaped((1536, NB))),
        in_specs=[
            SM,
            pl.BlockSpec((16, KB, ROWS_STEP, 32, LANES), lambda g: (0, 0, g, 0, 0)),
            whole_head,
            whole_head,
            whole_tail,
            whole_tail,
        ],
        out_specs=(by_rows, by_rows, own_rows),
        scratch_shapes=[pltpu.VMEM((rows, 1280), F32)],
        compiler_params=pltpu.CompilerParams(vmem_limit_bytes=VMEM_LIMIT),
        cost_estimate=cost(20),
    )(meta, left_parts, head_h, head_l, tail_h, tail_l)

    whole_right = pl.BlockSpec((768, 1280), lambda g: (0, 0))
    whole_child = pl.BlockSpec((6, 512, LANES), lambda g: (0, 0, 0))
    front_rows = pl.BlockSpec((1536 * ROWS_STEP, LANES), lambda g: (g, 0))
    out = pl.pallas_call(
        schur_kernel,
        grid=(steps,),
        out_shape=shaped((9216, LANES)),
        in_specs=[SM, by_rows, by_rows, own_rows, whole_right, whole_right, whole_head, whole_tail, front_rows]
        + [whole_child] * 3,
        out_specs=front_rows,
        compiler_params=pltpu.CompilerParams(vmem_limit_bytes=VMEM_LIMIT),
        cost_estimate=cost(18),
    )(
        meta,
        yh,
        yl,
        own,
        rh,
        rl,
        head_u,
        tail_u,
        parent.reshape(9216, LANES),
        *(x.reshape(6, 512, LANES) for x in (above, middle, below)),
    )
    return out.reshape(6, 1, NB, 3, 1, NB)


def solution(mesh):
    in_specs = (
        P(None, "prow", None, None, "pcol", None),
        P(None, "prow", None, None, "pcol", None),
        P(),
    )
    out_specs = P(None, "prow", None, None, "pcol", None)
    return jax.shard_map(
        per_device, mesh=mesh, in_specs=in_specs, out_specs=out_specs, check_vma=False
    )
```

```python
import jax
import jax.numpy as jnp
from jax import lax
from jax.experimental import pallas as pl
from jax.experimental.pallas import tpu as pltpu
from jax.sharding import PartitionSpec as P

KB = 5
NB = 256
HB = 128
LANES = 128
F32 = jnp.float32
BF16 = jnp.bfloat16
VMEM_LIMIT = 60 * 1024 * 1024
VM = pl.BlockSpec(memory_space=pltpu.VMEM)
SM = pl.BlockSpec(memory_space=pltpu.SMEM)


def route_of(meta, child, residue):
    there, slot = False, 0
    for turn in range(4):
        target = meta[child * 16 + 4 * turn + residue]
        here = target % 8 == meta[32]
        there = jnp.logical_or(there, here)
        slot = jnp.where(here, target // 8, slot)
    return there, slot


def turn_for(meta, target_row):
    child, residue = meta[32] // 4, meta[32] % 4
    chosen = 0
    for turn in range(1, 4):
        chosen = jnp.where(meta[child * 16 + 4 * turn + residue] % 8 == target_row, turn, chosen)
    return chosen


def routed_from(meta, n):
    flip, d = n // 3, n % 3
    row = meta[32]
    residue = (3 * (row + 8 - d)) % 4
    parity = ((row + 16 - 3 * residue - d) // 4) % 2
    child = (parity + flip) % 2
    first = 4 * parity + residue
    second = first + 8
    is_first = meta[child * 16 + first] == 3 * first + d
    is_second = meta[child * 16 + second] == 3 * second + d
    block = jnp.where(is_first, first, second)
    return child, jnp.logical_or(is_first, is_second), (3 * block + d) // 8


ROUTED = (1, 4, 0, 3, 2, 5)


def pick_kernel(meta, parts_ref, out_ref):
    for target_row in range(8):
        turn = turn_for(meta, target_row)
        for v in range(2):
            out_ref[target_row, v] = parts_ref[v, turn]


def assemble_kernel(meta, first_ref, rest_ref, got_ref, out_ref):
    for j in range(KB):
        out_ref[j, 0] = first_ref[j]
        out_ref[j, 1:6] = rest_ref[j]
    for child in range(2):
        for residue in range(4):
            there, slot = route_of(meta, child, residue)
            for v in range(2):
                column = meta[child * 16 + v]

                @pl.when(jnp.logical_and(there, column < KB))
                def _():
                    out_ref[column, slot] = out_ref[column, slot] + got_ref[4 * child + residue, v]


def chunk_kernel(meta, mine_ref, got_a_ref, got_b_ref, out_ref):
    for row, picks in enumerate(CHUNKS):

        @pl.when(meta[32] == row)
        def _():
            for at in range(3):
                kind, index = picks[at] if at < len(picks) else (0, 0)
                source = (mine_ref, got_a_ref, got_b_ref)[kind]
                out_ref[at] = source[index]


CHUNKS = [
    [(0, 0), (0, 5), (0, 6)],
    [(0, 1), (0, 2), (0, 6)],
    [(0, 2), (0, 3), (0, 4)],
    [(0, 3), (0, 4)],
    [(0, 4), (0, 5), (0, 6)],
    [(1, 0), (1, 1), (0, 6)],
    [(1, 0), (1, 1), (1, 2)],
    [(2, 0)],
]
UPPER_AT = {
    (0, 0): (0, 0),
    (0, 1): (7, 0),
    (0, 2): (6, 0),
    (0, 3): (6, 1),
    (0, 4): (6, 2),
    (1, 1): (1, 0),
    (1, 2): (1, 1),
    (1, 3): (5, 0),
    (1, 4): (5, 1),
    (2, 2): (2, 0),
    (2, 3): (2, 1),
    (2, 4): (2, 2),
    (3, 3): (3, 0),
    (3, 4): (3, 1),
    (4, 4): (4, 0),
}
CHILD_AT = {
    (0, 0, 0): (0, 1),
    (0, 0, 1): (0, 2),
    (0, 1, 1): (1, 2),
    (1, 0, 0): (4, 1),
    (1, 0, 1): (4, 2),
    (1, 1, 1): (5, 2),
}


def exact(a, b, dims):
    return lax.dot_general(a, b, (dims, ((), ())), precision=lax.Precision.HIGHEST, preferred_element_type=F32)


def dot3(ah, al, bh, bl, dims):
    def dot(a, b):
        return lax.dot_general(a, b, (dims, ((), ())), preferred_element_type=F32)

    return dot(ah, bh) + (dot(ah, bl) + dot(al, bh))


NN = ((1,), (0,))
NT = ((1,), (1,))
TN = ((0,), (0,))


def factor_128(a_ref, x_ref, u_ref):
    shape = (8, LANES)
    lane = lax.broadcasted_iota(jnp.int32, (HB, LANES), 1)
    sub = lax.broadcasted_iota(jnp.int32, (HB, LANES), 0)
    x_ref[...] = jnp.where(lane == sub, 1.0, 0.0).astype(F32)
    for g in range(HB // 8):
        rows = slice(8 * g, 8 * g + 8)
        a_g = a_ref[rows, :]
        x_g = x_ref[rows, :]
        cols = [jnp.broadcast_to(a_g[:, 8 * g + s : 8 * g + s + 1], shape) for s in range(8)]
        d = [[jnp.broadcast_to(cols[s][t : t + 1, :], shape) for s in range(t + 1)] for t in range(8)]
        low = [[None] * 8 for _ in range(8)]
        rinv = []
        for s in range(8):
            r = lax.rsqrt(d[s][s])
            rinv.append(r)
            for t in range(s + 1, 8):
                low[t][s] = d[t][s] * r
            for t in range(s + 1, 8):
                for t2 in range(s + 1, t + 1):
                    d[t][t2] = d[t][t2] - low[t][s] * low[t2][s]
        ub, xb = [], []
        for t in range(8):
            ua = jnp.broadcast_to(a_g[t : t + 1, :], shape)
            xa = jnp.broadcast_to(x_g[t : t + 1, :], shape)
            for s in range(t):
                ua = ua - low[t][s] * ub[s]
                xa = xa - low[t][s] * xb[s]
            ub.append(ua * rinv[t])
            xb.append(xa * rinv[t])
            u_ref[8 * g + t : 8 * g + t + 1, :] = ub[t][0:1, :]
            x_ref[8 * g + t : 8 * g + t + 1, :] = xb[t][0:1, :]
        for i in range(g + 1, HB // 8):
            rows_i = slice(8 * i, 8 * i + 8)
            a_i = a_ref[rows_i, :]
            x_i = x_ref[rows_i, :]
            w = []
            for t in range(8):
                wt = jnp.broadcast_to(a_i[:, 8 * g + t : 8 * g + t + 1], shape)
                for s in range(t):
                    wt = wt - low[t][s] * w[s]
                w.append(wt * rinv[t])
            for t in range(8):
                a_i = a_i - w[t] * ub[t]
                x_i = x_i - w[t] * xb[t]
            a_ref[rows_i, :] = a_i
            x_ref[rows_i, :] = x_i
    u_ref[...] = jnp.where(lane >= sub, u_ref[...], 0.0)


def split(a):
    high = a.astype(BF16)
    return high, (a - high.astype(F32)).astype(BF16)


CUT = 2
REST = KB - CUT


def packed(n, k, i):
    return k * (2 * n + 1 - k) // 2 + i - k


HEADS = packed(KB, CUT, CUT)
TAILS = packed(REST, REST, REST)


def eliminate(n, steps, f_ref, u_ref, th_ref, tl_ref, v_ref, a_s, x_s, u_s):
    @pl.loop(0, 2 * steps)
    def _(step):
        k = step // 2
        half = step % 2
        kk = k * n + k
        pk = packed(n, k, k)

        @pl.when(half == 0)
        def _():
            a_s[...] = f_ref[kk, 0:HB, 0:HB]

        @pl.when(half == 1)
        def _():
            u12 = exact(v_ref[0:HB, 0:HB], f_ref[kk, 0:HB, HB:NB], NN)
            u_ref[pk, 0:HB, HB:NB] = u12
            a_s[...] = f_ref[kk, HB:NB, HB:NB] - exact(u12, u12, TN)

        factor_128(a_s, x_s, u_s)

        @pl.when(half == 0)
        def _():
            u_ref[pk, 0:HB, 0:HB] = u_s[...]
            v_ref[0:HB, 0:HB] = x_s[...]

        @pl.when(half == 1)
        def _():
            u_ref[pk, HB:NB, HB:NB] = u_s[...]
            u_ref[pk, HB:NB, 0:HB] = jnp.zeros((HB, HB), F32)
            v_ref[HB:NB, HB:NB] = x_s[...]
            v_ref[0:HB, HB:NB] = jnp.zeros((HB, HB), F32)
            lx = exact(u_ref[pk, 0:HB, HB:NB], v_ref[0:HB, 0:HB], TN)
            v_ref[HB:NB, 0:HB] = -exact(x_s[...], lx, NN)
            high, low = split(v_ref[...].T)
            th_ref[pk] = high
            tl_ref[pk] = low
            vh, vl = split(v_ref[...])

            @pl.loop(k + 1, n)
            def _(i):
                u = dot3(vh, vl, *split(f_ref[k * n + i]), NN)
                at = packed(n, k, i)
                u_ref[at] = u
                high, low = split(u)
                th_ref[at] = high
                tl_ref[at] = low

            @pl.loop(k + 1, n)
            def _(i):
                at_i = packed(n, k, i)

                @pl.loop(i, n)
                def _(j):
                    at_j = packed(n, k, j)
                    f_ref[i * n + j] = f_ref[i * n + j] - dot3(
                        th_ref[at_i], tl_ref[at_i], th_ref[at_j], tl_ref[at_j], TN
                    )


def chain_head_kernel(meta, parts_ref, u_ref, th_ref, tl_ref, rest_ref, f_ref, *scratch):
    def take(at, s, h):
        return parts_ref[at[0], s, at[1], pl.ds(h, 16, stride=2), :]

    for (k, i), at in UPPER_AT.items():
        for s in range(16):
            for h in range(2):
                f_ref[k * KB + i, 16 * s : 16 * s + 16, HB * h : HB * h + HB] = take(at, s, h)
    for (c, u, v), at in CHILD_AT.items():
        k = meta[c * 16 + u]
        i = meta[c * 16 + v]

        @pl.when(jnp.logical_and(k < KB, i < KB))
        def _():
            for s in range(16):
                for h in range(2):
                    place = (k * KB + i, slice(16 * s, 16 * s + 16), slice(HB * h, HB * h + HB))
                    f_ref[place] = f_ref[place] + take(at, s, h)

    eliminate(KB, CUT, f_ref, u_ref, th_ref, tl_ref, *scratch)
    for i in range(REST):
        for j in range(i, REST):
            rest_ref[packed(REST, i, j)] = f_ref[(CUT + i) * KB + CUT + j]


def chain_tail_kernel(rest_ref, u_ref, th_ref, tl_ref, f_ref, *scratch):
    for i in range(REST):
        for j in range(i, REST):
            f_ref[i * REST + j] = rest_ref[packed(REST, i, j)]
    eliminate(REST, REST, f_ref, u_ref, th_ref, tl_ref, *scratch)


def solve_rows(raw_ref, yh_ref, yl_ref, factors):
    head_h, head_l, tail_h, tail_l = factors

    def factor(m, k):
        if m < CUT:
            return head_h[packed(KB, m, k)], head_l[packed(KB, m, k)]
        at = packed(REST, m - CUT, k - CUT)
        return tail_h[at], tail_l[at]

    for k in range(KB):
        at = slice(NB * k, NB * k + NB)
        t = raw_ref[:, at]
        for m in range(k):
            am = slice(NB * m, NB * m + NB)
            t = t - dot3(yh_ref[:, am], yl_ref[:, am], *factor(m, k), NN)
        high, low = split(t)
        y = dot3(high, low, *factor(k, k), NN)
        raw_ref[:, at] = y
        high, low = split(y)
        yh_ref[:, at] = high
        yl_ref[:, at] = low


def right_kernel(parts_ref, hh_ref, hl_ref, th_ref, tl_ref, yh_ref, yl_ref, raw):
    @pl.loop(0, 16)
    def _(s):
        for c in range(3):
            for j in range(KB):
                for h in range(2):
                    raw[pl.ds(pl.multiple_of(NB * c + 16 * s, 16), 16), NB * j + HB * h : NB * j + HB * h + HB] = parts_ref[
                        s, j, c, pl.ds(h, 16, stride=2), :
                    ]
    solve_rows(raw, yh_ref, yl_ref, (hh_ref, hl_ref, th_ref, tl_ref))


ROWS_STEP = 2


def left_kernel(meta, parts_ref, hh_ref, hl_ref, th_ref, tl_ref, yh_ref, yl_ref, own_ref, raw):
    @pl.loop(0, 16)
    def _(s):
        for a in range(ROWS_STEP):
            for j in range(KB):
                for h in range(2):
                    raw[pl.ds(pl.multiple_of(NB * a + 16 * s, 16), 16), NB * j + HB * h : NB * j + HB * h + HB] = parts_ref[
                        s, j, a, pl.ds(h, 16, stride=2), :
                    ]
    solve_rows(raw, yh_ref, yl_ref, (hh_ref, hl_ref, th_ref, tl_ref))
    for j in range(KB):

        @pl.when(meta[33] == j)
        def _():
            own_ref[...] = raw[:, NB * j : NB * j + NB]


def schur_kernel(meta, yh, yl, own_ref, rh_ref, rl_ref, head_ref, tail_ref, parent_ref, child_0, child_1, child_2, out_ref):
    step = pl.program_id(0)
    row, col = meta[32], meta[33]
    routes = []
    for n in ROUTED:
        routes.append(routed_from(meta, n))

    for a in range(ROWS_STEP):
        slot = step * ROWS_STEP + a
        block_row = row + 8 * slot
        rows = slice(NB * a, NB * a + NB)
        for c in range(3):
            block_col = col + 16 * c

            def put(h, value):
                out_ref[pl.ds(1536 * a + 2 * c + h, NB, stride=6), :] = value

            @pl.when(jnp.logical_and(block_row >= KB, block_col >= KB))
            def _():
                cols = slice(NB * c, NB * c + NB)
                product = dot3(yh[rows, :], yl[rows, :], rh_ref[cols, :], rl_ref[cols, :], NT)
                for h in range(2):
                    put(h, parent_ref[pl.ds(1536 * a + 2 * c + h, NB, stride=6), :] - product[:, HB * h : HB * h + HB])
                turn = block_col % 3
                source = block_col // 3
                for n, (child, there, to) in enumerate(routes):
                    here = jnp.logical_and(there, to == slot)
                    here = jnp.logical_and(here, meta[child * 16 + source] == block_col)
                    for d, child_ref in enumerate((child_0, child_1, child_2)):

                        @pl.when(jnp.logical_and(here, turn == d))
                        def _():
                            for h in range(2):
                                at = pl.ds(1536 * a + 2 * c + h, NB, stride=6)
                                out_ref[at, :] = out_ref[at, :] + child_ref[n, pl.ds(h, NB, stride=2), :]

            @pl.when(jnp.logical_and(block_row < KB, block_col >= KB))
            def _():
                for h in range(2):
                    put(h, jnp.zeros((NB, HB), F32))

            if c == 0:

                @pl.when(jnp.logical_and(block_row >= KB, block_col < KB))
                def _():
                    for h in range(2):
                        put(h, own_ref[rows, HB * h : HB * h + HB])

                in_lead = jnp.logical_and(block_row < KB, block_col < KB)
                upper = block_row < block_col

                @pl.when(jnp.logical_and(in_lead, upper))
                def _():
                    for h in range(2):
                        put(h, jnp.zeros((NB, HB), F32))

                lower = jnp.logical_and(in_lead, jnp.logical_not(upper))

                @pl.when(jnp.logical_and(lower, block_col < CUT))
                def _():
                    block = head_ref[jnp.clip(packed(KB, block_col, block_row), 0, HEADS - 1)].T
                    for h in range(2):
                        put(h, block[:, HB * h : HB * h + HB])

                @pl.when(jnp.logical_and(lower, block_col >= CUT))
                def _():
                    at = jnp.clip(packed(REST, block_col - CUT, block_row - CUT), 0, TAILS - 1)
                    block = tail_ref[at].T
                    for h in range(2):
                        put(h, block[:, HB * h : HB * h + HB])


def cost(microseconds):
    return pl.CostEstimate(flops=int(microseconds * 1.1e9), bytes_accessed=1 << 20, transcendentals=0)


def call(kernel, out_shape, in_specs, scratch, microseconds=2):
    return pl.pallas_call(
        kernel,
        out_shape=out_shape,
        in_specs=in_specs,
        out_specs=jax.tree.map(lambda _: VM, out_shape),
        scratch_shapes=scratch,
        compiler_params=pltpu.CompilerParams(vmem_limit_bytes=VMEM_LIMIT),
        cost_estimate=cost(microseconds),
    )


def shaped(shape, dtype=F32):
    return jax.ShapeDtypeStruct(shape, dtype)


def per_device(parent, children, index_maps):
    row = lax.axis_index("prow")
    col = lax.axis_index("pcol")
    meta = jnp.concatenate([index_maps.reshape(-1), jnp.stack([row, col]).astype(jnp.int32)])
    front = parent.reshape(6, NB, 3, 2, LANES)
    lead = front[:, :, 0].reshape(6, 16, 32, LANES)
    child = children.reshape(4, 16, 32, LANES)

    child_id = row // 4
    twos = child.reshape(2, 2, 512, LANES)
    picked = [lax.dynamic_index_in_dim(twos, (child_id + flip) % 2, 1, keepdims=False) for flip in range(2)]

    first = jnp.stack([lead[0], child[0]], axis=1)
    first = lax.all_to_all(first, "pcol", 0, 0, tiled=True)
    mine = jnp.concatenate([first[0:KB, 0], first[0:2, 1]], axis=0)
    mine, *picked = lax.optimization_barrier((mine, *picked))
    shed = jnp.where(row == 0, mine[2:5], mine[3:6])
    got_a = lax.ppermute(shed, "prow", [(0, 6), (1, 5)])
    got_b = lax.ppermute(mine[1:2], "prow", [(0, 7)])
    chunk = call(chunk_kernel, shaped((3, 32, LANES)), [SM, VM, VM, VM], [])(meta, mine, got_a, got_b)
    chunk = lax.all_gather(chunk, "pcol")
    lead_parts = lax.all_gather(chunk, "prow")

    rest = jnp.concatenate([lead[1:], child], axis=0).transpose(1, 0, 2, 3)
    rest, chunk = lax.optimization_barrier((rest, chunk))
    rest = lax.all_to_all(rest, "pcol", 0, 0, tiled=True)
    pieces = call(pick_kernel, shaped((8, 2, 32, LANES)), [SM, VM], [])(meta, rest[0:2, 5:9])
    pieces = lax.all_to_all(pieces, "prow", 0, 0, tiled=True)
    slices = call(assemble_kernel, shaped((KB, 6, 32, LANES)), [SM, VM, VM, VM], [])(
        meta, mine[0:KB], rest[0:KB, 0:5], pieces
    )

    left_parts = lax.all_gather(slices, "pcol")

    lead_parts, slices, *picked = lax.optimization_barrier((lead_parts, slices, *picked))
    got = []
    for flip in range(2):
        perm = []
        for p in range(8):
            target = (3 * (p % 4) + 1 + 4 * ((p // 4 + flip) % 2)) % 8
            perm += [(p * 16 + q, target * 16 + (3 * q + 1) % 16) for q in range(1, 16)]
        got.append(lax.ppermute(picked[flip], ("prow", "pcol"), perm))
    even, odd = slices[:, 0::2], slices[:, 1::2]
    is_even = col % 2 == 0
    perm_a, perm_b = [], []
    for p in range(8):
        for s in range(16):
            perm_a.append((p * 16 + s, (s // 2) * 16 + p + 8 * (s % 2)))
            perm_b.append((p * 16 + s, (s // 2) * 16 + p + 8 * (1 - s % 2)))
    pair_a = lax.ppermute(jnp.where(is_even, even, odd), ("prow", "pcol"), perm_a)
    pair_b = lax.ppermute(jnp.where(is_even, odd, even), ("prow", "pcol"), perm_b)
    low_side = col < 8
    pair = jnp.stack([jnp.where(low_side, pair_a, pair_b), jnp.where(low_side, pair_b, pair_a)])

    scratch = [
        pltpu.VMEM((NB, NB), F32),
        pltpu.VMEM((HB, HB), F32),
        pltpu.VMEM((HB, HB), F32),
        pltpu.VMEM((HB, HB), F32),
    ]
    head_u, head_h, head_l, left_over = call(
        chain_head_kernel,
        (
            shaped((HEADS, NB, NB)),
            shaped((HEADS, NB, NB), BF16),
            shaped((HEADS, NB, NB), BF16),
            shaped((TAILS, NB, NB)),
        ),
        [SM, VM],
        [pltpu.VMEM((KB * KB, NB, NB), F32)] + scratch,
        32,
    )(meta, lead_parts)

    left_over, pair, *got = lax.optimization_barrier((left_over, pair, *got))

    residue = (3 * (row + 7)) % 4
    parity = ((row + 15 - 3 * residue) // 4) % 2
    chosen = {}
    for flip in range(2):
        block = 4 * parity + residue
        origin = meta[(parity + flip) % 2 * 16 + block] - 3 * block
        for d in range(3):
            which = jnp.where(origin == d, 0, 1)
            chosen[flip, d] = lax.dynamic_index_in_dim(got[flip], which, 0, keepdims=False)
    down = jnp.stack([chosen[0, 0], chosen[1, 0]])
    up = jnp.stack([chosen[0, 2], chosen[1, 2]])
    down = lax.ppermute(down, "prow", [(p, (p + 7) % 8) for p in range(8)])
    up = lax.ppermute(up, "prow", [(p, (p + 1) % 8) for p in range(8)])
    right_parts = lax.all_gather(pair, "prow").reshape(16, KB, 3, 32, LANES)
    tail_u, tail_h, tail_l = call(
        chain_tail_kernel,
        (shaped((TAILS, NB, NB)), shaped((TAILS, NB, NB), BF16), shaped((TAILS, NB, NB), BF16)),
        [VM],
        [pltpu.VMEM((REST * REST, NB, NB), F32)] + scratch,
        40,
    )(left_over)

    middle = jnp.concatenate([jnp.stack([chosen[0, 1], chosen[1, 1]]), down, up])
    middle, tail_h = lax.optimization_barrier((middle, tail_h))
    below = lax.ppermute(middle, "pcol", [(q, (q + 1) % 16) for q in range(16)])
    above = lax.ppermute(middle, "pcol", [(q, (q + 15) % 16) for q in range(16)])

    rh, rl = call(
        right_kernel,
        (shaped((768, 1280), BF16), shaped((768, 1280), BF16)),
        [VM] * 5,
        [pltpu.VMEM((768, 1280), F32)],
        12,
    )(right_parts, head_h, head_l, tail_h, tail_l)

    rows = NB * ROWS_STEP
    steps = 6 // ROWS_STEP
    whole_head = pl.BlockSpec((HEADS, NB, NB), lambda g: (0, 0, 0))
    whole_tail = pl.BlockSpec((TAILS, NB, NB), lambda g: (0, 0, 0))
    by_rows = pl.BlockSpec((rows, 1280), lambda g: (g, 0))
    own_rows = pl.BlockSpec((rows, NB), lambda g: (g, 0))
    yh, yl, own = pl.pallas_call(
        left_kernel,
        grid=(steps,),
        out_shape=(shaped((1536, 1280), BF16), shaped((1536, 1280), BF16), shaped((1536, NB))),
        in_specs=[
            SM,
            pl.BlockSpec((16, KB, ROWS_STEP, 32, LANES), lambda g: (0, 0, g, 0, 0)),
            whole_head,
            whole_head,
            whole_tail,
            whole_tail,
        ],
        out_specs=(by_rows, by_rows, own_rows),
        scratch_shapes=[pltpu.VMEM((rows, 1280), F32)],
        compiler_params=pltpu.CompilerParams(vmem_limit_bytes=VMEM_LIMIT),
        cost_estimate=cost(20),
    )(meta, left_parts, head_h, head_l, tail_h, tail_l)

    whole_right = pl.BlockSpec((768, 1280), lambda g: (0, 0))
    whole_child = pl.BlockSpec((6, 512, LANES), lambda g: (0, 0, 0))
    front_rows = pl.BlockSpec((1536 * ROWS_STEP, LANES), lambda g: (g, 0))
    out = pl.pallas_call(
        schur_kernel,
        grid=(steps,),
        out_shape=shaped((9216, LANES)),
        in_specs=[SM, by_rows, by_rows, own_rows, whole_right, whole_right, whole_head, whole_tail, front_rows]
        + [whole_child] * 3,
        out_specs=front_rows,
        compiler_params=pltpu.CompilerParams(vmem_limit_bytes=VMEM_LIMIT),
        cost_estimate=cost(18),
    )(
        meta,
        yh,
        yl,
        own,
        rh,
        rl,
        head_u,
        tail_u,
        parent.reshape(9216, LANES),
        *(x.reshape(6, 512, LANES) for x in (above, middle, below)),
    )
    return out.reshape(6, 1, NB, 3, 1, NB)


def solution(mesh):
    in_specs = (
        P(None, "prow", None, None, "pcol", None),
        P(None, "prow", None, None, "pcol", None),
        P(),
    )
    out_specs = P(None, "prow", None, None, "pcol", None)
    return jax.shard_map(
        per_device, mesh=mesh, in_specs=in_specs, out_specs=out_specs, check_vma=False
    )
```

```python
import jax
import jax.numpy as jnp
from jax import lax
from jax.experimental import pallas as pl
from jax.experimental.pallas import tpu as pltpu
from jax.sharding import PartitionSpec as P

KB = 5
NB = 256
HB = 128
LANES = 128
F32 = jnp.float32
BF16 = jnp.bfloat16
VMEM_LIMIT = 60 * 1024 * 1024
VM = pl.BlockSpec(memory_space=pltpu.VMEM)
SM = pl.BlockSpec(memory_space=pltpu.SMEM)


def route_of(meta, child, residue):
    there, slot = False, 0
    for turn in range(4):
        target = meta[child * 16 + 4 * turn + residue]
        here = target % 8 == meta[32]
        there = jnp.logical_or(there, here)
        slot = jnp.where(here, target // 8, slot)
    return there, slot


def turn_for(meta, target_row):
    child, residue = meta[32] // 4, meta[32] % 4
    chosen = 0
    for turn in range(1, 4):
        chosen = jnp.where(meta[child * 16 + 4 * turn + residue] % 8 == target_row, turn, chosen)
    return chosen


def routed_from(meta, n):
    flip, d = n // 3, n % 3
    row = meta[32]
    residue = (3 * (row + 8 - d)) % 4
    parity = ((row + 16 - 3 * residue - d) // 4) % 2
    child = (parity + flip) % 2
    first = 4 * parity + residue
    second = first + 8
    is_first = meta[child * 16 + first] == 3 * first + d
    is_second = meta[child * 16 + second] == 3 * second + d
    block = jnp.where(is_first, first, second)
    return child, jnp.logical_or(is_first, is_second), (3 * block + d) // 8


ROUTED = (1, 4, 0, 3, 2, 5)


def pick_kernel(meta, parts_ref, out_ref):
    for target_row in range(8):
        turn = turn_for(meta, target_row)
        for v in range(2):
            out_ref[target_row, v] = parts_ref[v, turn]


def assemble_kernel(meta, first_ref, rest_ref, got_ref, out_ref):
    for j in range(KB):
        out_ref[j, 0] = first_ref[j]
        out_ref[j, 1:6] = rest_ref[j]
    for child in range(2):
        for residue in range(4):
            there, slot = route_of(meta, child, residue)
            for v in range(2):
                column = meta[child * 16 + v]

                @pl.when(jnp.logical_and(there, column < KB))
                def _():
                    out_ref[column, slot] = out_ref[column, slot] + got_ref[4 * child + residue, v]


def chunk_kernel(meta, mine_ref, got_a_ref, got_b_ref, out_ref):
    for row, picks in enumerate(CHUNKS):

        @pl.when(meta[32] == row)
        def _():
            for at in range(3):
                kind, index = picks[at] if at < len(picks) else (0, 0)
                source = (mine_ref, got_a_ref, got_b_ref)[kind]
                out_ref[at] = source[index]


CHUNKS = [
    [(0, 0), (0, 5), (0, 6)],
    [(0, 1), (0, 2), (0, 6)],
    [(0, 2), (0, 3), (0, 4)],
    [(0, 3), (0, 4)],
    [(0, 4), (0, 5), (0, 6)],
    [(1, 0), (1, 1), (0, 6)],
    [(1, 0), (1, 1), (1, 2)],
    [(2, 0)],
]
UPPER_AT = {
    (0, 0): (0, 0),
    (0, 1): (7, 0),
    (0, 2): (6, 0),
    (0, 3): (6, 1),
    (0, 4): (6, 2),
    (1, 1): (1, 0),
    (1, 2): (1, 1),
    (1, 3): (5, 0),
    (1, 4): (5, 1),
    (2, 2): (2, 0),
    (2, 3): (2, 1),
    (2, 4): (2, 2),
    (3, 3): (3, 0),
    (3, 4): (3, 1),
    (4, 4): (4, 0),
}
CHILD_AT = {
    (0, 0, 0): (0, 1),
    (0, 0, 1): (0, 2),
    (0, 1, 1): (1, 2),
    (1, 0, 0): (4, 1),
    (1, 0, 1): (4, 2),
    (1, 1, 1): (5, 2),
}


def exact(a, b, dims):
    return lax.dot_general(a, b, (dims, ((), ())), precision=lax.Precision.HIGHEST, preferred_element_type=F32)


def dot3(ah, al, bh, bl, dims):
    def dot(a, b):
        return lax.dot_general(a, b, (dims, ((), ())), preferred_element_type=F32)

    return dot(ah, bh) + (dot(ah, bl) + dot(al, bh))


NN = ((1,), (0,))
NT = ((1,), (1,))
TN = ((0,), (0,))


def factor_128(a_ref, x_ref, u_ref):
    shape = (8, LANES)
    lane = lax.broadcasted_iota(jnp.int32, (HB, LANES), 1)
    sub = lax.broadcasted_iota(jnp.int32, (HB, LANES), 0)
    x_ref[...] = jnp.where(lane == sub, 1.0, 0.0).astype(F32)
    for g in range(HB // 8):
        rows = slice(8 * g, 8 * g + 8)
        a_g = a_ref[rows, :]
        x_g = x_ref[rows, :]
        cols = [jnp.broadcast_to(a_g[:, 8 * g + s : 8 * g + s + 1], shape) for s in range(8)]
        d = [[jnp.broadcast_to(cols[s][t : t + 1, :], shape) for s in range(t + 1)] for t in range(8)]
        low = [[None] * 8 for _ in range(8)]
        rinv = []
        for s in range(8):
            r = lax.rsqrt(d[s][s])
            rinv.append(r)
            for t in range(s + 1, 8):
                low[t][s] = d[t][s] * r
            for t in range(s + 1, 8):
                for t2 in range(s + 1, t + 1):
                    d[t][t2] = d[t][t2] - low[t][s] * low[t2][s]
        ub, xb = [], []
        for t in range(8):
            ua = jnp.broadcast_to(a_g[t : t + 1, :], shape)
            xa = jnp.broadcast_to(x_g[t : t + 1, :], shape)
            for s in range(t):
                ua = ua - low[t][s] * ub[s]
                xa = xa - low[t][s] * xb[s]
            ub.append(ua * rinv[t])
            xb.append(xa * rinv[t])
            u_ref[8 * g + t : 8 * g + t + 1, :] = ub[t][0:1, :]
            x_ref[8 * g + t : 8 * g + t + 1, :] = xb[t][0:1, :]
        for i in range(g + 1, HB // 8):
            rows_i = slice(8 * i, 8 * i + 8)
            a_i = a_ref[rows_i, :]
            x_i = x_ref[rows_i, :]
            w = []
            for t in range(8):
                wt = jnp.broadcast_to(a_i[:, 8 * g + t : 8 * g + t + 1], shape)
                for s in range(t):
                    wt = wt - low[t][s] * w[s]
                w.append(wt * rinv[t])
            for t in range(8):
                a_i = a_i - w[t] * ub[t]
                x_i = x_i - w[t] * xb[t]
            a_ref[rows_i, :] = a_i
            x_ref[rows_i, :] = x_i
    u_ref[...] = jnp.where(lane >= sub, u_ref[...], 0.0)


def split(a):
    high = a.astype(BF16)
    return high, (a - high.astype(F32)).astype(BF16)


CUT = 2
REST = KB - CUT


def place_head(k, i):
    if isinstance(i, int):
        return k + (i if i < CUT else 2 * i - 1)
    return k + jnp.where(i < CUT, i, 2 * i - 1)


def place_tail(k, i):
    return i * (i + 1) // 2 + k


HEADS = CUT * KB - 1
TAILS = REST * (REST + 1) // 2


def eliminate(n, steps, place, f_ref, u_ref, th_ref, tl_ref, v_ref, a_s, x_s, u_s):
    @pl.loop(0, 2 * steps)
    def _(step):
        k = step // 2
        half = step % 2
        kk = k * n + k
        pk = place(k, k)

        @pl.when(half == 0)
        def _():
            a_s[...] = f_ref[kk, 0:HB, 0:HB]

        @pl.when(half == 1)
        def _():
            u12 = exact(v_ref[0:HB, 0:HB], f_ref[kk, 0:HB, HB:NB], NN)
            u_ref[pk, 0:HB, HB:NB] = u12
            a_s[...] = f_ref[kk, HB:NB, HB:NB] - exact(u12, u12, TN)

        factor_128(a_s, x_s, u_s)

        @pl.when(half == 0)
        def _():
            u_ref[pk, 0:HB, 0:HB] = u_s[...]
            v_ref[0:HB, 0:HB] = x_s[...]

        @pl.when(half == 1)
        def _():
            u_ref[pk, HB:NB, HB:NB] = u_s[...]
            u_ref[pk, HB:NB, 0:HB] = jnp.zeros((HB, HB), F32)
            v_ref[HB:NB, HB:NB] = x_s[...]
            v_ref[0:HB, HB:NB] = jnp.zeros((HB, HB), F32)
            lx = exact(u_ref[pk, 0:HB, HB:NB], v_ref[0:HB, 0:HB], TN)
            v_ref[HB:NB, 0:HB] = -exact(x_s[...], lx, NN)
            high, low = split(v_ref[...].T)
            th_ref[pk] = high
            tl_ref[pk] = low
            vh, vl = split(v_ref[...])

            @pl.loop(k + 1, n)
            def _(i):
                u = dot3(vh, vl, *split(f_ref[k * n + i]), NN)
                at = place(k, i)
                u_ref[at] = u
                high, low = split(u)
                th_ref[at] = high
                tl_ref[at] = low

            @pl.loop(k + 1, n)
            def _(i):
                at_i = place(k, i)

                @pl.loop(i, n)
                def _(j):
                    at_j = place(k, j)
                    f_ref[i * n + j] = f_ref[i * n + j] - dot3(
                        th_ref[at_i], tl_ref[at_i], th_ref[at_j], tl_ref[at_j], TN
                    )


def chain_head_kernel(meta, parts_ref, u_ref, th_ref, tl_ref, rest_ref, f_ref, *scratch):
    def take(at, s, h):
        return parts_ref[at[0], s, at[1], pl.ds(h, 16, stride=2), :]

    for (k, i), at in UPPER_AT.items():
        for s in range(16):
            for h in range(2):
                f_ref[k * KB + i, 16 * s : 16 * s + 16, HB * h : HB * h + HB] = take(at, s, h)
    for (c, u, v), at in CHILD_AT.items():
        k = meta[c * 16 + u]
        i = meta[c * 16 + v]

        @pl.when(jnp.logical_and(k < KB, i < KB))
        def _():
            for s in range(16):
                for h in range(2):
                    place = (k * KB + i, slice(16 * s, 16 * s + 16), slice(HB * h, HB * h + HB))
                    f_ref[place] = f_ref[place] + take(at, s, h)

    eliminate(KB, CUT, place_head, f_ref, u_ref, th_ref, tl_ref, *scratch)
    for i in range(REST):
        for j in range(i, REST):
            rest_ref[place_tail(i, j)] = f_ref[(CUT + i) * KB + CUT + j]


def chain_tail_kernel(rest_ref, u_ref, th_ref, tl_ref, f_ref, *scratch):
    for i in range(REST):
        for j in range(i, REST):
            f_ref[i * REST + j] = rest_ref[place_tail(i, j)]
    eliminate(REST, REST, place_tail, f_ref, u_ref, th_ref, tl_ref, *scratch)


def solve_rows(raw_ref, yh_ref, yl_ref, factors):
    head_h, head_l, tail_h, tail_l = factors

    def column(high, low, start, count):
        return [ref[start : start + count].reshape(count * NB, NB) for ref in (high, low)]

    for k in range(KB):
        at = slice(NB * k, NB * k + NB)
        t = raw_ref[:, at]
        if k > 0:
            count = min(k, CUT)
            before = slice(0, NB * count)
            part = column(head_h, head_l, place_head(0, k), count)
            t = t - dot3(yh_ref[:, before], yl_ref[:, before], *part, NN)
        if k > CUT:
            before = slice(NB * CUT, NB * k)
            part = column(tail_h, tail_l, place_tail(0, k - CUT), k - CUT)
            t = t - dot3(yh_ref[:, before], yl_ref[:, before], *part, NN)
        high, low = split(t)
        if k < CUT:
            own = column(head_h, head_l, place_head(k, k), 1)
        else:
            own = column(tail_h, tail_l, place_tail(k - CUT, k - CUT), 1)
        y = dot3(high, low, *own, NN)
        raw_ref[:, at] = y
        high, low = split(y)
        yh_ref[:, at] = high
        yl_ref[:, at] = low


def right_kernel(parts_ref, hh_ref, hl_ref, th_ref, tl_ref, yh_ref, yl_ref, raw):
    @pl.loop(0, 16)
    def _(s):
        for c in range(3):
            for j in range(KB):
                for h in range(2):
                    raw[pl.ds(pl.multiple_of(NB * c + 16 * s, 16), 16), NB * j + HB * h : NB * j + HB * h + HB] = parts_ref[
                        s, j, c, pl.ds(h, 16, stride=2), :
                    ]
    solve_rows(raw, yh_ref, yl_ref, (hh_ref, hl_ref, th_ref, tl_ref))


ROWS_STEP = 2


def left_kernel(meta, parts_ref, hh_ref, hl_ref, th_ref, tl_ref, yh_ref, yl_ref, own_ref, raw):
    @pl.loop(0, 16)
    def _(s):
        for a in range(ROWS_STEP):
            for j in range(KB):
                for h in range(2):
                    raw[pl.ds(pl.multiple_of(NB * a + 16 * s, 16), 16), NB * j + HB * h : NB * j + HB * h + HB] = parts_ref[
                        s, j, a, pl.ds(h, 16, stride=2), :
                    ]
    solve_rows(raw, yh_ref, yl_ref, (hh_ref, hl_ref, th_ref, tl_ref))
    for j in range(KB):

        @pl.when(meta[33] == j)
        def _():
            own_ref[...] = raw[:, NB * j : NB * j + NB]


def schur_kernel(meta, yh, yl, own_ref, rh_ref, rl_ref, head_ref, tail_ref, parent_ref, child_0, child_1, child_2, out_ref):
    step = pl.program_id(0)
    row, col = meta[32], meta[33]
    routes = []
    for n in ROUTED:
        routes.append(routed_from(meta, n))

    for a in range(ROWS_STEP):
        slot = step * ROWS_STEP + a
        block_row = row + 8 * slot
        rows = slice(NB * a, NB * a + NB)
        for c in range(3):
            block_col = col + 16 * c

            def put(h, value):
                out_ref[pl.ds(1536 * a + 2 * c + h, NB, stride=6), :] = value

            @pl.when(jnp.logical_and(block_row >= KB, block_col >= KB))
            def _():
                cols = slice(NB * c, NB * c + NB)
                product = dot3(yh[rows, :], yl[rows, :], rh_ref[cols, :], rl_ref[cols, :], NT)
                for h in range(2):
                    put(h, parent_ref[pl.ds(1536 * a + 2 * c + h, NB, stride=6), :] - product[:, HB * h : HB * h + HB])
                turn = block_col % 3
                source = block_col // 3
                for n, (child, there, to) in enumerate(routes):
                    here = jnp.logical_and(there, to == slot)
                    here = jnp.logical_and(here, meta[child * 16 + source] == block_col)
                    for d, child_ref in enumerate((child_0, child_1, child_2)):

                        @pl.when(jnp.logical_and(here, turn == d))
                        def _():
                            for h in range(2):
                                at = pl.ds(1536 * a + 2 * c + h, NB, stride=6)
                                out_ref[at, :] = out_ref[at, :] + child_ref[n, pl.ds(h, NB, stride=2), :]

            @pl.when(jnp.logical_and(block_row < KB, block_col >= KB))
            def _():
                for h in range(2):
                    put(h, jnp.zeros((NB, HB), F32))

            if c == 0:

                @pl.when(jnp.logical_and(block_row >= KB, block_col < KB))
                def _():
                    for h in range(2):
                        put(h, own_ref[rows, HB * h : HB * h + HB])

                in_lead = jnp.logical_and(block_row < KB, block_col < KB)
                upper = block_row < block_col

                @pl.when(jnp.logical_and(in_lead, upper))
                def _():
                    for h in range(2):
                        put(h, jnp.zeros((NB, HB), F32))

                lower = jnp.logical_and(in_lead, jnp.logical_not(upper))

                @pl.when(jnp.logical_and(lower, block_col < CUT))
                def _():
                    block = head_ref[jnp.clip(place_head(block_col, block_row), 0, HEADS - 1)].T
                    for h in range(2):
                        put(h, block[:, HB * h : HB * h + HB])

                @pl.when(jnp.logical_and(lower, block_col >= CUT))
                def _():
                    at = jnp.clip(place_tail(block_col - CUT, block_row - CUT), 0, TAILS - 1)
                    block = tail_ref[at].T
                    for h in range(2):
                        put(h, block[:, HB * h : HB * h + HB])


def cost(microseconds):
    return pl.CostEstimate(flops=int(microseconds * 1.1e9), bytes_accessed=1 << 20, transcendentals=0)


def call(kernel, out_shape, in_specs, scratch, microseconds=2):
    return pl.pallas_call(
        kernel,
        out_shape=out_shape,
        in_specs=in_specs,
        out_specs=jax.tree.map(lambda _: VM, out_shape),
        scratch_shapes=scratch,
        compiler_params=pltpu.CompilerParams(vmem_limit_bytes=VMEM_LIMIT),
        cost_estimate=cost(microseconds),
    )


def shaped(shape, dtype=F32):
    return jax.ShapeDtypeStruct(shape, dtype)


def per_device(parent, children, index_maps):
    row = lax.axis_index("prow")
    col = lax.axis_index("pcol")
    meta = jnp.concatenate([index_maps.reshape(-1), jnp.stack([row, col]).astype(jnp.int32)])
    front = parent.reshape(6, NB, 3, 2, LANES)
    lead = front[:, :, 0].reshape(6, 16, 32, LANES)
    child = children.reshape(4, 16, 32, LANES)

    child_id = row // 4
    twos = child.reshape(2, 2, 512, LANES)
    picked = [lax.dynamic_index_in_dim(twos, (child_id + flip) % 2, 1, keepdims=False) for flip in range(2)]

    first = jnp.stack([lead[0], child[0]], axis=1)
    first = lax.all_to_all(first, "pcol", 0, 0, tiled=True)
    mine = jnp.concatenate([first[0:KB, 0], first[0:2, 1]], axis=0)
    mine, *picked = lax.optimization_barrier((mine, *picked))
    shed = jnp.where(row == 0, mine[2:5], mine[3:6])
    got_a = lax.ppermute(shed, "prow", [(0, 6), (1, 5)])
    got_b = lax.ppermute(mine[1:2], "prow", [(0, 7)])
    chunk = call(chunk_kernel, shaped((3, 32, LANES)), [SM, VM, VM, VM], [])(meta, mine, got_a, got_b)
    chunk = lax.all_gather(chunk, "pcol")
    lead_parts = lax.all_gather(chunk, "prow")

    rest = jnp.concatenate([lead[1:], child], axis=0).transpose(1, 0, 2, 3)
    rest, chunk = lax.optimization_barrier((rest, chunk))
    rest = lax.all_to_all(rest, "pcol", 0, 0, tiled=True)
    pieces = call(pick_kernel, shaped((8, 2, 32, LANES)), [SM, VM], [])(meta, rest[0:2, 5:9])
    pieces, *picked = lax.optimization_barrier((pieces, *picked))
    pieces = lax.all_to_all(pieces, "prow", 0, 0, tiled=True)

    got = []
    for flip in range(2):
        perm = []
        for p in range(8):
            target = (3 * (p % 4) + 1 + 4 * ((p // 4 + flip) % 2)) % 8
            perm += [(p * 16 + q, target * 16 + (3 * q + 1) % 16) for q in range(1, 16)]
        got.append(lax.ppermute(picked[flip], ("prow", "pcol"), perm))
    pieces, *got = lax.optimization_barrier((pieces, *got))
    slices = call(assemble_kernel, shaped((KB, 6, 32, LANES)), [SM, VM, VM, VM], [])(
        meta, mine[0:KB], rest[0:KB, 0:5], pieces
    )

    left_parts = lax.all_gather(slices, "pcol")

    lead_parts, slices, *got = lax.optimization_barrier((lead_parts, slices, *got))

    residue = (3 * (row + 7)) % 4
    parity = ((row + 15 - 3 * residue) // 4) % 2
    chosen = {}
    for flip in range(2):
        block = 4 * parity + residue
        origin = meta[(parity + flip) % 2 * 16 + block] - 3 * block
        for d in range(3):
            which = jnp.where(origin == d, 0, 1)
            chosen[flip, d] = lax.dynamic_index_in_dim(got[flip], which, 0, keepdims=False)
    down = jnp.stack([chosen[0, 0], chosen[1, 0]])
    up = jnp.stack([chosen[0, 2], chosen[1, 2]])
    down = lax.ppermute(down, "prow", [(p, (p + 7) % 8) for p in range(8)])
    up = lax.ppermute(up, "prow", [(p, (p + 1) % 8) for p in range(8)])
    even, odd = slices[:, 0::2], slices[:, 1::2]
    is_even = col % 2 == 0
    perm_a, perm_b = [], []
    for p in range(8):
        for s in range(16):
            perm_a.append((p * 16 + s, (s // 2) * 16 + p + 8 * (s % 2)))
            perm_b.append((p * 16 + s, (s // 2) * 16 + p + 8 * (1 - s % 2)))
    pair_a = lax.ppermute(jnp.where(is_even, even, odd), ("prow", "pcol"), perm_a)
    pair_b = lax.ppermute(jnp.where(is_even, odd, even), ("prow", "pcol"), perm_b)
    low_side = col < 8
    pair = jnp.stack([jnp.where(low_side, pair_a, pair_b), jnp.where(low_side, pair_b, pair_a)])
    pairs = jnp.broadcast_to(pair[None], (8,) + pair.shape)

    scratch = [
        pltpu.VMEM((NB, NB), F32),
        pltpu.VMEM((HB, HB), F32),
        pltpu.VMEM((HB, HB), F32),
        pltpu.VMEM((HB, HB), F32),
    ]
    head_u, head_h, head_l, left_over = call(
        chain_head_kernel,
        (
            shaped((HEADS, NB, NB)),
            shaped((HEADS, NB, NB), BF16),
            shaped((HEADS, NB, NB), BF16),
            shaped((TAILS, NB, NB)),
        ),
        [SM, VM],
        [pltpu.VMEM((KB * KB, NB, NB), F32)] + scratch,
        32,
    )(meta, lead_parts)

    left_over, pairs, down, up = lax.optimization_barrier((left_over, pairs, down, up))
    right_parts = lax.all_to_all(pairs, "prow", 0, 0, tiled=True).reshape(16, KB, 3, 32, LANES)
    tail_u, tail_h, tail_l = call(
        chain_tail_kernel,
        (shaped((TAILS, NB, NB)), shaped((TAILS, NB, NB), BF16), shaped((TAILS, NB, NB), BF16)),
        [VM],
        [pltpu.VMEM((REST * REST, NB, NB), F32)] + scratch,
        40,
    )(left_over)

    middle = jnp.concatenate([jnp.stack([chosen[0, 1], chosen[1, 1]]), down, up])
    middle, tail_h = lax.optimization_barrier((middle, tail_h))
    below = lax.ppermute(middle, "pcol", [(q, (q + 1) % 16) for q in range(16)])
    above = lax.ppermute(middle, "pcol", [(q, (q + 15) % 16) for q in range(16)])

    rows = NB * ROWS_STEP
    steps = 6 // ROWS_STEP
    whole_head = pl.BlockSpec((HEADS, NB, NB), lambda g: (0, 0, 0))
    whole_tail = pl.BlockSpec((TAILS, NB, NB), lambda g: (0, 0, 0))
    by_rows = pl.BlockSpec((rows, 1280), lambda g: (g, 0))
    own_rows = pl.BlockSpec((rows, NB), lambda g: (g, 0))
    yh, yl, own = pl.pallas_call(
        left_kernel,
        grid=(steps,),
        out_shape=(shaped((1536, 1280), BF16), shaped((1536, 1280), BF16), shaped((1536, NB))),
        in_specs=[
            SM,
            pl.BlockSpec((16, KB, ROWS_STEP, 32, LANES), lambda g: (0, 0, g, 0, 0)),
            whole_head,
            whole_head,
            whole_tail,
            whole_tail,
        ],
        out_specs=(by_rows, by_rows, own_rows),
        scratch_shapes=[pltpu.VMEM((rows, 1280), F32)],
        compiler_params=pltpu.CompilerParams(vmem_limit_bytes=VMEM_LIMIT),
        cost_estimate=cost(20),
    )(meta, left_parts, head_h, head_l, tail_h, tail_l)

    right_parts, own = lax.optimization_barrier((right_parts, own))
    rh, rl = call(
        right_kernel,
        (shaped((768, 1280), BF16), shaped((768, 1280), BF16)),
        [VM] * 5,
        [pltpu.VMEM((768, 1280), F32)],
        12,
    )(right_parts, head_h, head_l, tail_h, tail_l)

    whole_right = pl.BlockSpec((768, 1280), lambda g: (0, 0))
    whole_child = pl.BlockSpec((6, 512, LANES), lambda g: (0, 0, 0))
    front_rows = pl.BlockSpec((1536 * ROWS_STEP, LANES), lambda g: (g, 0))
    out = pl.pallas_call(
        schur_kernel,
        grid=(steps,),
        out_shape=shaped((9216, LANES)),
        in_specs=[SM, by_rows, by_rows, own_rows, whole_right, whole_right, whole_head, whole_tail, front_rows]
        + [whole_child] * 3,
        out_specs=front_rows,
        compiler_params=pltpu.CompilerParams(vmem_limit_bytes=VMEM_LIMIT),
        cost_estimate=cost(18),
    )(
        meta,
        yh,
        yl,
        own,
        rh,
        rl,
        head_u,
        tail_u,
        parent.reshape(9216, LANES),
        *(x.reshape(6, 512, LANES) for x in (above, middle, below)),
    )
    return out.reshape(6, 1, NB, 3, 1, NB)


def solution(mesh):
    in_specs = (
        P(None, "prow", None, None, "pcol", None),
        P(None, "prow", None, None, "pcol", None),
        P(),
    )
    out_specs = P(None, "prow", None, None, "pcol", None)
    return jax.shard_map(
        per_device, mesh=mesh, in_specs=in_specs, out_specs=out_specs, check_vma=False
    )
```

```python
import jax
import jax.numpy as jnp
from jax import lax
from jax.experimental import pallas as pl
from jax.experimental.pallas import tpu as pltpu
from jax.sharding import PartitionSpec as P

KB = 5
NB = 256
HB = 128
LANES = 128
F32 = jnp.float32
BF16 = jnp.bfloat16
VMEM_LIMIT = 60 * 1024 * 1024
VM = pl.BlockSpec(memory_space=pltpu.VMEM)
SM = pl.BlockSpec(memory_space=pltpu.SMEM)


def route_of(meta, child, residue):
    there, slot = False, 0
    for turn in range(4):
        target = meta[child * 16 + 4 * turn + residue]
        here = target % 8 == meta[32]
        there = jnp.logical_or(there, here)
        slot = jnp.where(here, target // 8, slot)
    return there, slot


def turn_for(meta, target_row):
    child, residue = meta[32] // 4, meta[32] % 4
    chosen = 0
    for turn in range(1, 4):
        chosen = jnp.where(meta[child * 16 + 4 * turn + residue] % 8 == target_row, turn, chosen)
    return chosen


def routed_from(meta, n):
    flip, d = n // 3, n % 3
    row = meta[32]
    residue = (3 * (row + 8 - d)) % 4
    parity = ((row + 16 - 3 * residue - d) // 4) % 2
    child = (parity + flip) % 2
    first = 4 * parity + residue
    second = first + 8
    is_first = meta[child * 16 + first] == 3 * first + d
    is_second = meta[child * 16 + second] == 3 * second + d
    block = jnp.where(is_first, first, second)
    return child, jnp.logical_or(is_first, is_second), (3 * block + d) // 8


ROUTED = (1, 4, 0, 3, 2, 5)


def pick_kernel(meta, parts_ref, out_ref):
    for target_row in range(8):
        turn = turn_for(meta, target_row)
        for v in range(2):
            out_ref[target_row, v] = parts_ref[v, turn]


def assemble_kernel(meta, first_ref, rest_ref, got_ref, out_ref):
    for j in range(KB):
        out_ref[j, 0] = first_ref[j]
        out_ref[j, 1:6] = rest_ref[j]
    for child in range(2):
        for residue in range(4):
            there, slot = route_of(meta, child, residue)
            for v in range(2):
                column = meta[child * 16 + v]

                @pl.when(jnp.logical_and(there, column < KB))
                def _():
                    out_ref[column, slot] = out_ref[column, slot] + got_ref[4 * child + residue, v]


def chunk_kernel(meta, mine_ref, got_a_ref, got_b_ref, out_ref):
    for row, picks in enumerate(CHUNKS):

        @pl.when(meta[32] == row)
        def _():
            for at in range(3):
                kind, index = picks[at] if at < len(picks) else (0, 0)
                source = (mine_ref, got_a_ref, got_b_ref)[kind]
                out_ref[at] = source[index]


CHUNKS = [
    [(0, 0), (0, 5), (0, 6)],
    [(0, 1), (0, 2), (0, 6)],
    [(0, 2), (0, 3), (0, 4)],
    [(0, 3), (0, 4)],
    [(0, 4), (0, 5), (0, 6)],
    [(1, 0), (1, 1), (0, 6)],
    [(1, 0), (1, 1), (1, 2)],
    [(2, 0)],
]
UPPER_AT = {
    (0, 0): (0, 0),
    (0, 1): (7, 0),
    (0, 2): (6, 0),
    (0, 3): (6, 1),
    (0, 4): (6, 2),
    (1, 1): (1, 0),
    (1, 2): (1, 1),
    (1, 3): (5, 0),
    (1, 4): (5, 1),
    (2, 2): (2, 0),
    (2, 3): (2, 1),
    (2, 4): (2, 2),
    (3, 3): (3, 0),
    (3, 4): (3, 1),
    (4, 4): (4, 0),
}
CHILD_AT = {
    (0, 0, 0): (0, 1),
    (0, 0, 1): (0, 2),
    (0, 1, 1): (1, 2),
    (1, 0, 0): (4, 1),
    (1, 0, 1): (4, 2),
    (1, 1, 1): (5, 2),
}


def exact(a, b, dims):
    return lax.dot_general(a, b, (dims, ((), ())), precision=lax.Precision.HIGHEST, preferred_element_type=F32)


def dot3(ah, al, bh, bl, dims):
    def dot(a, b):
        return lax.dot_general(a, b, (dims, ((), ())), preferred_element_type=F32)

    return dot(ah, bh) + (dot(ah, bl) + dot(al, bh))


NN = ((1,), (0,))
NT = ((1,), (1,))
TN = ((0,), (0,))


def factor_128(a_ref, x_ref, u_ref):
    shape = (8, LANES)
    lane = lax.broadcasted_iota(jnp.int32, (HB, LANES), 1)
    sub = lax.broadcasted_iota(jnp.int32, (HB, LANES), 0)
    x_ref[...] = jnp.where(lane == sub, 1.0, 0.0).astype(F32)
    for g in range(HB // 8):
        rows = slice(8 * g, 8 * g + 8)
        a_g = a_ref[rows, :]
        x_g = x_ref[rows, :]
        cols = [jnp.broadcast_to(a_g[:, 8 * g + s : 8 * g + s + 1], shape) for s in range(8)]
        d = [[jnp.broadcast_to(cols[s][t : t + 1, :], shape) for s in range(t + 1)] for t in range(8)]
        low = [[None] * 8 for _ in range(8)]
        rinv = []
        for s in range(8):
            r = lax.rsqrt(d[s][s])
            rinv.append(r)
            for t in range(s + 1, 8):
                low[t][s] = d[t][s] * r
            for t in range(s + 1, 8):
                for t2 in range(s + 1, t + 1):
                    d[t][t2] = d[t][t2] - low[t][s] * low[t2][s]
        ub, xb = [], []
        for t in range(8):
            ua = jnp.broadcast_to(a_g[t : t + 1, :], shape)
            xa = jnp.broadcast_to(x_g[t : t + 1, :], shape)
            for s in range(t):
                ua = ua - low[t][s] * ub[s]
                xa = xa - low[t][s] * xb[s]
            ub.append(ua * rinv[t])
            xb.append(xa * rinv[t])
            u_ref[8 * g + t : 8 * g + t + 1, :] = ub[t][0:1, :]
            x_ref[8 * g + t : 8 * g + t + 1, :] = xb[t][0:1, :]
        for i in range(g + 1, HB // 8):
            rows_i = slice(8 * i, 8 * i + 8)
            a_i = a_ref[rows_i, :]
            x_i = x_ref[rows_i, :]
            w = []
            for t in range(8):
                wt = jnp.broadcast_to(a_i[:, 8 * g + t : 8 * g + t + 1], shape)
                for s in range(t):
                    wt = wt - low[t][s] * w[s]
                w.append(wt * rinv[t])
            for t in range(8):
                a_i = a_i - w[t] * ub[t]
                x_i = x_i - w[t] * xb[t]
            a_ref[rows_i, :] = a_i
            x_ref[rows_i, :] = x_i
    u_ref[...] = jnp.where(lane >= sub, u_ref[...], 0.0)


def split(a):
    high = a.astype(BF16)
    return high, (a - high.astype(F32)).astype(BF16)


STAGES = ((0, 1), (1, 2), (3, 2))


def place(n, k, i):
    return k * (2 * n + 1 - k) // 2 + i - k


def sizes(stage):
    start, steps = STAGES[stage]
    n = KB - start
    rest = n - steps
    return n, place(n, steps, steps), rest * (rest + 1) // 2


def eliminate(n, steps, f_ref, u_ref, th_ref, tl_ref, v_ref, a_s, x_s, u_s):
    @pl.loop(0, 2 * steps)
    def _(step):
        k = step // 2
        half = step % 2
        kk = k * n + k
        pk = place(n, k, k)

        @pl.when(half == 0)
        def _():
            a_s[...] = f_ref[kk, 0:HB, 0:HB]

        @pl.when(half == 1)
        def _():
            u12 = exact(v_ref[0:HB, 0:HB], f_ref[kk, 0:HB, HB:NB], NN)
            u_ref[pk, 0:HB, HB:NB] = u12
            a_s[...] = f_ref[kk, HB:NB, HB:NB] - exact(u12, u12, TN)

        factor_128(a_s, x_s, u_s)

        @pl.when(half == 0)
        def _():
            u_ref[pk, 0:HB, 0:HB] = u_s[...]
            v_ref[0:HB, 0:HB] = x_s[...]

        @pl.when(half == 1)
        def _():
            u_ref[pk, HB:NB, HB:NB] = u_s[...]
            u_ref[pk, HB:NB, 0:HB] = jnp.zeros((HB, HB), F32)
            v_ref[HB:NB, HB:NB] = x_s[...]
            v_ref[0:HB, HB:NB] = jnp.zeros((HB, HB), F32)
            lx = exact(u_ref[pk, 0:HB, HB:NB], v_ref[0:HB, 0:HB], TN)
            v_ref[HB:NB, 0:HB] = -exact(x_s[...], lx, NN)
            high, low = split(v_ref[...].T)
            th_ref[pk] = high
            tl_ref[pk] = low
            vh, vl = split(v_ref[...])

            @pl.loop(k + 1, n)
            def _(i):
                u = dot3(vh, vl, *split(f_ref[k * n + i]), NN)
                at = place(n, k, i)
                u_ref[at] = u
                high, low = split(u)
                th_ref[at] = high
                tl_ref[at] = low

            @pl.loop(k + 1, n)
            def _(i):
                at_i = place(n, k, i)

                @pl.loop(i, n)
                def _(j):
                    at_j = place(n, k, j)
                    f_ref[i * n + j] = f_ref[i * n + j] - dot3(
                        th_ref[at_i], tl_ref[at_i], th_ref[at_j], tl_ref[at_j], TN
                    )


def hand_on(n, steps, f_ref, rest_ref):
    for i in range(n - steps):
        for j in range(i, n - steps):
            rest_ref[place(n - steps, i, j)] = f_ref[(steps + i) * n + steps + j]


def chain_first_kernel(meta, parts_ref, u_ref, th_ref, tl_ref, rest_ref, f_ref, *scratch):
    def take(at, s, h):
        return parts_ref[at[0], s, at[1], pl.ds(h, 16, stride=2), :]

    for (k, i), at in UPPER_AT.items():
        for s in range(16):
            for h in range(2):
                f_ref[k * KB + i, 16 * s : 16 * s + 16, HB * h : HB * h + HB] = take(at, s, h)
    for (c, u, v), at in CHILD_AT.items():
        k = meta[c * 16 + u]
        i = meta[c * 16 + v]

        @pl.when(jnp.logical_and(k < KB, i < KB))
        def _():
            for s in range(16):
                for h in range(2):
                    place_of = (k * KB + i, slice(16 * s, 16 * s + 16), slice(HB * h, HB * h + HB))
                    f_ref[place_of] = f_ref[place_of] + take(at, s, h)

    steps = STAGES[0][1]
    eliminate(KB, steps, f_ref, u_ref, th_ref, tl_ref, *scratch)
    hand_on(KB, steps, f_ref, rest_ref)


def chain_next_kernel(stage, left_ref, u_ref, th_ref, tl_ref, *refs):
    n, _, rest = sizes(stage)
    steps = STAGES[stage][1]
    rest_ref, (f_ref, *scratch) = (refs[0], refs[1:]) if rest else (None, refs)
    for i in range(n):
        for j in range(i, n):
            f_ref[i * n + j] = left_ref[place(n, i, j)]
    eliminate(n, steps, f_ref, u_ref, th_ref, tl_ref, *scratch)
    if rest:
        hand_on(n, steps, f_ref, rest_ref)


def stage_of(k):
    return sum(1 for start, _ in STAGES if start <= k) - 1


def solve_rows(raw_ref, yh_ref, yl_ref, factors):
    def factor(m, k):
        stage = stage_of(m)
        start = STAGES[stage][0]
        at = place(KB - start, m - start, k - start)
        return factors[2 * stage][at], factors[2 * stage + 1][at]

    for k in range(KB):
        at = slice(NB * k, NB * k + NB)
        t = raw_ref[:, at]
        for m in range(k):
            am = slice(NB * m, NB * m + NB)
            t = t - dot3(yh_ref[:, am], yl_ref[:, am], *factor(m, k), NN)
        high, low = split(t)
        y = dot3(high, low, *factor(k, k), NN)
        raw_ref[:, at] = y
        high, low = split(y)
        yh_ref[:, at] = high
        yl_ref[:, at] = low


def right_kernel(parts_ref, *refs):
    *factors, yh_ref, yl_ref, raw = refs

    @pl.loop(0, 16)
    def _(s):
        for c in range(3):
            for j in range(KB):
                for h in range(2):
                    raw[pl.ds(pl.multiple_of(NB * c + 16 * s, 16), 16), NB * j + HB * h : NB * j + HB * h + HB] = parts_ref[
                        s, j, c, pl.ds(h, 16, stride=2), :
                    ]
    solve_rows(raw, yh_ref, yl_ref, factors)


ROWS_STEP = 2


def left_kernel(meta, parts_ref, *refs):
    *factors, yh_ref, yl_ref, own_ref, raw = refs

    @pl.loop(0, 16)
    def _(s):
        for a in range(ROWS_STEP):
            for j in range(KB):
                for h in range(2):
                    raw[pl.ds(pl.multiple_of(NB * a + 16 * s, 16), 16), NB * j + HB * h : NB * j + HB * h + HB] = parts_ref[
                        s, j, a, pl.ds(h, 16, stride=2), :
                    ]
    solve_rows(raw, yh_ref, yl_ref, factors)
    for j in range(KB):

        @pl.when(meta[33] == j)
        def _():
            own_ref[...] = raw[:, NB * j : NB * j + NB]


SCHUR_STEP = 1


def schur_kernel(meta, yh, yl, own_ref, rh_ref, rl_ref, u_0, u_1, u_2, parent_ref, child_0, child_1, child_2, out_ref):
    step = pl.program_id(0)
    row, col = meta[32], meta[33]
    routes = []
    for n in ROUTED:
        routes.append(routed_from(meta, n))

    for a in range(SCHUR_STEP):
        slot = step * SCHUR_STEP + a
        block_row = row + 8 * slot
        rows = slice(NB * a, NB * a + NB)
        for c in range(3):
            block_col = col + 16 * c

            def put(h, value):
                out_ref[pl.ds(1536 * a + 2 * c + h, NB, stride=6), :] = value

            @pl.when(jnp.logical_and(block_row >= KB, block_col >= KB))
            def _():
                cols = slice(NB * c, NB * c + NB)
                product = dot3(yh[rows, :], yl[rows, :], rh_ref[cols, :], rl_ref[cols, :], NT)
                for h in range(2):
                    put(h, parent_ref[pl.ds(1536 * a + 2 * c + h, NB, stride=6), :] - product[:, HB * h : HB * h + HB])
                turn = block_col % 3
                source = block_col // 3
                for n, (child, there, to) in enumerate(routes):
                    here = jnp.logical_and(there, to == slot)
                    here = jnp.logical_and(here, meta[child * 16 + source] == block_col)
                    for d, child_ref in enumerate((child_0, child_1, child_2)):

                        @pl.when(jnp.logical_and(here, turn == d))
                        def _():
                            for h in range(2):
                                at = pl.ds(1536 * a + 2 * c + h, NB, stride=6)
                                out_ref[at, :] = out_ref[at, :] + child_ref[n, pl.ds(h, NB, stride=2), :]

            @pl.when(jnp.logical_and(block_row < KB, block_col >= KB))
            def _():
                for h in range(2):
                    put(h, jnp.zeros((NB, HB), F32))

            if c == 0:

                @pl.when(jnp.logical_and(block_row >= KB, block_col < KB))
                def _():
                    for h in range(2):
                        put(h, own_ref[rows, HB * h : HB * h + HB])

                in_lead = jnp.logical_and(block_row < KB, block_col < KB)
                upper = block_row < block_col

                @pl.when(jnp.logical_and(in_lead, upper))
                def _():
                    for h in range(2):
                        put(h, jnp.zeros((NB, HB), F32))

                lower = jnp.logical_and(in_lead, jnp.logical_not(upper))
                for stage, u_ref in enumerate((u_0, u_1, u_2)):
                    start, steps = STAGES[stage]
                    inside = jnp.logical_and(block_col >= start, block_col < start + steps)

                    @pl.when(jnp.logical_and(lower, inside))
                    def _():
                        n, count, _ = sizes(stage)
                        block = u_ref[jnp.clip(place(n, block_col - start, block_row - start), 0, count - 1)].T
                        for h in range(2):
                            put(h, block[:, HB * h : HB * h + HB])


def cost(microseconds):
    return pl.CostEstimate(flops=int(microseconds * 1.1e9), bytes_accessed=1 << 20, transcendentals=0)


def call(kernel, out_shape, in_specs, scratch, microseconds=2):
    return pl.pallas_call(
        kernel,
        out_shape=out_shape,
        in_specs=in_specs,
        out_specs=jax.tree.map(lambda _: VM, out_shape),
        scratch_shapes=scratch,
        compiler_params=pltpu.CompilerParams(vmem_limit_bytes=VMEM_LIMIT),
        cost_estimate=cost(microseconds),
    )


def shaped(shape, dtype=F32):
    return jax.ShapeDtypeStruct(shape, dtype)


def per_device(parent, children, index_maps):
    row = lax.axis_index("prow")
    col = lax.axis_index("pcol")
    meta = jnp.concatenate([index_maps.reshape(-1), jnp.stack([row, col]).astype(jnp.int32)])
    front = parent.reshape(6, NB, 3, 2, LANES)
    lead = front[:, :, 0].reshape(6, 16, 32, LANES)
    child = children.reshape(4, 16, 32, LANES)

    child_id = row // 4
    twos = child.reshape(2, 2, 512, LANES)
    picked = [lax.dynamic_index_in_dim(twos, (child_id + flip) % 2, 1, keepdims=False) for flip in range(2)]

    first = jnp.stack([lead[0], child[0]], axis=1)
    first = lax.all_to_all(first, "pcol", 0, 0, tiled=True)
    mine = jnp.concatenate([first[0:KB, 0], first[0:2, 1]], axis=0)
    mine, *picked = lax.optimization_barrier((mine, *picked))
    shed = jnp.where(row == 0, mine[2:5], mine[3:6])
    got_a = lax.ppermute(shed, "prow", [(0, 6), (1, 5)])
    got_b = lax.ppermute(mine[1:2], "prow", [(0, 7)])
    chunk = call(chunk_kernel, shaped((3, 32, LANES)), [SM, VM, VM, VM], [])(meta, mine, got_a, got_b)
    chunk = lax.all_gather(chunk, "pcol")
    lead_parts = lax.all_gather(chunk, "prow")

    rest = jnp.concatenate([lead[1:], child], axis=0).transpose(1, 0, 2, 3)
    rest, chunk = lax.optimization_barrier((rest, chunk))
    rest = lax.all_to_all(rest, "pcol", 0, 0, tiled=True)
    pieces = call(pick_kernel, shaped((8, 2, 32, LANES)), [SM, VM], [])(meta, rest[0:2, 5:9])
    pieces, *picked = lax.optimization_barrier((pieces, *picked))
    pieces = lax.all_to_all(pieces, "prow", 0, 0, tiled=True)

    got = []
    for flip in range(2):
        perm = []
        for p in range(8):
            target = (3 * (p % 4) + 1 + 4 * ((p // 4 + flip) % 2)) % 8
            perm += [(p * 16 + q, target * 16 + (3 * q + 1) % 16) for q in range(1, 16)]
        got.append(lax.ppermute(picked[flip], ("prow", "pcol"), perm))
    scratch = [
        pltpu.VMEM((NB, NB), F32),
        pltpu.VMEM((HB, HB), F32),
        pltpu.VMEM((HB, HB), F32),
        pltpu.VMEM((HB, HB), F32),
    ]

    def chain_shapes(stage):
        _, count, rest = sizes(stage)
        shapes = (shaped((count, NB, NB)), shaped((count, NB, NB), BF16), shaped((count, NB, NB), BF16))
        return shapes + ((shaped((rest, NB, NB)),) if rest else ())

    def chain_scratch(stage):
        return [pltpu.VMEM((sizes(stage)[0] ** 2, NB, NB), F32)] + scratch

    u_0, h_0, l_0, left_over = call(chain_first_kernel, chain_shapes(0), [SM, VM], chain_scratch(0), 18)(meta, lead_parts)
    pieces, left_over, *got = lax.optimization_barrier((pieces, left_over, *got))
    slices = call(assemble_kernel, shaped((KB, 6, 32, LANES)), [SM, VM, VM, VM], [])(
        meta, mine[0:KB], rest[0:KB, 0:5], pieces
    )

    left_parts = lax.all_gather(slices, "pcol")

    left_over, slices, *got = lax.optimization_barrier((left_over, slices, *got))

    residue = (3 * (row + 7)) % 4
    parity = ((row + 15 - 3 * residue) // 4) % 2
    chosen = {}
    for flip in range(2):
        block = 4 * parity + residue
        origin = meta[(parity + flip) % 2 * 16 + block] - 3 * block
        for d in range(3):
            which = jnp.where(origin == d, 0, 1)
            chosen[flip, d] = lax.dynamic_index_in_dim(got[flip], which, 0, keepdims=False)
    down = jnp.stack([chosen[0, 0], chosen[1, 0]])
    up = jnp.stack([chosen[0, 2], chosen[1, 2]])
    down = lax.ppermute(down, "prow", [(p, (p + 7) % 8) for p in range(8)])
    up = lax.ppermute(up, "prow", [(p, (p + 1) % 8) for p in range(8)])
    even, odd = slices[:, 0::2], slices[:, 1::2]
    is_even = col % 2 == 0
    perm_a, perm_b = [], []
    for p in range(8):
        for s in range(16):
            perm_a.append((p * 16 + s, (s // 2) * 16 + p + 8 * (s % 2)))
            perm_b.append((p * 16 + s, (s // 2) * 16 + p + 8 * (1 - s % 2)))
    pair_a = lax.ppermute(jnp.where(is_even, even, odd), ("prow", "pcol"), perm_a)
    pair_b = lax.ppermute(jnp.where(is_even, odd, even), ("prow", "pcol"), perm_b)
    low_side = col < 8
    pair = jnp.stack([jnp.where(low_side, pair_a, pair_b), jnp.where(low_side, pair_b, pair_a)])
    pairs = jnp.broadcast_to(pair[None], (8,) + pair.shape)

    u_1, h_1, l_1, left_over = call(
        lambda *refs: chain_next_kernel(1, *refs), chain_shapes(1), [VM], chain_scratch(1), 28
    )(left_over)

    left_over, pairs, down, up = lax.optimization_barrier((left_over, pairs, down, up))
    right_parts = lax.all_to_all(pairs, "prow", 0, 0, tiled=True).reshape(16, KB, 3, 32, LANES)
    u_2, h_2, l_2 = call(lambda *refs: chain_next_kernel(2, *refs), chain_shapes(2), [VM], chain_scratch(2), 26)(left_over)
    factors = (h_0, l_0, h_1, l_1, h_2, l_2)

    middle = jnp.concatenate([jnp.stack([chosen[0, 1], chosen[1, 1]]), down, up])
    middle, *factors = lax.optimization_barrier((middle, *factors))
    below = lax.ppermute(middle, "pcol", [(q, (q + 1) % 16) for q in range(16)])
    above = lax.ppermute(middle, "pcol", [(q, (q + 15) % 16) for q in range(16)])

    rows = NB * ROWS_STEP
    steps = 6 // ROWS_STEP
    whole = [pl.BlockSpec((sizes(stage)[1], NB, NB), lambda g: (0, 0, 0)) for stage in range(3)]
    by_rows = pl.BlockSpec((rows, 1280), lambda g: (g, 0))
    own_rows = pl.BlockSpec((rows, NB), lambda g: (g, 0))
    yh, yl, own = pl.pallas_call(
        left_kernel,
        grid=(steps,),
        out_shape=(shaped((1536, 1280), BF16), shaped((1536, 1280), BF16), shaped((1536, NB))),
        in_specs=[
            SM,
            pl.BlockSpec((16, KB, ROWS_STEP, 32, LANES), lambda g: (0, 0, g, 0, 0)),
            *(spec for spec in whole for _ in range(2)),
        ],
        out_specs=(by_rows, by_rows, own_rows),
        scratch_shapes=[pltpu.VMEM((rows, 1280), F32)],
        compiler_params=pltpu.CompilerParams(vmem_limit_bytes=VMEM_LIMIT),
        cost_estimate=cost(20),
    )(meta, left_parts, *factors)

    right_parts, own = lax.optimization_barrier((right_parts, own))
    rh, rl = call(
        right_kernel,
        (shaped((768, 1280), BF16), shaped((768, 1280), BF16)),
        [VM] * 7,
        [pltpu.VMEM((768, 1280), F32)],
        12,
    )(right_parts, *factors)

    whole_right = pl.BlockSpec((768, 1280), lambda g: (0, 0))
    whole_child = pl.BlockSpec((6, 512, LANES), lambda g: (0, 0, 0))
    front_rows = pl.BlockSpec((1536 * SCHUR_STEP, LANES), lambda g: (g, 0))
    y_rows = pl.BlockSpec((NB * SCHUR_STEP, 1280), lambda g: (g, 0))
    own_block = pl.BlockSpec((NB * SCHUR_STEP, NB), lambda g: (g, 0))
    out = pl.pallas_call(
        schur_kernel,
        grid=(6 // SCHUR_STEP,),
        out_shape=shaped((9216, LANES)),
        in_specs=[SM, y_rows, y_rows, own_block, whole_right, whole_right, *whole, front_rows]
        + [whole_child] * 3,
        out_specs=front_rows,
        compiler_params=pltpu.CompilerParams(vmem_limit_bytes=VMEM_LIMIT),
        cost_estimate=cost(18),
    )(
        meta,
        yh,
        yl,
        own,
        rh,
        rl,
        u_0,
        u_1,
        u_2,
        parent.reshape(9216, LANES),
        *(x.reshape(6, 512, LANES) for x in (above, middle, below)),
    )
    return out.reshape(6, 1, NB, 3, 1, NB)


def solution(mesh):
    in_specs = (
        P(None, "prow", None, None, "pcol", None),
        P(None, "prow", None, None, "pcol", None),
        P(),
    )
    out_specs = P(None, "prow", None, None, "pcol", None)
    return jax.shard_map(
        per_device, mesh=mesh, in_specs=in_specs, out_specs=out_specs, check_vma=False
    )
```

```python
import jax
import jax.numpy as jnp
from jax import lax
from jax.experimental import pallas as pl
from jax.experimental.pallas import tpu as pltpu
from jax.sharding import PartitionSpec as P

KB = 5
NB = 256
HB = 128
LANES = 128
F32 = jnp.float32
BF16 = jnp.bfloat16
VMEM_LIMIT = 60 * 1024 * 1024
VM = pl.BlockSpec(memory_space=pltpu.VMEM)
SM = pl.BlockSpec(memory_space=pltpu.SMEM)


def route_of(meta, child, residue):
    there, slot = False, 0
    for turn in range(4):
        target = meta[child * 16 + 4 * turn + residue]
        here = target % 8 == meta[32]
        there = jnp.logical_or(there, here)
        slot = jnp.where(here, target // 8, slot)
    return there, slot


def turn_for(meta, target_row):
    child, residue = meta[32] // 4, meta[32] % 4
    chosen = 0
    for turn in range(1, 4):
        chosen = jnp.where(meta[child * 16 + 4 * turn + residue] % 8 == target_row, turn, chosen)
    return chosen


def routed_from(meta, n):
    flip, d = n // 3, n % 3
    row = meta[32]
    residue = (3 * (row + 8 - d)) % 4
    parity = ((row + 16 - 3 * residue - d) // 4) % 2
    child = (parity + flip) % 2
    first = 4 * parity + residue
    second = first + 8
    is_first = meta[child * 16 + first] == 3 * first + d
    is_second = meta[child * 16 + second] == 3 * second + d
    block = jnp.where(is_first, first, second)
    return child, jnp.logical_or(is_first, is_second), (3 * block + d) // 8


ROUTED = (1, 4, 0, 3, 2, 5)


def pick_kernel(meta, parts_ref, out_ref):
    for target_row in range(8):
        turn = turn_for(meta, target_row)
        for v in range(2):
            out_ref[target_row, v] = parts_ref[v, turn]


def assemble_kernel(meta, first_ref, rest_ref, got_ref, out_ref):
    for j in range(KB):
        out_ref[j, 0] = first_ref[j]
        out_ref[j, 1:6] = rest_ref[j]
    for child in range(2):
        for residue in range(4):
            there, slot = route_of(meta, child, residue)
            for v in range(2):
                column = meta[child * 16 + v]

                @pl.when(jnp.logical_and(there, column < KB))
                def _():
                    out_ref[column, slot] = out_ref[column, slot] + got_ref[4 * child + residue, v]


def chunk_kernel(meta, mine_ref, got_a_ref, got_b_ref, out_ref):
    for row, picks in enumerate(CHUNKS):

        @pl.when(meta[32] == row)
        def _():
            for at in range(3):
                kind, index = picks[at] if at < len(picks) else (0, 0)
                source = (mine_ref, got_a_ref, got_b_ref)[kind]
                out_ref[at] = source[index]


CHUNKS = [
    [(0, 0), (0, 5), (0, 6)],
    [(0, 1), (0, 2), (0, 6)],
    [(0, 2), (0, 3), (0, 4)],
    [(0, 3), (0, 4)],
    [(0, 4), (0, 5), (0, 6)],
    [(1, 0), (1, 1), (0, 6)],
    [(1, 0), (1, 1), (1, 2)],
    [(2, 0)],
]
UPPER_AT = {
    (0, 0): (0, 0),
    (0, 1): (7, 0),
    (0, 2): (6, 0),
    (0, 3): (6, 1),
    (0, 4): (6, 2),
    (1, 1): (1, 0),
    (1, 2): (1, 1),
    (1, 3): (5, 0),
    (1, 4): (5, 1),
    (2, 2): (2, 0),
    (2, 3): (2, 1),
    (2, 4): (2, 2),
    (3, 3): (3, 0),
    (3, 4): (3, 1),
    (4, 4): (4, 0),
}
CHILD_AT = {
    (0, 0, 0): (0, 1),
    (0, 0, 1): (0, 2),
    (0, 1, 1): (1, 2),
    (1, 0, 0): (4, 1),
    (1, 0, 1): (4, 2),
    (1, 1, 1): (5, 2),
}


def exact(a, b, dims):
    return lax.dot_general(a, b, (dims, ((), ())), precision=lax.Precision.HIGHEST, preferred_element_type=F32)


def dot3(ah, al, bh, bl, dims):
    def dot(a, b):
        return lax.dot_general(a, b, (dims, ((), ())), preferred_element_type=F32)

    return dot(ah, bh) + (dot(ah, bl) + dot(al, bh))


NN = ((1,), (0,))
NT = ((1,), (1,))
TN = ((0,), (0,))


def factor_128(a_ref, x_ref, u_ref):
    shape = (8, LANES)
    lane = lax.broadcasted_iota(jnp.int32, (HB, LANES), 1)
    sub = lax.broadcasted_iota(jnp.int32, (HB, LANES), 0)
    x_ref[...] = jnp.where(lane == sub, 1.0, 0.0).astype(F32)
    for g in range(HB // 8):
        rows = slice(8 * g, 8 * g + 8)
        a_g = a_ref[rows, :]
        x_g = x_ref[rows, :]
        cols = [jnp.broadcast_to(a_g[:, 8 * g + s : 8 * g + s + 1], shape) for s in range(8)]
        d = [[jnp.broadcast_to(cols[s][t : t + 1, :], shape) for s in range(t + 1)] for t in range(8)]
        low = [[None] * 8 for _ in range(8)]
        rinv = []
        for s in range(8):
            r = lax.rsqrt(d[s][s])
            rinv.append(r)
            for t in range(s + 1, 8):
                low[t][s] = d[t][s] * r
            for t in range(s + 1, 8):
                for t2 in range(s + 1, t + 1):
                    d[t][t2] = d[t][t2] - low[t][s] * low[t2][s]
        ub, xb = [], []
        for t in range(8):
            ua = jnp.broadcast_to(a_g[t : t + 1, :], shape)
            xa = jnp.broadcast_to(x_g[t : t + 1, :], shape)
            for s in range(t):
                ua = ua - low[t][s] * ub[s]
                xa = xa - low[t][s] * xb[s]
            ub.append(ua * rinv[t])
            xb.append(xa * rinv[t])
            u_ref[8 * g + t : 8 * g + t + 1, :] = ub[t][0:1, :]
            x_ref[8 * g + t : 8 * g + t + 1, :] = xb[t][0:1, :]
        for i in range(g + 1, HB // 8):
            rows_i = slice(8 * i, 8 * i + 8)
            a_i = a_ref[rows_i, :]
            x_i = x_ref[rows_i, :]
            w = []
            for t in range(8):
                wt = jnp.broadcast_to(a_i[:, 8 * g + t : 8 * g + t + 1], shape)
                for s in range(t):
                    wt = wt - low[t][s] * w[s]
                w.append(wt * rinv[t])
            for t in range(8):
                a_i = a_i - w[t] * ub[t]
                x_i = x_i - w[t] * xb[t]
            a_ref[rows_i, :] = a_i
            x_ref[rows_i, :] = x_i
    u_ref[...] = jnp.where(lane >= sub, u_ref[...], 0.0)


def split(a):
    high = a.astype(BF16)
    return high, (a - high.astype(F32)).astype(BF16)


CUT = 2
REST = KB - CUT


def place_head(k, i):
    if isinstance(i, int):
        return k + (i if i < CUT else 2 * i - 1)
    return k + jnp.where(i < CUT, i, 2 * i - 1)


def place_tail(k, i):
    return i * (i + 1) // 2 + k


HEADS = CUT * KB - 1
TAILS = REST * (REST + 1) // 2


def eliminate(n, steps, place, f_ref, u_ref, th_ref, tl_ref, v_ref, a_s, x_s, u_s):
    @pl.loop(0, 2 * steps)
    def _(step):
        k = step // 2
        half = step % 2
        kk = k * n + k
        pk = place(k, k)

        @pl.when(half == 0)
        def _():
            a_s[...] = f_ref[kk, 0:HB, 0:HB]

        @pl.when(half == 1)
        def _():
            u12 = exact(v_ref[0:HB, 0:HB], f_ref[kk, 0:HB, HB:NB], NN)
            u_ref[pk, 0:HB, HB:NB] = u12
            a_s[...] = f_ref[kk, HB:NB, HB:NB] - exact(u12, u12, TN)

        factor_128(a_s, x_s, u_s)

        @pl.when(half == 0)
        def _():
            u_ref[pk, 0:HB, 0:HB] = u_s[...]
            v_ref[0:HB, 0:HB] = x_s[...]

        @pl.when(half == 1)
        def _():
            u_ref[pk, HB:NB, HB:NB] = u_s[...]
            u_ref[pk, HB:NB, 0:HB] = jnp.zeros((HB, HB), F32)
            v_ref[HB:NB, HB:NB] = x_s[...]
            v_ref[0:HB, HB:NB] = jnp.zeros((HB, HB), F32)
            lx = exact(u_ref[pk, 0:HB, HB:NB], v_ref[0:HB, 0:HB], TN)
            v_ref[HB:NB, 0:HB] = -exact(x_s[...], lx, NN)
            high, low = split(v_ref[...].T)
            th_ref[pk] = high
            tl_ref[pk] = low
            vh, vl = split(v_ref[...])

            @pl.loop(k + 1, n)
            def _(i):
                u = dot3(vh, vl, *split(f_ref[k * n + i]), NN)
                at = place(k, i)
                u_ref[at] = u
                high, low = split(u)
                th_ref[at] = high
                tl_ref[at] = low

            @pl.loop(k + 1, n)
            def _(i):
                at_i = place(k, i)

                @pl.loop(i, n)
                def _(j):
                    at_j = place(k, j)
                    f_ref[i * n + j] = f_ref[i * n + j] - dot3(
                        th_ref[at_i], tl_ref[at_i], th_ref[at_j], tl_ref[at_j], TN
                    )


def chain_head_kernel(meta, parts_ref, u_ref, th_ref, tl_ref, rest_ref, f_ref, *scratch):
    def take(at, s, h):
        return parts_ref[at[0], s, at[1], pl.ds(h, 16, stride=2), :]

    for (k, i), at in UPPER_AT.items():
        for s in range(16):
            for h in range(2):
                f_ref[k * KB + i, 16 * s : 16 * s + 16, HB * h : HB * h + HB] = take(at, s, h)
    for (c, u, v), at in CHILD_AT.items():
        k = meta[c * 16 + u]
        i = meta[c * 16 + v]

        @pl.when(jnp.logical_and(k < KB, i < KB))
        def _():
            for s in range(16):
                for h in range(2):
                    place = (k * KB + i, slice(16 * s, 16 * s + 16), slice(HB * h, HB * h + HB))
                    f_ref[place] = f_ref[place] + take(at, s, h)

    eliminate(KB, CUT, place_head, f_ref, u_ref, th_ref, tl_ref, *scratch)
    for i in range(REST):
        for j in range(i, REST):
            rest_ref[place_tail(i, j)] = f_ref[(CUT + i) * KB + CUT + j]


def chain_tail_kernel(rest_ref, u_ref, th_ref, tl_ref, f_ref, *scratch):
    for i in range(REST):
        for j in range(i, REST):
            f_ref[i * REST + j] = rest_ref[place_tail(i, j)]
    eliminate(REST, REST, place_tail, f_ref, u_ref, th_ref, tl_ref, *scratch)


def solve_rows(raw_ref, yh_ref, yl_ref, factors):
    head_h, head_l, tail_h, tail_l = factors

    def factor(m, k):
        if m < CUT:
            at = place_head(m, k)
            return head_h[at], head_l[at]
        at = place_tail(m - CUT, k - CUT)
        return tail_h[at], tail_l[at]

    for k in range(KB):
        at = slice(NB * k, NB * k + NB)
        t = raw_ref[:, at]
        for m in range(k):
            am = slice(NB * m, NB * m + NB)
            t = t - dot3(yh_ref[:, am], yl_ref[:, am], *factor(m, k), NN)
        high, low = split(t)
        y = dot3(high, low, *factor(k, k), NN)
        raw_ref[:, at] = y
        high, low = split(y)
        yh_ref[:, at] = high
        yl_ref[:, at] = low


def right_kernel(parts_ref, hh_ref, hl_ref, th_ref, tl_ref, yh_ref, yl_ref, raw):
    @pl.loop(0, 16)
    def _(s):
        for c in range(3):
            for j in range(KB):
                for h in range(2):
                    raw[pl.ds(pl.multiple_of(NB * c + 16 * s, 16), 16), NB * j + HB * h : NB * j + HB * h + HB] = parts_ref[
                        s, j, c, pl.ds(h, 16, stride=2), :
                    ]
    solve_rows(raw, yh_ref, yl_ref, (hh_ref, hl_ref, th_ref, tl_ref))


ROWS_STEP = 2


def left_kernel(meta, parts_ref, hh_ref, hl_ref, th_ref, tl_ref, yh_ref, yl_ref, own_ref, raw):
    @pl.loop(0, 16)
    def _(s):
        for a in range(ROWS_STEP):
            for j in range(KB):
                for h in range(2):
                    raw[pl.ds(pl.multiple_of(NB * a + 16 * s, 16), 16), NB * j + HB * h : NB * j + HB * h + HB] = parts_ref[
                        s, j, a, pl.ds(h, 16, stride=2), :
                    ]
    solve_rows(raw, yh_ref, yl_ref, (hh_ref, hl_ref, th_ref, tl_ref))
    for j in range(KB):

        @pl.when(meta[33] == j)
        def _():
            own_ref[...] = raw[:, NB * j : NB * j + NB]


SCHUR_STEP = 1


def schur_kernel(meta, yh, yl, own_ref, rh_ref, rl_ref, head_ref, tail_ref, parent_ref, child_0, child_1, child_2, out_ref):
    step = pl.program_id(0)
    row, col = meta[32], meta[33]
    routes = []
    for n in ROUTED:
        routes.append(routed_from(meta, n))

    for a in range(SCHUR_STEP):
        slot = step * SCHUR_STEP + a
        block_row = row + 8 * slot
        rows = slice(NB * a, NB * a + NB)
        for c in range(3):
            block_col = col + 16 * c

            def put(h, value):
                out_ref[pl.ds(1536 * a + 2 * c + h, NB, stride=6), :] = value

            @pl.when(jnp.logical_and(block_row >= KB, block_col >= KB))
            def _():
                cols = slice(NB * c, NB * c + NB)
                product = dot3(yh[rows, :], yl[rows, :], rh_ref[cols, :], rl_ref[cols, :], NT)
                for h in range(2):
                    put(h, parent_ref[pl.ds(1536 * a + 2 * c + h, NB, stride=6), :] - product[:, HB * h : HB * h + HB])
                turn = block_col % 3
                source = block_col // 3
                for n, (child, there, to) in enumerate(routes):
                    here = jnp.logical_and(there, to == slot)
                    here = jnp.logical_and(here, meta[child * 16 + source] == block_col)
                    for d, child_ref in enumerate((child_0, child_1, child_2)):

                        @pl.when(jnp.logical_and(here, turn == d))
                        def _():
                            for h in range(2):
                                at = pl.ds(1536 * a + 2 * c + h, NB, stride=6)
                                out_ref[at, :] = out_ref[at, :] + child_ref[n, pl.ds(h, NB, stride=2), :]

            @pl.when(jnp.logical_and(block_row < KB, block_col >= KB))
            def _():
                for h in range(2):
                    put(h, jnp.zeros((NB, HB), F32))

            if c == 0:

                @pl.when(jnp.logical_and(block_row >= KB, block_col < KB))
                def _():
                    for h in range(2):
                        put(h, own_ref[rows, HB * h : HB * h + HB])

                in_lead = jnp.logical_and(block_row < KB, block_col < KB)
                upper = block_row < block_col

                @pl.when(jnp.logical_and(in_lead, upper))
                def _():
                    for h in range(2):
                        put(h, jnp.zeros((NB, HB), F32))

                lower = jnp.logical_and(in_lead, jnp.logical_not(upper))

                @pl.when(jnp.logical_and(lower, block_col < CUT))
                def _():
                    block = head_ref[jnp.clip(place_head(block_col, block_row), 0, HEADS - 1)].T
                    for h in range(2):
                        put(h, block[:, HB * h : HB * h + HB])

                @pl.when(jnp.logical_and(lower, block_col >= CUT))
                def _():
                    at = jnp.clip(place_tail(block_col - CUT, block_row - CUT), 0, TAILS - 1)
                    block = tail_ref[at].T
                    for h in range(2):
                        put(h, block[:, HB * h : HB * h + HB])


def cost(microseconds):
    return pl.CostEstimate(flops=int(microseconds * 1.1e9), bytes_accessed=1 << 20, transcendentals=0)


def call(kernel, out_shape, in_specs, scratch, microseconds=2):
    return pl.pallas_call(
        kernel,
        out_shape=out_shape,
        in_specs=in_specs,
        out_specs=jax.tree.map(lambda _: VM, out_shape),
        scratch_shapes=scratch,
        compiler_params=pltpu.CompilerParams(vmem_limit_bytes=VMEM_LIMIT),
        cost_estimate=cost(microseconds),
    )


def shaped(shape, dtype=F32):
    return jax.ShapeDtypeStruct(shape, dtype)


def per_device(parent, children, index_maps):
    row = lax.axis_index("prow")
    col = lax.axis_index("pcol")
    meta = jnp.concatenate([index_maps.reshape(-1), jnp.stack([row, col]).astype(jnp.int32)])
    front = parent.reshape(6, NB, 3, 2, LANES)
    lead = front[:, :, 0].reshape(6, 16, 32, LANES)
    child = children.reshape(4, 16, 32, LANES)

    child_id = row // 4
    twos = child.reshape(2, 2, 512, LANES)
    picked = [lax.dynamic_index_in_dim(twos, (child_id + flip) % 2, 1, keepdims=False) for flip in range(2)]

    first = jnp.stack([lead[0], child[0]], axis=1)
    first = lax.all_to_all(first, "pcol", 0, 0, tiled=True)
    mine = jnp.concatenate([first[0:KB, 0], first[0:2, 1]], axis=0)
    mine, *picked = lax.optimization_barrier((mine, *picked))
    shed = jnp.where(row == 0, mine[2:5], mine[3:6])
    got_a = lax.ppermute(shed, "prow", [(0, 6), (1, 5)])
    got_b = lax.ppermute(mine[1:2], "prow", [(0, 7)])
    chunk = call(chunk_kernel, shaped((3, 32, LANES)), [SM, VM, VM, VM], [])(meta, mine, got_a, got_b)
    chunk = lax.all_gather(chunk, "pcol")
    lead_parts = lax.all_gather(chunk, "prow")

    rest = jnp.concatenate([lead[1:], child], axis=0).transpose(1, 0, 2, 3)
    rest, chunk = lax.optimization_barrier((rest, chunk))
    rest = lax.all_to_all(rest, "pcol", 0, 0, tiled=True)
    pieces = call(pick_kernel, shaped((8, 2, 32, LANES)), [SM, VM], [])(meta, rest[0:2, 5:9])
    pieces, *picked = lax.optimization_barrier((pieces, *picked))
    pieces = lax.all_to_all(pieces, "prow", 0, 0, tiled=True)

    got = []
    for flip in range(2):
        perm = []
        for p in range(8):
            target = (3 * (p % 4) + 1 + 4 * ((p // 4 + flip) % 2)) % 8
            perm += [(p * 16 + q, target * 16 + (3 * q + 1) % 16) for q in range(1, 16)]
        got.append(lax.ppermute(picked[flip], ("prow", "pcol"), perm))
    pieces, *got = lax.optimization_barrier((pieces, *got))
    slices = call(assemble_kernel, shaped((KB, 6, 32, LANES)), [SM, VM, VM, VM], [])(
        meta, mine[0:KB], rest[0:KB, 0:5], pieces
    )

    left_parts = lax.all_gather(slices, "pcol")

    lead_parts, slices, *got = lax.optimization_barrier((lead_parts, slices, *got))

    residue = (3 * (row + 7)) % 4
    parity = ((row + 15 - 3 * residue) // 4) % 2
    chosen = {}
    for flip in range(2):
        block = 4 * parity + residue
        origin = meta[(parity + flip) % 2 * 16 + block] - 3 * block
        for d in range(3):
            which = jnp.where(origin == d, 0, 1)
            chosen[flip, d] = lax.dynamic_index_in_dim(got[flip], which, 0, keepdims=False)
    down = jnp.stack([chosen[0, 0], chosen[1, 0]])
    up = jnp.stack([chosen[0, 2], chosen[1, 2]])
    down = lax.ppermute(down, "prow", [(p, (p + 7) % 8) for p in range(8)])
    up = lax.ppermute(up, "prow", [(p, (p + 1) % 8) for p in range(8)])
    even, odd = slices[:, 0::2], slices[:, 1::2]
    is_even = col % 2 == 0
    perm_a, perm_b = [], []
    for p in range(8):
        for s in range(16):
            perm_a.append((p * 16 + s, (s // 2) * 16 + p + 8 * (s % 2)))
            perm_b.append((p * 16 + s, (s // 2) * 16 + p + 8 * (1 - s % 2)))
    pair_a = lax.ppermute(jnp.where(is_even, even, odd), ("prow", "pcol"), perm_a)
    pair_b = lax.ppermute(jnp.where(is_even, odd, even), ("prow", "pcol"), perm_b)
    low_side = col < 8
    pair = jnp.stack([jnp.where(low_side, pair_a, pair_b), jnp.where(low_side, pair_b, pair_a)])
    pairs = jnp.broadcast_to(pair[None], (8,) + pair.shape)

    scratch = [
        pltpu.VMEM((NB, NB), F32),
        pltpu.VMEM((HB, HB), F32),
        pltpu.VMEM((HB, HB), F32),
        pltpu.VMEM((HB, HB), F32),
    ]
    head_u, head_h, head_l, left_over = call(
        chain_head_kernel,
        (
            shaped((HEADS, NB, NB)),
            shaped((HEADS, NB, NB), BF16),
            shaped((HEADS, NB, NB), BF16),
            shaped((TAILS, NB, NB)),
        ),
        [SM, VM],
        [pltpu.VMEM((KB * KB, NB, NB), F32)] + scratch,
        32,
    )(meta, lead_parts)

    left_over, pairs, down, up = lax.optimization_barrier((left_over, pairs, down, up))
    right_parts = lax.all_to_all(pairs, "prow", 0, 0, tiled=True).reshape(16, KB, 3, 32, LANES)
    tail_u, tail_h, tail_l = call(
        chain_tail_kernel,
        (shaped((TAILS, NB, NB)), shaped((TAILS, NB, NB), BF16), shaped((TAILS, NB, NB), BF16)),
        [VM],
        [pltpu.VMEM((REST * REST, NB, NB), F32)] + scratch,
        40,
    )(left_over)

    middle = jnp.concatenate([jnp.stack([chosen[0, 1], chosen[1, 1]]), down, up])
    middle, tail_h = lax.optimization_barrier((middle, tail_h))
    below = lax.ppermute(middle, "pcol", [(q, (q + 1) % 16) for q in range(16)])
    above = lax.ppermute(middle, "pcol", [(q, (q + 15) % 16) for q in range(16)])

    rows = NB * ROWS_STEP
    steps = 6 // ROWS_STEP
    whole_head = pl.BlockSpec((HEADS, NB, NB), lambda g: (0, 0, 0))
    whole_tail = pl.BlockSpec((TAILS, NB, NB), lambda g: (0, 0, 0))
    by_rows = pl.BlockSpec((rows, 1280), lambda g: (g, 0))
    own_rows = pl.BlockSpec((rows, NB), lambda g: (g, 0))
    yh, yl, own = pl.pallas_call(
        left_kernel,
        grid=(steps,),
        out_shape=(shaped((1536, 1280), BF16), shaped((1536, 1280), BF16), shaped((1536, NB))),
        in_specs=[
            SM,
            pl.BlockSpec((16, KB, ROWS_STEP, 32, LANES), lambda g: (0, 0, g, 0, 0)),
            whole_head,
            whole_head,
            whole_tail,
            whole_tail,
        ],
        out_specs=(by_rows, by_rows, own_rows),
        scratch_shapes=[pltpu.VMEM((rows, 1280), F32)],
        compiler_params=pltpu.CompilerParams(vmem_limit_bytes=VMEM_LIMIT),
        cost_estimate=cost(20),
    )(meta, left_parts, head_h, head_l, tail_h, tail_l)

    right_parts, own = lax.optimization_barrier((right_parts, own))
    rh, rl = call(
        right_kernel,
        (shaped((768, 1280), BF16), shaped((768, 1280), BF16)),
        [VM] * 5,
        [pltpu.VMEM((768, 1280), F32)],
        12,
    )(right_parts, head_h, head_l, tail_h, tail_l)

    whole_right = pl.BlockSpec((768, 1280), lambda g: (0, 0))
    whole_child = pl.BlockSpec((6, 512, LANES), lambda g: (0, 0, 0))
    front_rows = pl.BlockSpec((1536 * SCHUR_STEP, LANES), lambda g: (g, 0))
    y_rows = pl.BlockSpec((NB * SCHUR_STEP, 1280), lambda g: (g, 0))
    own_block = pl.BlockSpec((NB * SCHUR_STEP, NB), lambda g: (g, 0))
    out = pl.pallas_call(
        schur_kernel,
        grid=(6 // SCHUR_STEP,),
        out_shape=shaped((9216, LANES)),
        in_specs=[SM, y_rows, y_rows, own_block, whole_right, whole_right, whole_head, whole_tail, front_rows]
        + [whole_child] * 3,
        out_specs=front_rows,
        compiler_params=pltpu.CompilerParams(vmem_limit_bytes=VMEM_LIMIT),
        cost_estimate=cost(18),
    )(
        meta,
        yh,
        yl,
        own,
        rh,
        rl,
        head_u,
        tail_u,
        parent.reshape(9216, LANES),
        *(x.reshape(6, 512, LANES) for x in (above, middle, below)),
    )
    return out.reshape(6, 1, NB, 3, 1, NB)


def solution(mesh):
    in_specs = (
        P(None, "prow", None, None, "pcol", None),
        P(None, "prow", None, None, "pcol", None),
        P(),
    )
    out_specs = P(None, "prow", None, None, "pcol", None)
    return jax.shard_map(
        per_device, mesh=mesh, in_specs=in_specs, out_specs=out_specs, check_vma=False
    )
```

```python
import jax
import jax.numpy as jnp
from jax import lax
from jax.experimental import pallas as pl
from jax.experimental.pallas import tpu as pltpu
from jax.sharding import PartitionSpec as P

KB = 5
NB = 256
HB = 128
LANES = 128
F32 = jnp.float32
BF16 = jnp.bfloat16
VMEM_LIMIT = 60 * 1024 * 1024
VM = pl.BlockSpec(memory_space=pltpu.VMEM)
SM = pl.BlockSpec(memory_space=pltpu.SMEM)


def route_of(meta, child, residue):
    there, slot = False, 0
    for turn in range(4):
        target = meta[child * 16 + 4 * turn + residue]
        here = target % 8 == meta[32]
        there = jnp.logical_or(there, here)
        slot = jnp.where(here, target // 8, slot)
    return there, slot


def turn_for(meta, target_row):
    child, residue = meta[32] // 4, meta[32] % 4
    chosen = 0
    for turn in range(1, 4):
        chosen = jnp.where(meta[child * 16 + 4 * turn + residue] % 8 == target_row, turn, chosen)
    return chosen


def routed_from(meta, n):
    flip, d = n // 3, n % 3
    row = meta[32]
    residue = (3 * (row + 8 - d)) % 4
    parity = ((row + 16 - 3 * residue - d) // 4) % 2
    child = (parity + flip) % 2
    first = 4 * parity + residue
    second = first + 8
    is_first = meta[child * 16 + first] == 3 * first + d
    is_second = meta[child * 16 + second] == 3 * second + d
    block = jnp.where(is_first, first, second)
    return child, jnp.logical_or(is_first, is_second), (3 * block + d) // 8


ROUTED = (1, 4, 0, 3, 2, 5)


def pick_kernel(meta, parts_ref, out_ref):
    for target_row in range(8):
        turn = turn_for(meta, target_row)
        for v in range(2):
            out_ref[target_row, v] = parts_ref[v, turn]


def assemble_kernel(meta, first_ref, rest_ref, got_ref, out_ref):
    for j in range(KB):
        out_ref[j, 0] = first_ref[j]
        out_ref[j, 1:6] = rest_ref[j]
    for child in range(2):
        for residue in range(4):
            there, slot = route_of(meta, child, residue)
            for v in range(2):
                column = meta[child * 16 + v]

                @pl.when(jnp.logical_and(there, column < KB))
                def _():
                    out_ref[column, slot] = out_ref[column, slot] + got_ref[4 * child + residue, v]


def chunk_kernel(meta, mine_ref, got_a_ref, got_b_ref, out_ref):
    for row, picks in enumerate(CHUNKS):

        @pl.when(meta[32] == row)
        def _():
            for at in range(3):
                kind, index = picks[at] if at < len(picks) else (0, 0)
                source = (mine_ref, got_a_ref, got_b_ref)[kind]
                out_ref[at] = source[index]


CHUNKS = [
    [(0, 0), (0, 5), (0, 6)],
    [(0, 1), (0, 2), (0, 6)],
    [(0, 2), (0, 3), (0, 4)],
    [(0, 3), (0, 4)],
    [(0, 4), (0, 5), (0, 6)],
    [(1, 0), (1, 1), (0, 6)],
    [(1, 0), (1, 1), (1, 2)],
    [(2, 0)],
]
UPPER_AT = {
    (0, 0): (0, 0),
    (0, 1): (7, 0),
    (0, 2): (6, 0),
    (0, 3): (6, 1),
    (0, 4): (6, 2),
    (1, 1): (1, 0),
    (1, 2): (1, 1),
    (1, 3): (5, 0),
    (1, 4): (5, 1),
    (2, 2): (2, 0),
    (2, 3): (2, 1),
    (2, 4): (2, 2),
    (3, 3): (3, 0),
    (3, 4): (3, 1),
    (4, 4): (4, 0),
}
CHILD_AT = {
    (0, 0, 0): (0, 1),
    (0, 0, 1): (0, 2),
    (0, 1, 1): (1, 2),
    (1, 0, 0): (4, 1),
    (1, 0, 1): (4, 2),
    (1, 1, 1): (5, 2),
}


def exact(a, b, dims):
    return lax.dot_general(a, b, (dims, ((), ())), precision=lax.Precision.HIGHEST, preferred_element_type=F32)


def dot3(ah, al, bh, bl, dims):
    def dot(a, b):
        return lax.dot_general(a, b, (dims, ((), ())), preferred_element_type=F32)

    return dot(ah, bh) + (dot(ah, bl) + dot(al, bh))


NN = ((1,), (0,))
NT = ((1,), (1,))
TN = ((0,), (0,))


def factor_128(a_ref, x_ref, u_ref):
    shape = (8, LANES)
    lane = lax.broadcasted_iota(jnp.int32, (HB, LANES), 1)
    sub = lax.broadcasted_iota(jnp.int32, (HB, LANES), 0)
    x_ref[...] = jnp.where(lane == sub, 1.0, 0.0).astype(F32)
    for g in range(HB // 8):
        rows = slice(8 * g, 8 * g + 8)
        a_g = a_ref[rows, :]
        x_g = x_ref[rows, :]
        cols = [jnp.broadcast_to(a_g[:, 8 * g + s : 8 * g + s + 1], shape) for s in range(8)]
        d = [[jnp.broadcast_to(cols[s][t : t + 1, :], shape) for s in range(t + 1)] for t in range(8)]
        low = [[None] * 8 for _ in range(8)]
        rinv = []
        for s in range(8):
            r = lax.rsqrt(d[s][s])
            rinv.append(r)
            for t in range(s + 1, 8):
                low[t][s] = d[t][s] * r
            for t in range(s + 1, 8):
                for t2 in range(s + 1, t + 1):
                    d[t][t2] = d[t][t2] - low[t][s] * low[t2][s]
        ub, xb = [], []
        for t in range(8):
            ua = jnp.broadcast_to(a_g[t : t + 1, :], shape)
            xa = jnp.broadcast_to(x_g[t : t + 1, :], shape)
            for s in range(t):
                ua = ua - low[t][s] * ub[s]
                xa = xa - low[t][s] * xb[s]
            ub.append(ua * rinv[t])
            xb.append(xa * rinv[t])
            u_ref[8 * g + t : 8 * g + t + 1, :] = ub[t][0:1, :]
            x_ref[8 * g + t : 8 * g + t + 1, :] = xb[t][0:1, :]
        for i in range(g + 1, HB // 8):
            rows_i = slice(8 * i, 8 * i + 8)
            a_i = a_ref[rows_i, :]
            x_i = x_ref[rows_i, :]
            w = []
            for t in range(8):
                wt = jnp.broadcast_to(a_i[:, 8 * g + t : 8 * g + t + 1], shape)
                for s in range(t):
                    wt = wt - low[t][s] * w[s]
                w.append(wt * rinv[t])
            for t in range(8):
                a_i = a_i - w[t] * ub[t]
                x_i = x_i - w[t] * xb[t]
            a_ref[rows_i, :] = a_i
            x_ref[rows_i, :] = x_i
    u_ref[...] = jnp.where(lane >= sub, u_ref[...], 0.0)


def split(a):
    high = a.astype(BF16)
    return high, (a - high.astype(F32)).astype(BF16)


CUT = 2
REST = KB - CUT


def place_head(k, i):
    if isinstance(i, int):
        return k + (i if i < CUT else 2 * i - 1)
    return k + jnp.where(i < CUT, i, 2 * i - 1)


def place_tail(k, i):
    return i * (i + 1) // 2 + k


HEADS = CUT * KB - 1
TAILS = REST * (REST + 1) // 2


def eliminate(n, steps, place, f_ref, u_ref, th_ref, tl_ref, v_ref, a_s, x_s, u_s):
    @pl.loop(0, 2 * steps)
    def _(step):
        k = step // 2
        half = step % 2
        kk = k * n + k
        pk = place(k, k)

        @pl.when(half == 0)
        def _():
            a_s[...] = f_ref[kk, 0:HB, 0:HB]

        @pl.when(half == 1)
        def _():
            u12 = exact(v_ref[0:HB, 0:HB], f_ref[kk, 0:HB, HB:NB], NN)
            u_ref[pk, 0:HB, HB:NB] = u12
            a_s[...] = f_ref[kk, HB:NB, HB:NB] - exact(u12, u12, TN)

        factor_128(a_s, x_s, u_s)

        @pl.when(half == 0)
        def _():
            u_ref[pk, 0:HB, 0:HB] = u_s[...]
            v_ref[0:HB, 0:HB] = x_s[...]

        @pl.when(half == 1)
        def _():
            u_ref[pk, HB:NB, HB:NB] = u_s[...]
            u_ref[pk, HB:NB, 0:HB] = jnp.zeros((HB, HB), F32)
            v_ref[HB:NB, HB:NB] = x_s[...]
            v_ref[0:HB, HB:NB] = jnp.zeros((HB, HB), F32)
            lx = exact(u_ref[pk, 0:HB, HB:NB], v_ref[0:HB, 0:HB], TN)
            v_ref[HB:NB, 0:HB] = -exact(x_s[...], lx, NN)
            high, low = split(v_ref[...].T)
            th_ref[pk] = high
            tl_ref[pk] = low
            vh, vl = split(v_ref[...])

            @pl.loop(k + 1, n)
            def _(i):
                u = dot3(vh, vl, *split(f_ref[k * n + i]), NN)
                at = place(k, i)
                u_ref[at] = u
                high, low = split(u)
                th_ref[at] = high
                tl_ref[at] = low

            @pl.loop(k + 1, n)
            def _(i):
                at_i = place(k, i)

                @pl.loop(i, n)
                def _(j):
                    at_j = place(k, j)
                    f_ref[i * n + j] = f_ref[i * n + j] - dot3(
                        th_ref[at_i], tl_ref[at_i], th_ref[at_j], tl_ref[at_j], TN
                    )


def chain_head_kernel(meta, parts_ref, u_ref, th_ref, tl_ref, rest_ref, f_ref, *scratch):
    def take(at, s, h):
        return parts_ref[at[0], s, at[1], pl.ds(h, 16, stride=2), :]

    for (k, i), at in UPPER_AT.items():
        for s in range(16):
            for h in range(2):
                f_ref[k * KB + i, 16 * s : 16 * s + 16, HB * h : HB * h + HB] = take(at, s, h)
    for (c, u, v), at in CHILD_AT.items():
        k = meta[c * 16 + u]
        i = meta[c * 16 + v]

        @pl.when(jnp.logical_and(k < KB, i < KB))
        def _():
            for s in range(16):
                for h in range(2):
                    place = (k * KB + i, slice(16 * s, 16 * s + 16), slice(HB * h, HB * h + HB))
                    f_ref[place] = f_ref[place] + take(at, s, h)

    eliminate(KB, CUT, place_head, f_ref, u_ref, th_ref, tl_ref, *scratch)
    for i in range(REST):
        for j in range(i, REST):
            rest_ref[place_tail(i, j)] = f_ref[(CUT + i) * KB + CUT + j]


def chain_tail_kernel(rest_ref, u_ref, th_ref, tl_ref, f_ref, *scratch):
    for i in range(REST):
        for j in range(i, REST):
            f_ref[i * REST + j] = rest_ref[place_tail(i, j)]
    eliminate(REST, REST, place_tail, f_ref, u_ref, th_ref, tl_ref, *scratch)


def solve_rows(raw_ref, yh_ref, yl_ref, factors):
    head_h, head_l, tail_h, tail_l = factors

    def factor(m, k):
        if m < CUT:
            at = place_head(m, k)
            return head_h[at], head_l[at]
        at = place_tail(m - CUT, k - CUT)
        return tail_h[at], tail_l[at]

    for k in range(KB):
        at = slice(NB * k, NB * k + NB)
        t = raw_ref[:, at]
        for m in range(k):
            am = slice(NB * m, NB * m + NB)
            t = t - dot3(yh_ref[:, am], yl_ref[:, am], *factor(m, k), NN)
        high, low = split(t)
        y = dot3(high, low, *factor(k, k), NN)
        raw_ref[:, at] = y
        high, low = split(y)
        yh_ref[:, at] = high
        yl_ref[:, at] = low


def right_kernel(parts_ref, hh_ref, hl_ref, th_ref, tl_ref, yh_ref, yl_ref, raw):
    @pl.loop(0, 16)
    def _(s):
        for c in range(3):
            for j in range(KB):
                for h in range(2):
                    raw[pl.ds(pl.multiple_of(NB * c + 16 * s, 16), 16), NB * j + HB * h : NB * j + HB * h + HB] = parts_ref[
                        s, j, c, pl.ds(h, 16, stride=2), :
                    ]
    solve_rows(raw, yh_ref, yl_ref, (hh_ref, hl_ref, th_ref, tl_ref))


ROWS_STEP = 2


def left_kernel(meta, parts_ref, hh_ref, hl_ref, th_ref, tl_ref, yh_ref, yl_ref, own_ref, raw):
    @pl.loop(0, 16)
    def _(s):
        for a in range(ROWS_STEP):
            for j in range(KB):
                for h in range(2):
                    raw[pl.ds(pl.multiple_of(NB * a + 16 * s, 16), 16), NB * j + HB * h : NB * j + HB * h + HB] = parts_ref[
                        s, j, a, pl.ds(h, 16, stride=2), :
                    ]
    solve_rows(raw, yh_ref, yl_ref, (hh_ref, hl_ref, th_ref, tl_ref))
    for j in range(KB):

        @pl.when(meta[33] == j)
        def _():
            own_ref[...] = raw[:, NB * j : NB * j + NB]


SCHUR_STEP = 1


def schur_kernel(meta, yh, yl, own_ref, rh_ref, rl_ref, head_ref, tail_ref, parent_ref, child_0, child_1, child_2, out_ref):
    step = pl.program_id(0)
    row, col = meta[32], meta[33]
    routes = []
    for n in ROUTED:
        routes.append(routed_from(meta, n))

    for a in range(SCHUR_STEP):
        slot = step * SCHUR_STEP + a
        block_row = row + 8 * slot
        rows = slice(NB * a, NB * a + NB)
        for c in range(3):
            block_col = col + 16 * c

            def put(h, value):
                out_ref[pl.ds(1536 * a + 2 * c + h, NB, stride=6), :] = value

            @pl.when(jnp.logical_and(block_row >= KB, block_col >= KB))
            def _():
                cols = slice(NB * c, NB * c + NB)
                product = dot3(yh[rows, :], yl[rows, :], rh_ref[cols, :], rl_ref[cols, :], NT)
                for h in range(2):
                    put(h, parent_ref[pl.ds(1536 * a + 2 * c + h, NB, stride=6), :] - product[:, HB * h : HB * h + HB])
                turn = block_col % 3
                source = block_col // 3
                for n, (child, there, to) in enumerate(routes):
                    here = jnp.logical_and(there, to == slot)
                    here = jnp.logical_and(here, meta[child * 16 + source] == block_col)
                    for d, child_ref in enumerate((child_0, child_1, child_2)):

                        @pl.when(jnp.logical_and(here, turn == d))
                        def _():
                            for h in range(2):
                                at = pl.ds(1536 * a + 2 * c + h, NB, stride=6)
                                out_ref[at, :] = out_ref[at, :] + child_ref[n, pl.ds(h, NB, stride=2), :]

            @pl.when(jnp.logical_and(block_row < KB, block_col >= KB))
            def _():
                for h in range(2):
                    put(h, jnp.zeros((NB, HB), F32))

            if c == 0:

                @pl.when(jnp.logical_and(block_row >= KB, block_col < KB))
                def _():
                    for h in range(2):
                        put(h, own_ref[rows, HB * h : HB * h + HB])

                in_lead = jnp.logical_and(block_row < KB, block_col < KB)
                upper = block_row < block_col

                @pl.when(jnp.logical_and(in_lead, upper))
                def _():
                    for h in range(2):
                        put(h, jnp.zeros((NB, HB), F32))

                lower = jnp.logical_and(in_lead, jnp.logical_not(upper))

                @pl.when(jnp.logical_and(lower, block_col < CUT))
                def _():
                    block = head_ref[jnp.clip(place_head(block_col, block_row), 0, HEADS - 1)].T
                    for h in range(2):
                        put(h, block[:, HB * h : HB * h + HB])

                @pl.when(jnp.logical_and(lower, block_col >= CUT))
                def _():
                    at = jnp.clip(place_tail(block_col - CUT, block_row - CUT), 0, TAILS - 1)
                    block = tail_ref[at].T
                    for h in range(2):
                        put(h, block[:, HB * h : HB * h + HB])


def cost(microseconds):
    return pl.CostEstimate(flops=int(microseconds * 1.1e9), bytes_accessed=1 << 20, transcendentals=0)


def call(kernel, out_shape, in_specs, scratch, microseconds=2):
    return pl.pallas_call(
        kernel,
        out_shape=out_shape,
        in_specs=in_specs,
        out_specs=jax.tree.map(lambda _: VM, out_shape),
        scratch_shapes=scratch,
        compiler_params=pltpu.CompilerParams(vmem_limit_bytes=VMEM_LIMIT),
        cost_estimate=cost(microseconds),
    )


def shaped(shape, dtype=F32):
    return jax.ShapeDtypeStruct(shape, dtype)


def per_device(parent, children, index_maps):
    row = lax.axis_index("prow")
    col = lax.axis_index("pcol")
    meta = jnp.concatenate([index_maps.reshape(-1), jnp.stack([row, col]).astype(jnp.int32)])
    front = parent.reshape(6, NB, 3, 2, LANES)
    lead = front[:, :, 0].reshape(6, 16, 32, LANES)
    child = children.reshape(4, 16, 32, LANES)

    child_id = row // 4
    twos = child.reshape(2, 2, 512, LANES)
    picked = [lax.dynamic_index_in_dim(twos, (child_id + flip) % 2, 1, keepdims=False) for flip in range(2)]

    first = jnp.stack([lead[0], child[0]], axis=1)
    first = lax.all_to_all(first, "pcol", 0, 0, tiled=True)
    mine = jnp.concatenate([first[0:KB, 0], first[0:2, 1]], axis=0)
    mine, *picked = lax.optimization_barrier((mine, *picked))
    shed = jnp.where(row == 0, mine[2:5], mine[3:6])
    got_a = lax.ppermute(shed, "prow", [(0, 6), (1, 5)])
    got_b = lax.ppermute(mine[1:2], "prow", [(0, 7)])
    chunk = call(chunk_kernel, shaped((3, 32, LANES)), [SM, VM, VM, VM], [])(meta, mine, got_a, got_b)
    chunk = lax.all_gather(chunk, "pcol")
    lead_parts = lax.all_gather(chunk, "prow")

    rest = jnp.concatenate([lead[1:], child], axis=0).transpose(1, 0, 2, 3)
    rest, chunk, *picked = lax.optimization_barrier((rest, chunk, *picked))
    rest = lax.all_to_all(rest, "pcol", 0, 0, tiled=True)

    got = []
    for flip in range(2):
        perm = []
        for p in range(8):
            target = (3 * (p % 4) + 1 + 4 * ((p // 4 + flip) % 2)) % 8
            perm += [(p * 16 + q, target * 16 + (3 * q + 1) % 16) for q in range(1, 16)]
        got.append(lax.ppermute(picked[flip], ("prow", "pcol"), perm))
    rest, *got = lax.optimization_barrier((rest, *got))
    pieces = call(pick_kernel, shaped((8, 2, 32, LANES)), [SM, VM], [])(meta, rest[0:2, 5:9])
    pieces = lax.all_to_all(pieces, "prow", 0, 0, tiled=True)

    slices = call(assemble_kernel, shaped((KB, 6, 32, LANES)), [SM, VM, VM, VM], [])(
        meta, mine[0:KB], rest[0:KB, 0:5], pieces
    )

    left_parts = lax.all_gather(slices, "pcol")

    lead_parts, slices, *got = lax.optimization_barrier((lead_parts, slices, *got))

    residue = (3 * (row + 7)) % 4
    parity = ((row + 15 - 3 * residue) // 4) % 2
    chosen = {}
    for flip in range(2):
        block = 4 * parity + residue
        origin = meta[(parity + flip) % 2 * 16 + block] - 3 * block
        for d in range(3):
            which = jnp.where(origin == d, 0, 1)
            chosen[flip, d] = lax.dynamic_index_in_dim(got[flip], which, 0, keepdims=False)
    down = jnp.stack([chosen[0, 0], chosen[1, 0]])
    up = jnp.stack([chosen[0, 2], chosen[1, 2]])
    down = lax.ppermute(down, "prow", [(p, (p + 7) % 8) for p in range(8)])
    up = lax.ppermute(up, "prow", [(p, (p + 1) % 8) for p in range(8)])
    even, odd = slices[:, 0::2], slices[:, 1::2]
    is_even = col % 2 == 0
    perm_a, perm_b = [], []
    for p in range(8):
        for s in range(16):
            perm_a.append((p * 16 + s, (s // 2) * 16 + p + 8 * (s % 2)))
            perm_b.append((p * 16 + s, (s // 2) * 16 + p + 8 * (1 - s % 2)))
    pair_a = lax.ppermute(jnp.where(is_even, even, odd), ("prow", "pcol"), perm_a)
    pair_b = lax.ppermute(jnp.where(is_even, odd, even), ("prow", "pcol"), perm_b)
    low_side = col < 8
    pair = jnp.stack([jnp.where(low_side, pair_a, pair_b), jnp.where(low_side, pair_b, pair_a)])
    pairs = jnp.broadcast_to(pair[None], (8,) + pair.shape)

    scratch = [
        pltpu.VMEM((NB, NB), F32),
        pltpu.VMEM((HB, HB), F32),
        pltpu.VMEM((HB, HB), F32),
        pltpu.VMEM((HB, HB), F32),
    ]
    head_u, head_h, head_l, left_over = call(
        chain_head_kernel,
        (
            shaped((HEADS, NB, NB)),
            shaped((HEADS, NB, NB), BF16),
            shaped((HEADS, NB, NB), BF16),
            shaped((TAILS, NB, NB)),
        ),
        [SM, VM],
        [pltpu.VMEM((KB * KB, NB, NB), F32)] + scratch,
        32,
    )(meta, lead_parts)

    left_over, pairs, down, up = lax.optimization_barrier((left_over, pairs, down, up))
    right_parts = lax.all_to_all(pairs, "prow", 0, 0, tiled=True).reshape(16, KB, 3, 32, LANES)
    tail_u, tail_h, tail_l = call(
        chain_tail_kernel,
        (shaped((TAILS, NB, NB)), shaped((TAILS, NB, NB), BF16), shaped((TAILS, NB, NB), BF16)),
        [VM],
        [pltpu.VMEM((REST * REST, NB, NB), F32)] + scratch,
        40,
    )(left_over)

    middle = jnp.concatenate([jnp.stack([chosen[0, 1], chosen[1, 1]]), down, up])
    middle, tail_h = lax.optimization_barrier((middle, tail_h))
    below = lax.ppermute(middle, "pcol", [(q, (q + 1) % 16) for q in range(16)])
    above = lax.ppermute(middle, "pcol", [(q, (q + 15) % 16) for q in range(16)])

    rows = NB * ROWS_STEP
    steps = 6 // ROWS_STEP
    whole_head = pl.BlockSpec((HEADS, NB, NB), lambda g: (0, 0, 0))
    whole_tail = pl.BlockSpec((TAILS, NB, NB), lambda g: (0, 0, 0))
    by_rows = pl.BlockSpec((rows, 1280), lambda g: (g, 0))
    own_rows = pl.BlockSpec((rows, NB), lambda g: (g, 0))
    yh, yl, own = pl.pallas_call(
        left_kernel,
        grid=(steps,),
        out_shape=(shaped((1536, 1280), BF16), shaped((1536, 1280), BF16), shaped((1536, NB))),
        in_specs=[
            SM,
            pl.BlockSpec((16, KB, ROWS_STEP, 32, LANES), lambda g: (0, 0, g, 0, 0)),
            whole_head,
            whole_head,
            whole_tail,
            whole_tail,
        ],
        out_specs=(by_rows, by_rows, own_rows),
        scratch_shapes=[pltpu.VMEM((rows, 1280), F32)],
        compiler_params=pltpu.CompilerParams(vmem_limit_bytes=VMEM_LIMIT),
        cost_estimate=cost(20),
    )(meta, left_parts, head_h, head_l, tail_h, tail_l)

    right_parts, own = lax.optimization_barrier((right_parts, own))
    rh, rl = call(
        right_kernel,
        (shaped((768, 1280), BF16), shaped((768, 1280), BF16)),
        [VM] * 5,
        [pltpu.VMEM((768, 1280), F32)],
        12,
    )(right_parts, head_h, head_l, tail_h, tail_l)

    whole_right = pl.BlockSpec((768, 1280), lambda g: (0, 0))
    whole_child = pl.BlockSpec((6, 512, LANES), lambda g: (0, 0, 0))
    front_rows = pl.BlockSpec((1536 * SCHUR_STEP, LANES), lambda g: (g, 0))
    y_rows = pl.BlockSpec((NB * SCHUR_STEP, 1280), lambda g: (g, 0))
    own_block = pl.BlockSpec((NB * SCHUR_STEP, NB), lambda g: (g, 0))
    out = pl.pallas_call(
        schur_kernel,
        grid=(6 // SCHUR_STEP,),
        out_shape=shaped((9216, LANES)),
        in_specs=[SM, y_rows, y_rows, own_block, whole_right, whole_right, whole_head, whole_tail, front_rows]
        + [whole_child] * 3,
        out_specs=front_rows,
        compiler_params=pltpu.CompilerParams(vmem_limit_bytes=VMEM_LIMIT),
        cost_estimate=cost(18),
    )(
        meta,
        yh,
        yl,
        own,
        rh,
        rl,
        head_u,
        tail_u,
        parent.reshape(9216, LANES),
        *(x.reshape(6, 512, LANES) for x in (above, middle, below)),
    )
    return out.reshape(6, 1, NB, 3, 1, NB)


def solution(mesh):
    in_specs = (
        P(None, "prow", None, None, "pcol", None),
        P(None, "prow", None, None, "pcol", None),
        P(),
    )
    out_specs = P(None, "prow", None, None, "pcol", None)
    return jax.shard_map(
        per_device, mesh=mesh, in_specs=in_specs, out_specs=out_specs, check_vma=False
    )
```

```python
import jax
import jax.numpy as jnp
from jax import lax
from jax.experimental import pallas as pl
from jax.experimental.pallas import tpu as pltpu
from jax.sharding import PartitionSpec as P

KB = 5
NB = 256
HB = 128
LANES = 128
F32 = jnp.float32
BF16 = jnp.bfloat16
VMEM_LIMIT = 60 * 1024 * 1024
VM = pl.BlockSpec(memory_space=pltpu.VMEM)
SM = pl.BlockSpec(memory_space=pltpu.SMEM)


def route_of(meta, child, residue):
    there, slot = False, 0
    for turn in range(4):
        target = meta[child * 16 + 4 * turn + residue]
        here = target % 8 == meta[32]
        there = jnp.logical_or(there, here)
        slot = jnp.where(here, target // 8, slot)
    return there, slot


def turn_for(meta, target_row):
    child, residue = meta[32] // 4, meta[32] % 4
    chosen = 0
    for turn in range(1, 4):
        chosen = jnp.where(meta[child * 16 + 4 * turn + residue] % 8 == target_row, turn, chosen)
    return chosen


def routed_from(meta, n):
    flip, d = n // 3, n % 3
    row = meta[32]
    residue = (3 * (row + 8 - d)) % 4
    parity = ((row + 16 - 3 * residue - d) // 4) % 2
    child = (parity + flip) % 2
    first = 4 * parity + residue
    second = first + 8
    is_first = meta[child * 16 + first] == 3 * first + d
    is_second = meta[child * 16 + second] == 3 * second + d
    block = jnp.where(is_first, first, second)
    return child, jnp.logical_or(is_first, is_second), (3 * block + d) // 8


ROUTED = (1, 4, 0, 3, 2, 5)


def pick_kernel(meta, parts_ref, out_ref):
    for target_row in range(8):
        turn = turn_for(meta, target_row)
        for v in range(2):
            out_ref[target_row, v] = parts_ref[v, turn]


def assemble_kernel(meta, first_ref, rest_ref, got_ref, out_ref):
    for j in range(KB):
        out_ref[j, 0] = first_ref[j]
        out_ref[j, 1:6] = rest_ref[j]
    for child in range(2):
        for residue in range(4):
            there, slot = route_of(meta, child, residue)
            for v in range(2):
                column = meta[child * 16 + v]

                @pl.when(jnp.logical_and(there, column < KB))
                def _():
                    out_ref[column, slot] = out_ref[column, slot] + got_ref[4 * child + residue, v]


def chunk_kernel(meta, mine_ref, got_a_ref, got_b_ref, out_ref):
    for row, picks in enumerate(CHUNKS):

        @pl.when(meta[32] == row)
        def _():
            for at in range(3):
                kind, index = picks[at] if at < len(picks) else (0, 0)
                source = (mine_ref, got_a_ref, got_b_ref)[kind]
                out_ref[at] = source[index]


CHUNKS = [
    [(0, 0), (0, 5), (0, 6)],
    [(0, 1), (0, 2), (0, 6)],
    [(0, 2), (0, 3), (0, 4)],
    [(0, 3), (0, 4)],
    [(0, 4), (0, 5), (0, 6)],
    [(1, 0), (1, 1), (0, 6)],
    [(1, 0), (1, 1), (1, 2)],
    [(2, 0)],
]
UPPER_AT = {
    (0, 0): (0, 0),
    (0, 1): (7, 0),
    (0, 2): (6, 0),
    (0, 3): (6, 1),
    (0, 4): (6, 2),
    (1, 1): (1, 0),
    (1, 2): (1, 1),
    (1, 3): (5, 0),
    (1, 4): (5, 1),
    (2, 2): (2, 0),
    (2, 3): (2, 1),
    (2, 4): (2, 2),
    (3, 3): (3, 0),
    (3, 4): (3, 1),
    (4, 4): (4, 0),
}
CHILD_AT = {
    (0, 0, 0): (0, 1),
    (0, 0, 1): (0, 2),
    (0, 1, 1): (1, 2),
    (1, 0, 0): (4, 1),
    (1, 0, 1): (4, 2),
    (1, 1, 1): (5, 2),
}


def exact(a, b, dims):
    return lax.dot_general(a, b, (dims, ((), ())), precision=lax.Precision.HIGHEST, preferred_element_type=F32)


def dot3(ah, al, bh, bl, dims):
    def dot(a, b):
        return lax.dot_general(a, b, (dims, ((), ())), preferred_element_type=F32)

    return dot(ah, bh) + (dot(ah, bl) + dot(al, bh))


NN = ((1,), (0,))
NT = ((1,), (1,))
TN = ((0,), (0,))


def factor_128(a_ref, x_ref, u_ref):
    shape = (8, LANES)
    lane = lax.broadcasted_iota(jnp.int32, (HB, LANES), 1)
    sub = lax.broadcasted_iota(jnp.int32, (HB, LANES), 0)
    x_ref[...] = jnp.where(lane == sub, 1.0, 0.0).astype(F32)
    for g in range(HB // 8):
        rows = slice(8 * g, 8 * g + 8)
        a_g = a_ref[rows, :]
        x_g = x_ref[rows, :]
        cols = [jnp.broadcast_to(a_g[:, 8 * g + s : 8 * g + s + 1], shape) for s in range(8)]
        d = [[jnp.broadcast_to(cols[s][t : t + 1, :], shape) for s in range(t + 1)] for t in range(8)]
        low = [[None] * 8 for _ in range(8)]
        rinv = []
        for s in range(8):
            r = lax.rsqrt(d[s][s])
            rinv.append(r)
            for t in range(s + 1, 8):
                low[t][s] = d[t][s] * r
            for t in range(s + 1, 8):
                for t2 in range(s + 1, t + 1):
                    d[t][t2] = d[t][t2] - low[t][s] * low[t2][s]
        ub, xb = [], []
        for t in range(8):
            ua = jnp.broadcast_to(a_g[t : t + 1, :], shape)
            xa = jnp.broadcast_to(x_g[t : t + 1, :], shape)
            for s in range(t):
                ua = ua - low[t][s] * ub[s]
                xa = xa - low[t][s] * xb[s]
            ub.append(ua * rinv[t])
            xb.append(xa * rinv[t])
            u_ref[8 * g + t : 8 * g + t + 1, :] = ub[t][0:1, :]
            x_ref[8 * g + t : 8 * g + t + 1, :] = xb[t][0:1, :]
        for i in range(g + 1, HB // 8):
            rows_i = slice(8 * i, 8 * i + 8)
            a_i = a_ref[rows_i, :]
            x_i = x_ref[rows_i, :]
            w = []
            for t in range(8):
                wt = jnp.broadcast_to(a_i[:, 8 * g + t : 8 * g + t + 1], shape)
                for s in range(t):
                    wt = wt - low[t][s] * w[s]
                w.append(wt * rinv[t])
            for t in range(8):
                a_i = a_i - w[t] * ub[t]
                x_i = x_i - w[t] * xb[t]
            a_ref[rows_i, :] = a_i
            x_ref[rows_i, :] = x_i
    u_ref[...] = jnp.where(lane >= sub, u_ref[...], 0.0)


def split(a):
    high = a.astype(BF16)
    return high, (a - high.astype(F32)).astype(BF16)


CUT = 2
REST = KB - CUT


def place_head(k, i):
    if isinstance(i, int):
        return k + (i if i < CUT else 2 * i - 1)
    return k + jnp.where(i < CUT, i, 2 * i - 1)


def place_tail(k, i):
    return i * (i + 1) // 2 + k


HEADS = CUT * KB - 1
TAILS = REST * (REST + 1) // 2


def eliminate(n, steps, place, f_ref, u_ref, th_ref, tl_ref, v_ref, a_s, x_s, u_s):
    @pl.loop(0, 2 * steps)
    def _(step):
        k = step // 2
        half = step % 2
        kk = k * n + k
        pk = place(k, k)

        @pl.when(half == 0)
        def _():
            a_s[...] = f_ref[kk, 0:HB, 0:HB]

        @pl.when(half == 1)
        def _():
            u12 = exact(v_ref[0:HB, 0:HB], f_ref[kk, 0:HB, HB:NB], NN)
            u_ref[pk, 0:HB, HB:NB] = u12
            a_s[...] = f_ref[kk, HB:NB, HB:NB] - exact(u12, u12, TN)

        factor_128(a_s, x_s, u_s)

        @pl.when(half == 0)
        def _():
            u_ref[pk, 0:HB, 0:HB] = u_s[...]
            v_ref[0:HB, 0:HB] = x_s[...]

        @pl.when(half == 1)
        def _():
            u_ref[pk, HB:NB, HB:NB] = u_s[...]
            u_ref[pk, HB:NB, 0:HB] = jnp.zeros((HB, HB), F32)
            v_ref[HB:NB, HB:NB] = x_s[...]
            v_ref[0:HB, HB:NB] = jnp.zeros((HB, HB), F32)
            lx = exact(u_ref[pk, 0:HB, HB:NB], v_ref[0:HB, 0:HB], TN)
            v_ref[HB:NB, 0:HB] = -exact(x_s[...], lx, NN)
            high, low = split(v_ref[...].T)
            th_ref[pk] = high
            tl_ref[pk] = low
            vh, vl = split(v_ref[...])

            @pl.loop(k + 1, n)
            def _(i):
                u = dot3(vh, vl, *split(f_ref[k * n + i]), NN)
                at = place(k, i)
                u_ref[at] = u
                high, low = split(u)
                th_ref[at] = high
                tl_ref[at] = low

            @pl.loop(k + 1, n)
            def _(i):
                at_i = place(k, i)

                @pl.loop(i, n)
                def _(j):
                    at_j = place(k, j)
                    f_ref[i * n + j] = f_ref[i * n + j] - dot3(
                        th_ref[at_i], tl_ref[at_i], th_ref[at_j], tl_ref[at_j], TN
                    )


def chain_head_kernel(meta, parts_ref, u_ref, th_ref, tl_ref, rest_ref, f_ref, *scratch):
    def take(at, s, h):
        return parts_ref[at[0], s, at[1], pl.ds(h, 16, stride=2), :]

    for (k, i), at in UPPER_AT.items():
        for s in range(16):
            for h in range(2):
                f_ref[k * KB + i, 16 * s : 16 * s + 16, HB * h : HB * h + HB] = take(at, s, h)
    for (c, u, v), at in CHILD_AT.items():
        k = meta[c * 16 + u]
        i = meta[c * 16 + v]

        @pl.when(jnp.logical_and(k < KB, i < KB))
        def _():
            for s in range(16):
                for h in range(2):
                    place = (k * KB + i, slice(16 * s, 16 * s + 16), slice(HB * h, HB * h + HB))
                    f_ref[place] = f_ref[place] + take(at, s, h)

    eliminate(KB, CUT, place_head, f_ref, u_ref, th_ref, tl_ref, *scratch)
    for i in range(REST):
        for j in range(i, REST):
            rest_ref[place_tail(i, j)] = f_ref[(CUT + i) * KB + CUT + j]


def chain_tail_kernel(rest_ref, u_ref, th_ref, tl_ref, f_ref, *scratch):
    for i in range(REST):
        for j in range(i, REST):
            f_ref[i * REST + j] = rest_ref[place_tail(i, j)]
    eliminate(REST, REST, place_tail, f_ref, u_ref, th_ref, tl_ref, *scratch)


def solve_rows(raw_ref, yh_ref, yl_ref, factors):
    head_h, head_l, tail_h, tail_l = factors

    def factor(m, k):
        if m < CUT:
            at = place_head(m, k)
            return head_h[at], head_l[at]
        at = place_tail(m - CUT, k - CUT)
        return tail_h[at], tail_l[at]

    for k in range(KB):
        at = slice(NB * k, NB * k + NB)
        t = raw_ref[:, at]
        for m in range(k):
            am = slice(NB * m, NB * m + NB)
            t = t - dot3(yh_ref[:, am], yl_ref[:, am], *factor(m, k), NN)
        high, low = split(t)
        y = dot3(high, low, *factor(k, k), NN)
        raw_ref[:, at] = y
        high, low = split(y)
        yh_ref[:, at] = high
        yl_ref[:, at] = low


def right_kernel(parts_ref, hh_ref, hl_ref, th_ref, tl_ref, yh_ref, yl_ref, raw):
    @pl.loop(0, 16)
    def _(s):
        for c in range(3):
            for j in range(KB):
                for h in range(2):
                    raw[pl.ds(pl.multiple_of(NB * c + 16 * s, 16), 16), NB * j + HB * h : NB * j + HB * h + HB] = parts_ref[
                        s, j, c, pl.ds(h, 16, stride=2), :
                    ]
    solve_rows(raw, yh_ref, yl_ref, (hh_ref, hl_ref, th_ref, tl_ref))


ROWS_STEP = 2


def left_kernel(meta, parts_ref, hh_ref, hl_ref, th_ref, tl_ref, yh_ref, yl_ref, own_ref, raw):
    @pl.loop(0, 16)
    def _(s):
        for a in range(ROWS_STEP):
            for j in range(KB):
                for h in range(2):
                    raw[pl.ds(pl.multiple_of(NB * a + 16 * s, 16), 16), NB * j + HB * h : NB * j + HB * h + HB] = parts_ref[
                        s, j, a, pl.ds(h, 16, stride=2), :
                    ]
    solve_rows(raw, yh_ref, yl_ref, (hh_ref, hl_ref, th_ref, tl_ref))
    for j in range(KB):

        @pl.when(meta[33] == j)
        def _():
            own_ref[...] = raw[:, NB * j : NB * j + NB]


SCHUR_STEP = 1


def schur_kernel(meta, yh, yl, own_ref, rh_ref, rl_ref, head_ref, tail_ref, parent_ref, child_0, more_0, child_1, child_2, more_2, out_ref):
    step = pl.program_id(0)
    row, col = meta[32], meta[33]
    routes = []
    for n in ROUTED:
        routes.append(routed_from(meta, n))

    for a in range(SCHUR_STEP):
        slot = step * SCHUR_STEP + a
        block_row = row + 8 * slot
        rows = slice(NB * a, NB * a + NB)
        for c in range(3):
            block_col = col + 16 * c

            def put(h, value):
                out_ref[pl.ds(1536 * a + 2 * c + h, NB, stride=6), :] = value

            @pl.when(jnp.logical_and(block_row >= KB, block_col >= KB))
            def _():
                cols = slice(NB * c, NB * c + NB)
                product = dot3(yh[rows, :], yl[rows, :], rh_ref[cols, :], rl_ref[cols, :], NT)
                for h in range(2):
                    put(h, parent_ref[pl.ds(1536 * a + 2 * c + h, NB, stride=6), :] - product[:, HB * h : HB * h + HB])
                turn = block_col % 3
                source = block_col // 3
                for n, (child, there, to) in enumerate(routes):
                    here = jnp.logical_and(there, to == slot)
                    here = jnp.logical_and(here, meta[child * 16 + source] == block_col)
                    for d, child_ref in enumerate(((child_0, more_0), (child_1,), (child_2, more_2))):

                        @pl.when(jnp.logical_and(here, turn == d))
                        def _():
                            per = 6 // len(child_ref)
                            for h in range(2):
                                at = pl.ds(1536 * a + 2 * c + h, NB, stride=6)
                                out_ref[at, :] = out_ref[at, :] + child_ref[n // per][n % per, pl.ds(h, NB, stride=2), :]

            @pl.when(jnp.logical_and(block_row < KB, block_col >= KB))
            def _():
                for h in range(2):
                    put(h, jnp.zeros((NB, HB), F32))

            if c == 0:

                @pl.when(jnp.logical_and(block_row >= KB, block_col < KB))
                def _():
                    for h in range(2):
                        put(h, own_ref[rows, HB * h : HB * h + HB])

                in_lead = jnp.logical_and(block_row < KB, block_col < KB)
                upper = block_row < block_col

                @pl.when(jnp.logical_and(in_lead, upper))
                def _():
                    for h in range(2):
                        put(h, jnp.zeros((NB, HB), F32))

                lower = jnp.logical_and(in_lead, jnp.logical_not(upper))

                @pl.when(jnp.logical_and(lower, block_col < CUT))
                def _():
                    block = head_ref[jnp.clip(place_head(block_col, block_row), 0, HEADS - 1)].T
                    for h in range(2):
                        put(h, block[:, HB * h : HB * h + HB])

                @pl.when(jnp.logical_and(lower, block_col >= CUT))
                def _():
                    at = jnp.clip(place_tail(block_col - CUT, block_row - CUT), 0, TAILS - 1)
                    block = tail_ref[at].T
                    for h in range(2):
                        put(h, block[:, HB * h : HB * h + HB])


def cost(microseconds):
    return pl.CostEstimate(flops=int(microseconds * 1.1e9), bytes_accessed=1 << 20, transcendentals=0)


def call(kernel, out_shape, in_specs, scratch, microseconds=2):
    return pl.pallas_call(
        kernel,
        out_shape=out_shape,
        in_specs=in_specs,
        out_specs=jax.tree.map(lambda _: VM, out_shape),
        scratch_shapes=scratch,
        compiler_params=pltpu.CompilerParams(vmem_limit_bytes=VMEM_LIMIT),
        cost_estimate=cost(microseconds),
    )


def shaped(shape, dtype=F32):
    return jax.ShapeDtypeStruct(shape, dtype)


def per_device(parent, children, index_maps):
    row = lax.axis_index("prow")
    col = lax.axis_index("pcol")
    meta = jnp.concatenate([index_maps.reshape(-1), jnp.stack([row, col]).astype(jnp.int32)])
    front = parent.reshape(6, NB, 3, 2, LANES)
    lead = front[:, :, 0].reshape(6, 16, 32, LANES)
    child = children.reshape(4, 16, 32, LANES)

    child_id = row // 4
    twos = child.reshape(2, 2, 512, LANES)
    picked = [lax.dynamic_index_in_dim(twos, (child_id + flip) % 2, 1, keepdims=False) for flip in range(2)]

    first = jnp.stack([lead[0], child[0]], axis=1)
    first = lax.all_to_all(first, "pcol", 0, 0, tiled=True)
    mine = jnp.concatenate([first[0:KB, 0], first[0:2, 1]], axis=0)
    mine, *picked = lax.optimization_barrier((mine, *picked))
    shed = jnp.where(row == 0, mine[2:5], mine[3:6])
    got_a = lax.ppermute(shed, "prow", [(0, 6), (1, 5)])
    got_b = lax.ppermute(mine[1:2], "prow", [(0, 7)])
    chunk = call(chunk_kernel, shaped((3, 32, LANES)), [SM, VM, VM, VM], [])(meta, mine, got_a, got_b)
    chunk = lax.all_gather(chunk, "pcol")
    lead_parts = lax.all_gather(chunk, "prow")

    rest = jnp.concatenate([lead[1:], child], axis=0).transpose(1, 0, 2, 3)
    rest, chunk = lax.optimization_barrier((rest, chunk))
    rest = lax.all_to_all(rest, "pcol", 0, 0, tiled=True)
    pieces = call(pick_kernel, shaped((8, 2, 32, LANES)), [SM, VM], [])(meta, rest[0:2, 5:9])
    pieces, *picked = lax.optimization_barrier((pieces, *picked))
    pieces = lax.all_to_all(pieces, "prow", 0, 0, tiled=True)

    got = []
    for flip in range(2):
        perm = []
        for p in range(8):
            target = (3 * (p % 4) + 1 + 4 * ((p // 4 + flip) % 2)) % 8
            perm += [(p * 16 + q, target * 16 + (3 * q + 1) % 16) for q in range(1, 16)]
        got.append(lax.ppermute(picked[flip], ("prow", "pcol"), perm))
    pieces, *got = lax.optimization_barrier((pieces, *got))
    slices = call(assemble_kernel, shaped((KB, 6, 32, LANES)), [SM, VM, VM, VM], [])(
        meta, mine[0:KB], rest[0:KB, 0:5], pieces
    )

    left_parts = lax.all_gather(slices, "pcol")

    lead_parts, slices, *got = lax.optimization_barrier((lead_parts, slices, *got))

    residue = (3 * (row + 7)) % 4
    parity = ((row + 15 - 3 * residue) // 4) % 2
    chosen = {}
    for flip in range(2):
        block = 4 * parity + residue
        origin = meta[(parity + flip) % 2 * 16 + block] - 3 * block
        for d in range(3):
            which = jnp.where(origin == d, 0, 1)
            chosen[flip, d] = lax.dynamic_index_in_dim(got[flip], which, 0, keepdims=False)
    down = jnp.stack([chosen[0, 0], chosen[1, 0]])
    up = jnp.stack([chosen[0, 2], chosen[1, 2]])
    down = lax.ppermute(down, "prow", [(p, (p + 7) % 8) for p in range(8)])
    up = lax.ppermute(up, "prow", [(p, (p + 1) % 8) for p in range(8)])
    even, odd = slices[:, 0::2], slices[:, 1::2]
    is_even = col % 2 == 0
    perm_a, perm_b = [], []
    for p in range(8):
        for s in range(16):
            perm_a.append((p * 16 + s, (s // 2) * 16 + p + 8 * (s % 2)))
            perm_b.append((p * 16 + s, (s // 2) * 16 + p + 8 * (1 - s % 2)))
    pair_a = lax.ppermute(jnp.where(is_even, even, odd), ("prow", "pcol"), perm_a)
    pair_b = lax.ppermute(jnp.where(is_even, odd, even), ("prow", "pcol"), perm_b)
    low_side = col < 8
    pair = jnp.stack([jnp.where(low_side, pair_a, pair_b), jnp.where(low_side, pair_b, pair_a)])
    pairs = jnp.broadcast_to(pair[None], (8,) + pair.shape)

    scratch = [
        pltpu.VMEM((NB, NB), F32),
        pltpu.VMEM((HB, HB), F32),
        pltpu.VMEM((HB, HB), F32),
        pltpu.VMEM((HB, HB), F32),
    ]
    head_u, head_h, head_l, left_over = call(
        chain_head_kernel,
        (
            shaped((HEADS, NB, NB)),
            shaped((HEADS, NB, NB), BF16),
            shaped((HEADS, NB, NB), BF16),
            shaped((TAILS, NB, NB)),
        ),
        [SM, VM],
        [pltpu.VMEM((KB * KB, NB, NB), F32)] + scratch,
        32,
    )(meta, lead_parts)

    left_over, pairs, down, up = lax.optimization_barrier((left_over, pairs, down, up))
    right_parts = lax.all_to_all(pairs, "prow", 0, 0, tiled=True).reshape(16, KB, 3, 32, LANES)
    tail_u, tail_h, tail_l = call(
        chain_tail_kernel,
        (shaped((TAILS, NB, NB)), shaped((TAILS, NB, NB), BF16), shaped((TAILS, NB, NB), BF16)),
        [VM],
        [pltpu.VMEM((REST * REST, NB, NB), F32)] + scratch,
        40,
    )(left_over)

    middle = jnp.concatenate([jnp.stack([chosen[0, 1], chosen[1, 1]]), down, up])
    middle, tail_h = lax.optimization_barrier((middle, tail_h))
    halves = (middle[0:3], middle[3:6])
    below = [lax.ppermute(half, "pcol", [(q, (q + 1) % 16) for q in range(16)]) for half in halves]
    above = [lax.ppermute(half, "pcol", [(q, (q + 15) % 16) for q in range(16)]) for half in halves]

    rows = NB * ROWS_STEP
    steps = 6 // ROWS_STEP
    whole_head = pl.BlockSpec((HEADS, NB, NB), lambda g: (0, 0, 0))
    whole_tail = pl.BlockSpec((TAILS, NB, NB), lambda g: (0, 0, 0))
    by_rows = pl.BlockSpec((rows, 1280), lambda g: (g, 0))
    own_rows = pl.BlockSpec((rows, NB), lambda g: (g, 0))
    yh, yl, own = pl.pallas_call(
        left_kernel,
        grid=(steps,),
        out_shape=(shaped((1536, 1280), BF16), shaped((1536, 1280), BF16), shaped((1536, NB))),
        in_specs=[
            SM,
            pl.BlockSpec((16, KB, ROWS_STEP, 32, LANES), lambda g: (0, 0, g, 0, 0)),
            whole_head,
            whole_head,
            whole_tail,
            whole_tail,
        ],
        out_specs=(by_rows, by_rows, own_rows),
        scratch_shapes=[pltpu.VMEM((rows, 1280), F32)],
        compiler_params=pltpu.CompilerParams(vmem_limit_bytes=VMEM_LIMIT),
        cost_estimate=cost(20),
    )(meta, left_parts, head_h, head_l, tail_h, tail_l)

    right_parts, own = lax.optimization_barrier((right_parts, own))
    rh, rl = call(
        right_kernel,
        (shaped((768, 1280), BF16), shaped((768, 1280), BF16)),
        [VM] * 5,
        [pltpu.VMEM((768, 1280), F32)],
        12,
    )(right_parts, head_h, head_l, tail_h, tail_l)

    whole_right = pl.BlockSpec((768, 1280), lambda g: (0, 0))
    whole_child = pl.BlockSpec((6, 512, LANES), lambda g: (0, 0, 0))
    half_child = pl.BlockSpec((3, 512, LANES), lambda g: (0, 0, 0))
    front_rows = pl.BlockSpec((1536 * SCHUR_STEP, LANES), lambda g: (g, 0))
    y_rows = pl.BlockSpec((NB * SCHUR_STEP, 1280), lambda g: (g, 0))
    own_block = pl.BlockSpec((NB * SCHUR_STEP, NB), lambda g: (g, 0))
    out = pl.pallas_call(
        schur_kernel,
        grid=(6 // SCHUR_STEP,),
        out_shape=shaped((9216, LANES)),
        in_specs=[SM, y_rows, y_rows, own_block, whole_right, whole_right, whole_head, whole_tail, front_rows]
        + [half_child, half_child, whole_child, half_child, half_child],
        out_specs=front_rows,
        compiler_params=pltpu.CompilerParams(vmem_limit_bytes=VMEM_LIMIT),
        cost_estimate=cost(18),
    )(
        meta,
        yh,
        yl,
        own,
        rh,
        rl,
        head_u,
        tail_u,
        parent.reshape(9216, LANES),
        *above,
        middle,
        *below,
    )
    return out.reshape(6, 1, NB, 3, 1, NB)


def solution(mesh):
    in_specs = (
        P(None, "prow", None, None, "pcol", None),
        P(None, "prow", None, None, "pcol", None),
        P(),
    )
    out_specs = P(None, "prow", None, None, "pcol", None)
    return jax.shard_map(
        per_device, mesh=mesh, in_specs=in_specs, out_specs=out_specs, check_vma=False
    )
```
